32 devices in a mesh: gx: 4 (over x, core), gy: 4 (over z), gz: 2 (over y).
Axes of the slice: x: 2, y: 2, z: 4, core: 2. Of those that a mesh axis runs over, the one named last changes fastest.
Arguments:
- e_field: float32 [3, 32, 64, 256], P(None, 'gx', 'gy', 'gz'), may hold values from -6 to 6
- h_field: float32 [3, 32, 64, 256], P(None, 'gx', 'gy', 'gz'), may hold values from -6 to 6
- permittivity: float32 [32, 64, 256], P('gx', 'gy', 'gz'), may hold values from 1 to 4
- wall_mask: int32 [32, 64, 256], P('gx', 'gy', 'gz'), may hold values 0 or 1
- poles: float32 [8, 3, 32, 64, 256], P(None, None, 'gx', 'gy', 'gz'), may hold values from -4 to 4
- pole_decay: float32 [8], replicated, may hold values from 0.2 to 0.95
- pole_gain: float32 [8], replicated, may hold values from 0.05 to 0.3
- face_cells: int32 [1024], P(('gx', 'gy', 'gz')), may hold values from 0 to 16383
- owners: int32 [1024, 1], P(('gx', 'gy', 'gz')), may hold values from 0 to 3; in each aligned block of 32 rows (0 to 31, 32 to 63, ...) at most 16 rows name the same one
- history: bfloat16 [63, 4, 1024], P(None, None, ('gx', 'gy', 'gz')), may hold values from -6 to 6
- steering: bfloat16 [4, 2048, 4096], P(None, ('gx', 'gy'), 'gz'), may hold values from -0.09375 to 0.09375
Outputs:
- e_next: float32 [3, 32, 64, 256], P(None, 'gx', 'gy', 'gz')
- h_next: float32 [3, 32, 64, 256], P(None, 'gx', 'gy', 'gz')
- poles_next: float32 [8, 3, 32, 64, 256], P(None, None, 'gx', 'gy', 'gz')
- far_field: float32 [2, 256, 4096], P(None, ('gx', 'gy'), 'gz')
The draws below stay inside these ranges and needn't reach their ends.
Inputs may be any that keep to these rules, and one draw needn't show every extreme that they name: `face_cells`: index of the sample's cell within its device's block, row-major over 8 x 16 x 128. `owners`: among the samples of one device at most 16 name the same owner, and some device has exactly 16 for one owner.
All inputs are finite; a program needn't handle non-finite values. No bound on the sum of `wall_mask` on one device may be relied on, other than what follows from the above.
Results may differ from the reference program's by a relative error of at most 0.00063.
Values may be sent and summed in bfloat16 or wider, within the bound.
A program may use at most 64 MiB of HBM per device.

```python
import math
import jax
import jax.numpy as jnp
import numpy as np
from jax import lax

CX = 8
CY = 16
CZ = 128
K_DEV = 32
POLES = 8
STEPS = 64
FREQS = 256
DIRS = 4096
NX = 32
NY = 64
NZ = 256
FACES = 1024
CAP = 16
TILE = 128
ROWS = 2048
N_GX = 4
N_GY = 4
N_GZ = 2


def plant(drawn, rng, smallest, high):
    dims = drawn.shape
    place = [jax.random.randint(jax.random.fold_in(rng, axis), (), 0, dims[axis]) for axis in range(len(dims))]
    drawn = drawn.at[tuple(place)].set(smallest)
    longest = dims.index(max(dims))
    place[longest] = (place[longest] + 1) % dims[longest]
    return drawn.at[tuple(place)].set(high)


def block_scale(key, dims, cuts, low, high):
    def one(position, blocks):
        draws = jax.random.uniform(jax.random.fold_in(jax.random.fold_in(key, 6), position), (blocks,), jnp.float32, low / len(cuts), high / len(cuts))
        return jnp.repeat(jnp.exp(draws), dims[position] // blocks).reshape((-1,) + (1,) * (len(dims) - position - 1))

    factor_of = one(*cuts[0])
    for cut in cuts[1:]:
        factor_of = factor_of * one(*cut)
    return factor_of


def shared_out(stream_key, own, number, rows, amount, top, most, lean):
    ranking = jax.random.permutation(stream_key, amount)
    packed, common = load_shares(amount, rows * top, most, lean, True), load_shares(amount, rows * top, most, lean, False)
    places = jnp.arange(amount)

    def named(sizes, rotation):
        used = int((sizes > 0).sum())
        fixed = max(1, used // 4)
        passed = fixed + (places - fixed + rotation * (used - fixed)) % max(1, amount - fixed)
        return jnp.zeros((amount,), jnp.int32).at[ranking[jnp.where(places < fixed, places, passed)]].set(jnp.asarray(sizes, jnp.int32))

    sizes = jnp.where(number % 4 == 0, named(packed, number // 4), named(common, number - number // 4 - 1))
    mixed = jax.random.permutation(jax.random.fold_in(own, 3), amount)
    giver, sink = mixed[0:amount // 2 * 2:2], mixed[1:amount // 2 * 2:2]
    room = jnp.minimum(sizes[giver] - 1, most - sizes[sink]) // 2
    room = jnp.where((giver == ranking[0]) | (sink == ranking[0]) | (sizes[sink] == 0), 0, jnp.maximum(room, 0))
    passed = jax.random.randint(jax.random.fold_in(own, 4), (amount // 2,), 0, 1 << 20) % (room + 1)
    sizes = sizes.at[giver].add(-passed).at[sink].add(passed)
    members = jnp.searchsorted(jnp.cumsum(sizes), jnp.arange(rows * top), side="right").astype(jnp.int32)
    table = members.reshape(top, rows).T
    table = table[jax.random.permutation(jax.random.fold_in(own, 1), rows)]
    rotation = jax.random.randint(jax.random.fold_in(own, 2), (rows, 1), 0, top)
    return jnp.take_along_axis(table, (jnp.arange(top)[None, :] + rotation) % top, axis=1)


def load_shares(number_of, total, limit, lean, full):
    weights = [(1 << 20) // math.isqrt(grade ** lean) + 1 for grade in range(1, number_of + 1)]
    largest = limit if full else min(limit, max(-(-total // number_of), total * weights[0] // sum(weights)))
    least = 1 if total - largest >= number_of - 1 else 0
    given, rest = [largest] + [least] * (number_of - 1), total - largest - least * (number_of - 1)
    while rest > 0:
        free = [i for i in range(1, number_of) if given[i] < largest] or [i for i in range(1, number_of) if given[i] < limit]
        pool, left = sum([weights[i] for i in free]), rest
        for i in free:
            more = min(limit - given[i], max(1, left * weights[i] // pool), rest)
            given[i] = given[i] + more
            rest = rest - more
    return np.array(given)


def normal_values(stream_key, shape, deviation, most, pieces=(), held_as=jnp.bfloat16):
    gain = block_scale(stream_key, shape, pieces, -0.22, 0.18) if pieces else 1.0
    entries = jax.random.normal(stream_key, shape, jnp.float32) * deviation * gain
    return jnp.minimum(jnp.maximum(entries, -most), most).astype(held_as)


def setup_inputs(seed: int = 0) -> dict:
    key_list = jax.random.split(jax.random.key(seed), 12)
    e_field = normal_values(key_list[0], (3, NX, NY, NZ), 1.0, 6.0, ((1, 4), (2, 4), (3, 2)), jnp.float32)
    h_field = normal_values(key_list[1], (3, NX, NY, NZ), 1.0, 6.0, ((1, 4), (2, 4), (3, 2)), jnp.float32)
    permittivity = jnp.clip(jnp.exp(math.log(4.0) - 1.3862944 * jax.random.uniform(key_list[2], (NX, NY, NZ), jnp.float32) ** block_scale(key_list[2], (NX, NY, NZ), ((0, 4), (1, 4), (2, 2)), -0.2, 0.2)), 1.0, 4.0)
    wall_mask = plant((jax.random.randint(key_list[3], (NX, NY, NZ), 0, 4) < 1).astype(jnp.int32), jax.random.fold_in(key_list[3], 1), 0, 1)
    poles = normal_values(key_list[4], (POLES, 3, NX, NY, NZ), 0.3, 4.0, ((2, 4), (3, 4), (4, 2)), jnp.float32)
    pole_decay = jnp.clip(jnp.exp(jax.random.uniform(key_list[5], (POLES,), jnp.float32, math.log(0.2), math.log(0.95))), 0.2, 0.95)
    pole_gain = jnp.clip(jax.random.uniform(key_list[6], (POLES,), jnp.float32, 0.05, 0.3), 0.05, 0.3)
    face_cells = plant(jax.random.randint(key_list[7], (FACES,), 0, CX * CY * CZ), jax.random.fold_in(key_list[7], 1), 0, (CX * CY * CZ) - 1).astype(jnp.int32)
    owners_keys = jax.random.split(jax.random.fold_in(key_list[8], 1), FACES // K_DEV)
    owners_turns = jax.random.permutation(jax.random.fold_in(key_list[8], 3), FACES // K_DEV)
    owners = jax.vmap(lambda own, number: shared_out(jax.random.fold_in(key_list[8], 2), own, number, K_DEV, N_GX, 1, CAP, 2))(owners_keys, owners_turns).reshape((FACES, 1))
    history = normal_values(key_list[9], (STEPS - 1, 4, FACES), 1.0, 6.0, ((2, 32),))
    steering = normal_values(key_list[10], (4, ROWS, DIRS), (2 * ROWS) ** -0.5, 0.09375, ((1, 16), (2, 2)))
    return {"e_field": e_field, "h_field": h_field, "permittivity": permittivity, "wall_mask": wall_mask, "poles": poles, "pole_decay": pole_decay, "pole_gain": pole_gain, "face_cells": face_cells, "owners": owners, "history": history, "steering": steering}


def forward(field, axis):
    widths = [(0, 0), (0, 0), (0, 0)]
    widths[axis] = (0, 1)
    return lax.slice_in_dim(jnp.pad(field, widths), 1, field.shape[axis] + 1, axis=axis)

def backward(field, axis):
    widths = [(0, 0), (0, 0), (0, 0)]
    widths[axis] = (1, 0)
    return lax.slice_in_dim(jnp.pad(field, widths), 0, field.shape[axis], axis=axis)

def spectral_table(freqs, steps):
    times = jnp.arange(steps, dtype=jnp.float32)
    levels = jnp.arange(freqs, dtype=jnp.float32) + 0.5
    phase = math.pi / (2.0 * freqs) * levels[:, None] * times[None, :]
    scale = 1.0 / math.sqrt(steps)
    return jnp.stack([jnp.cos(phase) * scale, -jnp.sin(phase) * scale])

def bucket_rank(owner, groups):
    onehot = (owner[..., None] == jnp.arange(groups, dtype=jnp.int32)).astype(jnp.int32)
    return lax.optimization_barrier(jnp.sum((jnp.cumsum(onehot, axis=-2) - onehot) * onehot, axis=-1))

def reference(e_field, h_field, permittivity, wall_mask, poles, pole_decay, pole_gain, face_cells, owners, history, steering):
    elec_x, elec_y, elec_z = (e_field[0], e_field[1], e_field[2])
    mag_x = h_field[0] - 0.5 * (forward(elec_z, 1) - elec_z - (forward(elec_y, 2) - elec_y))
    mag_y = h_field[1] - 0.5 * (forward(elec_x, 2) - elec_x - (forward(elec_z, 0) - elec_z))
    mag_z = h_field[2] - 0.5 * (forward(elec_y, 0) - elec_y - (forward(elec_x, 1) - elec_x))
    drive = jnp.stack([mag_z - backward(mag_z, 1) - (mag_y - backward(mag_y, 2)), mag_x - backward(mag_x, 2) - (mag_z - backward(mag_z, 0)), mag_y - backward(mag_y, 0) - (mag_x - backward(mag_x, 1))])
    h_next = jnp.stack([mag_x, mag_y, mag_z])
    poles_next = pole_decay[:, None, None, None, None] * poles + pole_gain[:, None, None, None, None] * drive[None]
    e_next = jnp.where(wall_mask[None] == 1, lax.optimization_barrier(jnp.sum(poles_next, axis=0)), e_field + (0.5 / permittivity)[None] * drive)
    devices = N_GX * N_GY * N_GZ
    span = CX * CY * CZ

    def blocks(field):
        shaped = field.reshape(N_GX, CX, N_GY, CY, N_GZ, CZ).transpose(0, 2, 4, 1, 3, 5)
        return shaped.reshape(devices, span)
    cells = face_cells.reshape(devices, K_DEV).astype(jnp.int32)
    picked = [blocks(e_next[0]), blocks(e_next[1]), blocks(h_next[0]), blocks(h_next[1])]
    fresh = jnp.stack([jnp.take_along_axis(block, cells, axis=1).reshape(-1) for block in picked]).astype(jnp.bfloat16)
    series = jnp.concatenate([history, fresh[None]], axis=0)
    owner = owners[:, 0].reshape(devices, K_DEV).astype(jnp.int32)
    rank = bucket_rank(owner, N_GX)
    device_ids = jnp.arange(devices, dtype=jnp.int32)
    source_x = device_ids // (N_GY * N_GZ)
    source_y = device_ids // N_GZ % N_GY
    source_z = device_ids % N_GZ
    row = (owner * N_GY + source_y[:, None]) * TILE + source_z[:, None] * (N_GX * CAP) + source_x[:, None] * CAP + rank
    row = row.reshape(-1).astype(jnp.int32)
    projected = jnp.zeros((STEPS, DIRS), jnp.float32)
    for comp in range(4):
        weights = jnp.take(steering[comp], row, axis=0)
        projected = projected + jnp.dot(series[:, comp, :], weights, preferred_element_type=jnp.float32)
    table = spectral_table(FREQS, STEPS)
    far_field = jnp.einsum('sft,td->sfd', table, projected, precision=lax.Precision.HIGHEST)
    return (e_next, h_next, poles_next, far_field)
```

```python
import functools
import math

import jax
import jax.numpy as jnp
import numpy as np
from jax import lax
from jax.experimental import pallas as pl
from jax.experimental.pallas import tpu as pltpu
from jax.sharding import PartitionSpec as P

FREQS = 256
MESH = pl.DeviceIdType.MESH


def spectral_rows(count, freqs, steps):
    times = np.arange(steps, dtype=np.float64)
    levels = np.arange(count, dtype=np.float64) + 0.5
    phase = math.pi / (2.0 * freqs) * levels[:, None] * times[None, :]
    scale = 1.0 / math.sqrt(steps)
    return np.stack([np.cos(phase) * scale, -np.sin(phase) * scale]).astype(np.float32)


def kernel(
    n_gx, n_gy, n_gz, cap, rows,
    decay, gain, e_ref, h_ref, perm_ref, mask_ref, cells_ref, own_col, own_row, hist_ref,
    table_ref, poles_hbm, steer_hbm,
    e_out, h_out, far_out, poles_out_hbm,
    poles, poles_out, steer, edge_j, edge_k, got_i, got_j, got_k,
    low_j, low_k, from_i, from_j, from_k, compact, tile, part, got_1, got_2, got_3, full,
    local_sem, halo_send, halo_recv, tile_send, tile_recv,
    core_send, core_recv, mid_send, mid_recv, end_send, end_recv,
    back_z_send, back_z_recv, back_x_send, back_x_recv, back_c_send, back_c_recv,
):
    gx, gy, gz = lax.axis_index("gx"), lax.axis_index("gy"), lax.axis_index("gz")
    n_x = n_gx // 2
    core, mid = lax.rem(gx, 2), gx // 2
    span_x, span_y, span_z = e_ref.shape[1:]

    load_poles = pltpu.make_async_copy(poles_hbm, poles, local_sem.at[0])
    load_poles.start()
    load_steer = pltpu.make_async_copy(steer_hbm, steer, local_sem.at[1])
    load_steer.start()

    barrier = pltpu.get_barrier_semaphore()
    partners = 0
    for da in range(n_gx):
        for dz in range(n_gz):
            if da or dz:
                peer = (lax.rem(gx + da, n_gx), gy, lax.rem(gz + dz, n_gz))
                pl.semaphore_signal(barrier, inc=1, device_id=peer, device_id_type=MESH)
                partners += 1
    for dw in range(1, n_gy):
        peer = (gx, lax.rem(gy + dw, n_gy), gz)
        pl.semaphore_signal(barrier, inc=1, device_id=peer, device_id_type=MESH)
        partners += 1
    pl.semaphore_wait(barrier, partners)

    def remote(src, dst, send, recv, peer):
        return pltpu.make_async_remote_copy(
            src_ref=src, dst_ref=dst, send_sem=send, recv_sem=recv,
            device_id=peer, device_id_type=MESH,
        )

    flat = (span_x * span_y, span_z)
    cells = (span_x, span_y, span_z)

    def column(field, lane):
        return jnp.transpose(field.reshape(flat))[lane : lane + 1]

    def spread(row):
        return jnp.transpose(jnp.broadcast_to(row, (span_z, flat[0]))).reshape(cells)

    up_i = remote(e_ref.at[pl.ds(1, 2), 0], got_i, halo_send.at[0], halo_recv.at[0], (gx - 1, gy, gz))
    up_j = remote(edge_j, got_j, halo_send.at[1], halo_recv.at[1], (gx, gy - 1, gz))
    up_k = remote(edge_k, got_k, halo_send.at[2], halo_recv.at[2], (gx, gy, gz - 1))
    down_i = remote(
        h_out.at[pl.ds(1, 2), span_x - 1], from_i, halo_send.at[3], halo_recv.at[3], (gx + 1, gy, gz)
    )
    down_j = remote(low_j, from_j, halo_send.at[4], halo_recv.at[4], (gx, gy + 1, gz))
    down_k = remote(low_k, from_k, halo_send.at[5], halo_recv.at[5], (gx, gy, gz + 1))

    @pl.when(gz > 0)
    def _():
        edge_k[0:1] = column(e_ref[0], 0)
        edge_k[1:2] = column(e_ref[1], 0)
        edge_k[2:8] = jnp.zeros((6, flat[0]), jnp.float32)
        up_k.start()

    @pl.when(gx > 0)
    def _():
        up_i.start()

    @pl.when(gy > 0)
    def _():
        edge_j[0] = e_ref[0, :, 0, :]
        edge_j[1] = e_ref[2, :, 0, :]
        up_j.start()

    @pl.when(gx == n_gx - 1)
    def _():
        got_i[...] = jnp.zeros(got_i.shape, jnp.float32)

    @pl.when(gy == n_gy - 1)
    def _():
        got_j[...] = jnp.zeros(got_j.shape, jnp.float32)

    @pl.when(gz == n_gz - 1)
    def _():
        got_k[...] = jnp.zeros(got_k.shape, jnp.float32)

    @pl.when(gx == 0)
    def _():
        from_i[...] = jnp.zeros(from_i.shape, jnp.float32)

    @pl.when(gy == 0)
    def _():
        from_j[...] = jnp.zeros(from_j.shape, jnp.float32)

    @pl.when(gz == 0)
    def _():
        from_k[...] = jnp.zeros(from_k.shape, jnp.float32)

    count = own_col.shape[0]
    earlier = lax.broadcasted_iota(jnp.int32, (count, count), 0) < lax.broadcasted_iota(
        jnp.int32, (count, count), 1
    )
    same = jnp.where((own_col[...] == own_row[...]) & earlier, 1.0, 0.0)
    rank = jnp.sum(same, axis=0, keepdims=True).astype(jnp.int32)
    slot = own_row[...] * rows + rank
    place = (
        lax.broadcasted_iota(jnp.int32, (n_gx * rows, count), 0) == slot
    ).astype(jnp.float32).astype(jnp.bfloat16)

    at_j = lax.broadcasted_iota(jnp.int32, cells, 1)
    at_k = lax.broadcasted_iota(jnp.int32, cells, 2)

    def next_j(field, halo):
        return jnp.where(at_j == span_y - 1, halo[:, None, :], pltpu.roll(field, span_y - 1, 1))

    def next_k(field, halo):
        return jnp.where(at_k == span_z - 1, spread(halo), pltpu.roll(field, span_z - 1, 2))

    def prev_j(field, halo):
        return jnp.where(at_j == 0, halo[:, None, :], pltpu.roll(field, 1, 1))

    def prev_k(field, halo):
        return jnp.where(at_k == 0, spread(halo), pltpu.roll(field, 1, 2))

    @pl.when(gx < n_gx - 1)
    def _():
        up_i.wait_recv()

    @pl.when(gy < n_gy - 1)
    def _():
        up_j.wait_recv()

    @pl.when(gz < n_gz - 1)
    def _():
        up_k.wait_recv()

    ex, ey, ez = e_ref[0], e_ref[1], e_ref[2]
    ey_i = jnp.concatenate([ey[1:], got_i[0][None]], axis=0)
    ez_i = jnp.concatenate([ez[1:], got_i[1][None]], axis=0)
    mag_x = h_ref[0] - 0.5 * (next_j(ez, got_j[1]) - ez - (next_k(ey, got_k[1:2]) - ey))
    h_out[0] = mag_x
    mag_y = h_ref[1] - 0.5 * (next_k(ex, got_k[0:1]) - ex - (ez_i - ez))
    h_out[1] = mag_y
    mag_z = h_ref[2] - 0.5 * (ey_i - ey - (next_j(ex, got_j[0]) - ex))
    h_out[2] = mag_z

    @pl.when(gx < n_gx - 1)
    def _():
        down_i.start()

    @pl.when(gz < n_gz - 1)
    def _():
        low_k[0:1] = column(h_out[0], span_z - 1)
        low_k[1:2] = column(h_out[1], span_z - 1)
        low_k[2:8] = jnp.zeros((6, flat[0]), jnp.float32)
        down_k.start()

    @pl.when(gy < n_gy - 1)
    def _():
        low_j[0] = h_out[0, :, span_y - 1, :]
        low_j[1] = h_out[2, :, span_y - 1, :]
        down_j.start()

    load_poles.wait()

    @pl.when(gx > 0)
    def _():
        down_i.wait_recv()

    @pl.when(gy > 0)
    def _():
        down_j.wait_recv()

    @pl.when(gz > 0)
    def _():
        down_k.wait_recv()

    mag_x, mag_y, mag_z = h_out[0], h_out[1], h_out[2]
    mag_y_i = jnp.concatenate([from_i[0][None], mag_y[:-1]], axis=0)
    mag_z_i = jnp.concatenate([from_i[1][None], mag_z[:-1]], axis=0)
    drives = (
        mag_z - prev_j(mag_z, from_j[1]) - (mag_y - prev_k(mag_y, from_k[1:2])),
        mag_x - prev_k(mag_x, from_k[0:1]) - (mag_z - mag_z_i),
        mag_y - mag_y_i - (mag_x - prev_j(mag_x, from_j[0])),
    )
    wall = mask_ref[...] == 1
    half_eps = 0.5 / perm_ref[...]
    for comp in range(3):
        drive = drives[comp]
        total = None
        for pole in range(poles.shape[0]):
            state = decay[pole] * poles[pole, comp] + gain[pole] * drive
            poles_out[pole, comp] = state
            total = state if total is None else total + state
        e_out[comp] = jnp.where(wall, total, e_ref[comp] + half_eps * drive)
    store_poles = pltpu.make_async_copy(poles_out, poles_out_hbm, local_sem.at[2])
    store_poles.start()

    cell = cells_ref[...]
    row_hot = (
        lax.broadcasted_iota(jnp.int32, (count, flat[0]), 1) == cell // span_z
    ).astype(jnp.float32).astype(jnp.bfloat16)
    lane_hot = lax.broadcasted_iota(jnp.int32, (count, span_z), 1) == lax.rem(cell, span_z)
    steps = hist_ref.shape[1] // 4
    lane = lax.broadcasted_iota(jnp.int32, hist_ref.shape, 1)
    samples = hist_ref[...].astype(jnp.float32)
    for comp, field in enumerate((e_out[0], e_out[1], h_out[0], h_out[1])):
        found = jnp.dot(
            row_hot, field.reshape(flat).astype(jnp.bfloat16), preferred_element_type=jnp.float32
        )
        fresh = jnp.sum(jnp.where(lane_hot, found, 0.0), axis=1, keepdims=True)
        samples = jnp.where(lane == comp * steps + steps - 1, fresh, samples)
    packed = jnp.dot(
        place, samples.astype(jnp.bfloat16), preferred_element_type=jnp.float32
    ).astype(jnp.bfloat16)
    compact[...] = packed.reshape(compact.shape)
    me = gz * n_gx + gx
    tile_copies = []
    for da in range(n_gx):
        for dz in range(n_gz):
            to_x, to_z = lax.rem(gx + da, n_gx), lax.rem(gz + dz, n_gz)
            if da or dz:
                index = da * n_gz + dz
                copy = remote(
                    compact.at[to_x], tile.at[me], tile_send.at[index], tile_recv.at[index],
                    (to_x, gy, to_z),
                )
                copy.start()
                tile_copies.append(copy)
    tile[me] = compact[gx]
    load_steer.wait()
    for copy in tile_copies:
        copy.wait_recv()

    sources = n_gx * n_gz
    slots = tile[...].reshape(sources * rows, 4 * steps)
    if rows != cap:
        place_row = lax.broadcasted_iota(jnp.int32, (sources * cap, sources * rows), 0)
        place_col = lax.broadcasted_iota(jnp.int32, (sources * cap, sources * rows), 1)
        keep = (place_col == place_row // cap * rows + lax.rem(place_row, cap)).astype(jnp.float32)
        slots = jnp.dot(
            keep.astype(jnp.bfloat16), slots, preferred_element_type=jnp.float32
        ).astype(jnp.bfloat16)
    turned = jnp.transpose(slots.astype(jnp.float32)).astype(jnp.bfloat16)
    currents = jnp.concatenate(
        [turned[comp * steps : (comp + 1) * steps] for comp in range(4)], axis=1
    )
    depth = 4 * slots.shape[0]

    chunks = part.shape[0]
    half = chunks // 2
    piece = half // n_x
    own = piece // n_gy
    t_blocks = steps // 8
    width = piece // t_blocks * 128

    def fill(start):
        offset = pl.multiple_of(start // t_blocks * 128, 128)
        weights = steer[:, :, pl.ds(offset, width)].reshape(depth, width)
        out = jnp.dot(currents, weights, preferred_element_type=jnp.float32)
        for block in range(width // 128):
            part[pl.ds(start + block * t_blocks, t_blocks)] = out[
                :, block * 128 : (block + 1) * 128
            ].reshape(t_blocks, 8, 128)

    order_x = list(range(1, n_x)) + [0]
    order_z = list(range(1, n_gy)) + [0]
    sends = []

    def begin(copy):
        copy.start()
        sends.append(copy)
        return copy

    other = (mid * 2 + 1 - core, gy, gz)
    first = {}
    for dq in order_x:
        to = lax.rem(mid + dq, n_x)
        start = (1 - core) * half + to * piece
        fill(start)
        first[dq] = begin(
            remote(
                part.at[pl.ds(start, piece)], got_1.at[pl.ds(to * piece, piece)],
                core_send.at[dq], core_recv.at[dq], other,
            )
        )
    for dq in order_x:
        fill(core * half + lax.rem(mid + dq, n_x) * piece)
    second = {}
    for dq in order_x:
        to = lax.rem(mid + dq, n_x)
        start = core * half + to * piece
        first[dq].wait_recv()
        part[pl.ds(start, piece)] += got_1[pl.ds(to * piece, piece)]
        if dq:
            for dw in order_z:
                at = lax.rem(gy + dw, n_gy) * own
                second[dq, dw] = begin(
                    remote(
                        part.at[pl.ds(start + at, own)], got_2.at[dq - 1, pl.ds(at, own)],
                        mid_send.at[dq - 1, dw], mid_recv.at[dq - 1, dw], (to * 2 + core, gy, gz),
                    )
                )
    base = core * half + mid * piece
    third = {}
    for dw in order_z:
        to = lax.rem(gy + dw, n_gy)
        at = to * own
        for dq in range(1, n_x):
            second[dq, dw].wait_recv()
            part[pl.ds(base + at, own)] += got_2[dq - 1, pl.ds(at, own)]
        if dw:
            third[dw] = begin(
                remote(
                    part.at[pl.ds(base + at, own)], got_3.at[dw - 1],
                    end_send.at[dw - 1], end_recv.at[dw - 1], (gx, to, gz),
                )
            )
    mine = base + gy * own
    total = part[pl.ds(mine, own)]
    for dw in range(1, n_gy):
        third[dw].wait_recv()
        total = total + got_3[dw - 1]
    full[pl.ds(mine, own)] = total

    last = {}

    def to_core(start, dq, dw):
        block = full.at[pl.ds(start, own)]
        last[dq, dw] = begin(
            remote(block, block, back_c_send.at[dq, dw], back_c_recv.at[dq, dw], other)
        )

    wide = {}

    def to_mid(start, dw):
        block = full.at[pl.ds(start, own)]
        for dq in range(1, n_x):
            wide[dq, dw] = begin(
                remote(
                    block, block, back_x_send.at[dq - 1, dw], back_x_recv.at[dq - 1, dw],
                    (lax.rem(mid + dq, n_x) * 2 + core, gy, gz),
                )
            )

    long = {}
    for dw in range(1, n_gy):
        block = full.at[pl.ds(mine, own)]
        long[dw] = begin(
            remote(
                block, block, back_z_send.at[dw - 1], back_z_recv.at[dw - 1],
                (gx, lax.rem(gy + dw, n_gy), gz),
            )
        )
    to_mid(mine, 0)
    to_core(mine, 0, 0)
    for dw in range(1, n_gy):
        long[dw].wait_recv()
        start = base + lax.rem(gy + n_gy - dw, n_gy) * own
        to_mid(start, dw)
        to_core(start, 0, dw)
    for dw in range(n_gy):
        for dq in range(1, n_x):
            wide[dq, dw].wait_recv()
            start = (
                core * half
                + lax.rem(mid + n_x - dq, n_x) * piece
                + lax.rem(gy + n_gy - dw, n_gy) * own
            )
            to_core(start, dq, dw)
    for dw in range(n_gy):
        for dq in range(n_x):
            last[dq, dw].wait_recv()
    for block in range(chunks // t_blocks):
        values = full[pl.ds(block * t_blocks, t_blocks)].reshape(steps, 128)
        far_out[:, block * 128 : (block + 1) * 128] = jnp.dot(
            table_ref[...], values, precision=lax.Precision.HIGHEST,
            preferred_element_type=jnp.float32,
        )

    for copy in sends + tile_copies:
        copy.wait_send()
    store_poles.wait()

    @pl.when(gx > 0)
    def _():
        up_i.wait_send()

    @pl.when(gy > 0)
    def _():
        up_j.wait_send()

    @pl.when(gz > 0)
    def _():
        up_k.wait_send()

    @pl.when(gx < n_gx - 1)
    def _():
        down_i.wait_send()

    @pl.when(gy < n_gy - 1)
    def _():
        down_j.wait_send()

    @pl.when(gz < n_gz - 1)
    def _():
        down_k.wait_send()


def per_device(
    e_field, h_field, permittivity, wall_mask, poles, pole_decay, pole_gain,
    face_cells, owners, history, steering,
):
    n_gx, n_gy, n_gz = (lax.axis_size(axis) for axis in ("gx", "gy", "gz"))
    n_x = n_gx // 2
    count = face_cells.shape[0]
    steps = history.shape[0] + 1
    cap = steering.shape[1] // (n_gx * n_gz)
    rows = -(-cap // 16) * 16
    dirs = steering.shape[2]
    blocks = n_gx * n_gy
    mine = FREQS // blocks
    _, span_x, span_y, span_z = e_field.shape
    flat = span_x * span_y

    table = spectral_rows(FREQS, FREQS, steps)
    table = table.reshape(2, blocks, mine, steps).transpose(1, 0, 2, 3).reshape(blocks, 2 * mine, steps)
    rank = lax.axis_index("gx") * n_gy + lax.axis_index("gy")
    table = lax.dynamic_index_in_dim(jnp.asarray(table), rank, 0, keepdims=False)
    hist = jnp.pad(jnp.transpose(history, (2, 1, 0)), ((0, 0), (0, 0), (0, 1))).reshape(count, 4 * steps)

    chunks = steps // 8 * (dirs // 128)
    half = chunks // 2
    piece = half // n_x
    own = piece // n_gy
    f32, bf16 = jnp.float32, jnp.bfloat16
    dma = lambda *dims: pltpu.SemaphoreType.DMA(dims)
    vmem = pl.BlockSpec(memory_space=pltpu.VMEM)
    smem = pl.BlockSpec(memory_space=pltpu.SMEM)
    hbm = pl.BlockSpec(memory_space=pl.ANY)
    wide = max(n_x - 1, 1)
    e_next, h_next, far, poles_next = pl.pallas_call(
        functools.partial(kernel, n_gx, n_gy, n_gz, cap, rows),
        out_shape=(
            jax.ShapeDtypeStruct(e_field.shape, f32),
            jax.ShapeDtypeStruct(h_field.shape, f32),
            jax.ShapeDtypeStruct((2 * mine, dirs), f32),
            jax.ShapeDtypeStruct(poles.shape, f32),
        ),
        in_specs=[smem, smem] + [vmem] * 9 + [hbm, hbm],
        out_specs=(vmem, vmem, vmem, hbm),
        scratch_shapes=[
            pltpu.VMEM(poles.shape, f32),
            pltpu.VMEM(poles.shape, f32),
            pltpu.VMEM(steering.shape, bf16),
            pltpu.VMEM((2, span_x, span_z), f32),
            pltpu.VMEM((8, flat), f32),
            pltpu.VMEM((2, span_y, span_z), f32),
            pltpu.VMEM((2, span_x, span_z), f32),
            pltpu.VMEM((8, flat), f32),
            pltpu.VMEM((2, span_x, span_z), f32),
            pltpu.VMEM((8, flat), f32),
            pltpu.VMEM((2, span_y, span_z), f32),
            pltpu.VMEM((2, span_x, span_z), f32),
            pltpu.VMEM((8, flat), f32),
            pltpu.VMEM((n_gx, rows, 4 * steps), bf16),
            pltpu.VMEM((n_gx * n_gz, rows, 4 * steps), bf16),
            pltpu.VMEM((chunks, 8, 128), f32),
            pltpu.VMEM((half, 8, 128), f32),
            pltpu.VMEM((wide, piece, 8, 128), f32),
            pltpu.VMEM((n_gy - 1, own, 8, 128), f32),
            pltpu.VMEM((chunks, 8, 128), f32),
            dma(3), dma(6), dma(6), dma(n_gx * n_gz), dma(n_gx * n_gz),
            dma(n_x), dma(n_x), dma(wide, n_gy), dma(wide, n_gy), dma(n_gy - 1), dma(n_gy - 1),
            dma(n_gy - 1), dma(n_gy - 1), dma(wide, n_gy), dma(wide, n_gy), dma(n_x, n_gy), dma(n_x, n_gy),
        ],
        compiler_params=pltpu.CompilerParams(
            collective_id=0, has_side_effects=True, vmem_limit_bytes=32 * 1024 * 1024
        ),
    )(
        pole_decay, pole_gain, e_field, h_field, permittivity, wall_mask,
        face_cells[:, None], owners, owners.reshape(1, count), hist, table, poles, steering,
    )
    return (e_next, h_next, poles_next, far.reshape(2, mine, dirs))


def solution(mesh):
    return jax.shard_map(
        per_device,
        mesh=mesh,
        in_specs=(
            P(None, "gx", "gy", "gz"),
            P(None, "gx", "gy", "gz"),
            P("gx", "gy", "gz"),
            P("gx", "gy", "gz"),
            P(None, None, "gx", "gy", "gz"),
            P(),
            P(),
            P(("gx", "gy", "gz")),
            P(("gx", "gy", "gz"), None),
            P(None, None, ("gx", "gy", "gz")),
            P(None, ("gx", "gy"), "gz"),
        ),
        out_specs=(
            P(None, "gx", "gy", "gz"),
            P(None, "gx", "gy", "gz"),
            P(None, None, "gx", "gy", "gz"),
            P(None, ("gx", "gy"), "gz"),
        ),
        check_vma=False,
    )
```

```python
import functools
import math

import jax
import jax.numpy as jnp
import numpy as np
from jax import lax
from jax.experimental import pallas as pl
from jax.experimental.pallas import tpu as pltpu
from jax.sharding import PartitionSpec as P

FREQS = 256
MESH = pl.DeviceIdType.MESH


def spectral_rows(count, freqs, steps):
    times = np.arange(steps, dtype=np.float64)
    levels = np.arange(count, dtype=np.float64) + 0.5
    phase = math.pi / (2.0 * freqs) * levels[:, None] * times[None, :]
    scale = 1.0 / math.sqrt(steps)
    return np.stack([np.cos(phase) * scale, -np.sin(phase) * scale]).astype(np.float32)


def kernel(
    n_gx, n_gy, n_gz, cap, rows,
    decay_hbm, gain_hbm, e_hbm, h_hbm, perm_hbm, mask_hbm, cells_hbm, owners_hbm, hist_hbm,
    table_hbm, poles_hbm, steer_hbm,
    e_out, h_out, far_out, poles_out,
    decay, gain, e_ref, h_ref, perm_ref, mask_ref, cells_ref, own_ref, hist_ref, table_ref,
    poles, steer, edge_j, edge_k, got_i, got_j, got_k,
    low_j, low_k, from_i, from_j, from_k, compact, tile, part, got_1, got_2, got_3, full,
    local_sem, halo_send, halo_recv, tile_send, tile_recv,
    core_send, core_recv, mid_send, mid_recv, end_send, end_recv,
    back_z_send, back_z_recv, back_x_send, back_x_recv, back_c_send, back_c_recv,
):
    gx, gy, gz = lax.axis_index("gx"), lax.axis_index("gy"), lax.axis_index("gz")
    n_x = n_gx // 2
    core, mid = lax.rem(gx, 2), gx // 2
    span_x, span_y, span_z = e_ref.shape[1:]

    block = gx * n_gy + gy
    loads = [
        pltpu.make_async_copy(source, target, local_sem.at[index])
        for index, (source, target) in enumerate((
            (e_hbm, e_ref), (h_hbm, h_ref), (owners_hbm, own_ref), (hist_hbm, hist_ref),
            (cells_hbm, cells_ref), (steer_hbm, steer), (poles_hbm, poles), (perm_hbm, perm_ref),
            (mask_hbm, mask_ref), (decay_hbm, decay), (gain_hbm, gain),
            (table_hbm.at[block], table_ref),
        ))
    ]
    for load in loads:
        load.start()

    barrier = pltpu.get_barrier_semaphore()
    partners = 0
    for da in range(n_gx):
        for dz in range(n_gz):
            if da or dz:
                peer = (lax.rem(gx + da, n_gx), gy, lax.rem(gz + dz, n_gz))
                pl.semaphore_signal(barrier, inc=1, device_id=peer, device_id_type=MESH)
                partners += 1
    for dw in range(1, n_gy):
        peer = (gx, lax.rem(gy + dw, n_gy), gz)
        pl.semaphore_signal(barrier, inc=1, device_id=peer, device_id_type=MESH)
        partners += 1
    pl.semaphore_wait(barrier, partners)

    def remote(src, dst, send, recv, peer):
        return pltpu.make_async_remote_copy(
            src_ref=src, dst_ref=dst, send_sem=send, recv_sem=recv,
            device_id=peer, device_id_type=MESH,
        )

    flat = (span_x * span_y, span_z)
    cells = (span_x, span_y, span_z)

    def column(field, lane):
        return jnp.transpose(field.reshape(flat))[lane : lane + 1]

    def spread(row):
        return jnp.transpose(jnp.broadcast_to(row, (span_z, flat[0]))).reshape(cells)

    up_i = remote(e_ref.at[pl.ds(1, 2), 0], got_i, halo_send.at[0], halo_recv.at[0], (gx - 1, gy, gz))
    up_j = remote(edge_j, got_j, halo_send.at[1], halo_recv.at[1], (gx, gy - 1, gz))
    up_k = remote(edge_k, got_k, halo_send.at[2], halo_recv.at[2], (gx, gy, gz - 1))
    down_i = remote(
        h_out.at[pl.ds(1, 2), span_x - 1], from_i, halo_send.at[3], halo_recv.at[3], (gx + 1, gy, gz)
    )
    down_j = remote(low_j, from_j, halo_send.at[4], halo_recv.at[4], (gx, gy + 1, gz))
    down_k = remote(low_k, from_k, halo_send.at[5], halo_recv.at[5], (gx, gy, gz + 1))

    loads[0].wait()

    @pl.when(gz > 0)
    def _():
        edge_k[0:1] = column(e_ref[0], 0)
        edge_k[1:2] = column(e_ref[1], 0)
        edge_k[2:8] = jnp.zeros((6, flat[0]), jnp.float32)
        up_k.start()

    @pl.when(gx > 0)
    def _():
        up_i.start()

    @pl.when(gy > 0)
    def _():
        edge_j[0] = e_ref[0, :, 0, :]
        edge_j[1] = e_ref[2, :, 0, :]
        up_j.start()

    @pl.when(gx == n_gx - 1)
    def _():
        got_i[...] = jnp.zeros(got_i.shape, jnp.float32)

    @pl.when(gy == n_gy - 1)
    def _():
        got_j[...] = jnp.zeros(got_j.shape, jnp.float32)

    @pl.when(gz == n_gz - 1)
    def _():
        got_k[...] = jnp.zeros(got_k.shape, jnp.float32)

    @pl.when(gx == 0)
    def _():
        from_i[...] = jnp.zeros(from_i.shape, jnp.float32)

    @pl.when(gy == 0)
    def _():
        from_j[...] = jnp.zeros(from_j.shape, jnp.float32)

    @pl.when(gz == 0)
    def _():
        from_k[...] = jnp.zeros(from_k.shape, jnp.float32)

    for load in loads[1:5]:
        load.wait()
    count = own_ref.shape[1]
    sample = lax.broadcasted_iota(jnp.int32, (count, count), 0)
    other_sample = lax.broadcasted_iota(jnp.int32, (count, count), 1)

    def upright(row):
        kept = jnp.where(sample == other_sample, row.astype(jnp.float32), 0.0)
        return jnp.sum(kept, axis=1, keepdims=True).astype(jnp.int32)

    own_row = own_ref[...]
    same = jnp.where((upright(own_row) == own_row) & (sample < other_sample), 1.0, 0.0)
    rank = jnp.sum(same, axis=0, keepdims=True).astype(jnp.int32)
    slot = own_row * rows + rank
    place = (
        lax.broadcasted_iota(jnp.int32, (n_gx * rows, count), 0) == slot
    ).astype(jnp.float32).astype(jnp.bfloat16)

    at_j = lax.broadcasted_iota(jnp.int32, cells, 1)
    at_k = lax.broadcasted_iota(jnp.int32, cells, 2)

    def next_j(field, halo):
        return jnp.where(at_j == span_y - 1, halo[:, None, :], pltpu.roll(field, span_y - 1, 1))

    def next_k(field, halo):
        return jnp.where(at_k == span_z - 1, spread(halo), pltpu.roll(field, span_z - 1, 2))

    def prev_j(field, halo):
        return jnp.where(at_j == 0, halo[:, None, :], pltpu.roll(field, 1, 1))

    def prev_k(field, halo):
        return jnp.where(at_k == 0, spread(halo), pltpu.roll(field, 1, 2))

    @pl.when(gx < n_gx - 1)
    def _():
        up_i.wait_recv()

    @pl.when(gy < n_gy - 1)
    def _():
        up_j.wait_recv()

    @pl.when(gz < n_gz - 1)
    def _():
        up_k.wait_recv()

    ex, ey, ez = e_ref[0], e_ref[1], e_ref[2]
    ey_i = jnp.concatenate([ey[1:], got_i[0][None]], axis=0)
    ez_i = jnp.concatenate([ez[1:], got_i[1][None]], axis=0)
    mag_x = h_ref[0] - 0.5 * (next_j(ez, got_j[1]) - ez - (next_k(ey, got_k[1:2]) - ey))
    h_out[0] = mag_x
    mag_y = h_ref[1] - 0.5 * (next_k(ex, got_k[0:1]) - ex - (ez_i - ez))
    h_out[1] = mag_y
    mag_z = h_ref[2] - 0.5 * (ey_i - ey - (next_j(ex, got_j[0]) - ex))
    h_out[2] = mag_z

    @pl.when(gx < n_gx - 1)
    def _():
        down_i.start()

    @pl.when(gz < n_gz - 1)
    def _():
        low_k[0:1] = column(h_out[0], span_z - 1)
        low_k[1:2] = column(h_out[1], span_z - 1)
        low_k[2:8] = jnp.zeros((6, flat[0]), jnp.float32)
        down_k.start()

    @pl.when(gy < n_gy - 1)
    def _():
        low_j[0] = h_out[0, :, span_y - 1, :]
        low_j[1] = h_out[2, :, span_y - 1, :]
        down_j.start()

    for load in loads[6:11]:
        load.wait()

    @pl.when(gx > 0)
    def _():
        down_i.wait_recv()

    @pl.when(gy > 0)
    def _():
        down_j.wait_recv()

    @pl.when(gz > 0)
    def _():
        down_k.wait_recv()

    mag_x, mag_y, mag_z = h_out[0], h_out[1], h_out[2]
    mag_y_i = jnp.concatenate([from_i[0][None], mag_y[:-1]], axis=0)
    mag_z_i = jnp.concatenate([from_i[1][None], mag_z[:-1]], axis=0)
    drives = (
        mag_z - prev_j(mag_z, from_j[1]) - (mag_y - prev_k(mag_y, from_k[1:2])),
        mag_x - prev_k(mag_x, from_k[0:1]) - (mag_z - mag_z_i),
        mag_y - mag_y_i - (mag_x - prev_j(mag_x, from_j[0])),
    )
    wall = mask_ref[...] == 1
    half_eps = 0.5 / perm_ref[...]
    for comp in range(3):
        drive = drives[comp]
        total = None
        for pole in range(poles.shape[0]):
            state = decay[pole] * poles[pole, comp] + gain[pole] * drive
            poles_out[pole, comp] = state
            total = state if total is None else total + state
        e_out[comp] = jnp.where(wall, total, e_ref[comp] + half_eps * drive)

    cell = upright(cells_ref[...])
    row_hot = (
        lax.broadcasted_iota(jnp.int32, (count, flat[0]), 1) == cell // span_z
    ).astype(jnp.float32).astype(jnp.bfloat16)
    lane_hot = lax.broadcasted_iota(jnp.int32, (count, span_z), 1) == lax.rem(cell, span_z)
    past = hist_ref.shape[2]
    steps = past + 1
    lane = lax.broadcasted_iota(jnp.int32, (count, 4 * steps), 1)
    samples = jnp.zeros((count, 4 * steps), jnp.float32)
    step_in = lax.broadcasted_iota(jnp.int32, (past, 4 * steps), 0)
    step_out = lax.broadcasted_iota(jnp.int32, (past, 4 * steps), 1)
    for comp in range(4):
        spot = (step_out == step_in + comp * steps).astype(jnp.float32).astype(jnp.bfloat16)
        samples += jnp.dot(hist_ref[comp], spot, preferred_element_type=jnp.float32)
    for comp, field in enumerate((e_out[0], e_out[1], h_out[0], h_out[1])):
        found = jnp.dot(
            row_hot, field.reshape(flat).astype(jnp.bfloat16), preferred_element_type=jnp.float32
        )
        fresh = jnp.sum(jnp.where(lane_hot, found, 0.0), axis=1, keepdims=True)
        samples = jnp.where(lane == comp * steps + steps - 1, fresh, samples)
    packed = jnp.dot(
        place, samples.astype(jnp.bfloat16), preferred_element_type=jnp.float32
    ).astype(jnp.bfloat16)
    compact[...] = packed.reshape(compact.shape)
    me = gz * n_gx + gx
    tile_copies = []
    for da in range(n_gx):
        for dz in range(n_gz):
            to_x, to_z = lax.rem(gx + da, n_gx), lax.rem(gz + dz, n_gz)
            if da or dz:
                index = da * n_gz + dz
                copy = remote(
                    compact.at[to_x], tile.at[me], tile_send.at[index], tile_recv.at[index],
                    (to_x, gy, to_z),
                )
                copy.start()
                tile_copies.append(copy)
    tile[me] = compact[gx]
    loads[5].wait()
    loads[11].wait()
    for copy in tile_copies:
        copy.wait_recv()

    sources = n_gx * n_gz
    slots = tile[...].reshape(sources * rows, 4 * steps)
    if rows != cap:
        place_row = lax.broadcasted_iota(jnp.int32, (sources * cap, sources * rows), 0)
        place_col = lax.broadcasted_iota(jnp.int32, (sources * cap, sources * rows), 1)
        keep = (place_col == place_row // cap * rows + lax.rem(place_row, cap)).astype(jnp.float32)
        slots = jnp.dot(
            keep.astype(jnp.bfloat16), slots, preferred_element_type=jnp.float32
        ).astype(jnp.bfloat16)
    turned = jnp.transpose(slots.astype(jnp.float32)).astype(jnp.bfloat16)
    currents = jnp.concatenate(
        [turned[comp * steps : (comp + 1) * steps] for comp in range(4)], axis=1
    )
    depth = 4 * slots.shape[0]

    chunks = part.shape[0]
    half = chunks // 2
    piece = half // n_x
    own = piece // n_gy
    t_blocks = steps // 8
    width = piece // t_blocks * 128

    def fill(start):
        offset = pl.multiple_of(start // t_blocks * 128, 128)
        weights = steer[:, :, pl.ds(offset, width)].reshape(depth, width)
        out = jnp.dot(currents, weights, preferred_element_type=jnp.float32)
        for block in range(width // 128):
            part[pl.ds(start + block * t_blocks, t_blocks)] = out[
                :, block * 128 : (block + 1) * 128
            ].reshape(t_blocks, 8, 128)

    order_x = list(range(1, n_x)) + [0]
    order_z = list(range(1, n_gy)) + [0]
    sends = []

    def begin(copy):
        copy.start()
        sends.append(copy)
        return copy

    other = (mid * 2 + 1 - core, gy, gz)
    first = {}
    for dq in order_x:
        to = lax.rem(mid + dq, n_x)
        start = (1 - core) * half + to * piece
        fill(start)
        first[dq] = begin(
            remote(
                part.at[pl.ds(start, piece)], got_1.at[pl.ds(to * piece, piece)],
                core_send.at[dq], core_recv.at[dq], other,
            )
        )
    for dq in order_x:
        fill(core * half + lax.rem(mid + dq, n_x) * piece)
    second = {}
    for dq in order_x:
        to = lax.rem(mid + dq, n_x)
        start = core * half + to * piece
        first[dq].wait_recv()
        part[pl.ds(start, piece)] += got_1[pl.ds(to * piece, piece)]
        if dq:
            for dw in order_z:
                at = lax.rem(gy + dw, n_gy) * own
                second[dq, dw] = begin(
                    remote(
                        part.at[pl.ds(start + at, own)], got_2.at[dq - 1, pl.ds(at, own)],
                        mid_send.at[dq - 1, dw], mid_recv.at[dq - 1, dw], (to * 2 + core, gy, gz),
                    )
                )
    base = core * half + mid * piece
    third = {}
    for dw in order_z:
        to = lax.rem(gy + dw, n_gy)
        at = to * own
        for dq in range(1, n_x):
            second[dq, dw].wait_recv()
            part[pl.ds(base + at, own)] += got_2[dq - 1, pl.ds(at, own)]
        if dw:
            third[dw] = begin(
                remote(
                    part.at[pl.ds(base + at, own)], got_3.at[dw - 1],
                    end_send.at[dw - 1], end_recv.at[dw - 1], (gx, to, gz),
                )
            )
    mine = base + gy * own
    total = part[pl.ds(mine, own)]
    for dw in range(1, n_gy):
        third[dw].wait_recv()
        total = total + got_3[dw - 1]
    full[pl.ds(mine, own)] = total

    last = {}

    def to_core(start, dq, dw):
        block = full.at[pl.ds(start, own)]
        last[dq, dw] = begin(
            remote(block, block, back_c_send.at[dq, dw], back_c_recv.at[dq, dw], other)
        )

    wide = {}

    def to_mid(start, dw):
        block = full.at[pl.ds(start, own)]
        for dq in range(1, n_x):
            wide[dq, dw] = begin(
                remote(
                    block, block, back_x_send.at[dq - 1, dw], back_x_recv.at[dq - 1, dw],
                    (lax.rem(mid + dq, n_x) * 2 + core, gy, gz),
                )
            )

    long = {}
    for dw in range(1, n_gy):
        block = full.at[pl.ds(mine, own)]
        long[dw] = begin(
            remote(
                block, block, back_z_send.at[dw - 1], back_z_recv.at[dw - 1],
                (gx, lax.rem(gy + dw, n_gy), gz),
            )
        )
    to_mid(mine, 0)
    to_core(mine, 0, 0)
    for dw in range(1, n_gy):
        long[dw].wait_recv()
        start = base + lax.rem(gy + n_gy - dw, n_gy) * own
        to_mid(start, dw)
        to_core(start, 0, dw)
    for dw in range(n_gy):
        for dq in range(1, n_x):
            wide[dq, dw].wait_recv()
            start = (
                core * half
                + lax.rem(mid + n_x - dq, n_x) * piece
                + lax.rem(gy + n_gy - dw, n_gy) * own
            )
            to_core(start, dq, dw)
    for dw in range(n_gy):
        for dq in range(n_x):
            last[dq, dw].wait_recv()
    for block in range(chunks // t_blocks):
        values = full[pl.ds(block * t_blocks, t_blocks)].reshape(steps, 128)
        far_out[:, block * 128 : (block + 1) * 128] = jnp.dot(
            table_ref[...], values, precision=lax.Precision.HIGHEST,
            preferred_element_type=jnp.float32,
        )

    for copy in sends + tile_copies:
        copy.wait_send()

    @pl.when(gx > 0)
    def _():
        up_i.wait_send()

    @pl.when(gy > 0)
    def _():
        up_j.wait_send()

    @pl.when(gz > 0)
    def _():
        up_k.wait_send()

    @pl.when(gx < n_gx - 1)
    def _():
        down_i.wait_send()

    @pl.when(gy < n_gy - 1)
    def _():
        down_j.wait_send()

    @pl.when(gz < n_gz - 1)
    def _():
        down_k.wait_send()


def hand_out(*refs):
    copies = [
        pltpu.make_async_copy(refs[index], refs[4 + index], refs[8].at[index]) for index in range(4)
    ]
    for copy in copies:
        copy.start()
    for copy in copies:
        copy.wait()


def per_device(
    e_field, h_field, permittivity, wall_mask, poles, pole_decay, pole_gain,
    face_cells, owners, history, steering,
):
    n_gx, n_gy, n_gz = (lax.axis_size(axis) for axis in ("gx", "gy", "gz"))
    n_x = n_gx // 2
    count = face_cells.shape[0]
    steps = history.shape[0] + 1
    cap = steering.shape[1] // (n_gx * n_gz)
    rows = -(-cap // 16) * 16
    dirs = steering.shape[2]
    blocks = n_gx * n_gy
    mine = FREQS // blocks
    _, span_x, span_y, span_z = e_field.shape
    flat = span_x * span_y

    table = spectral_rows(FREQS, FREQS, steps)
    table = table.reshape(2, blocks, mine, steps).transpose(1, 0, 2, 3).reshape(blocks, 2 * mine, steps)
    hist = jnp.transpose(history, (1, 2, 0))

    chunks = steps // 8 * (dirs // 128)
    half = chunks // 2
    piece = half // n_x
    own = piece // n_gy
    f32, bf16 = jnp.float32, jnp.bfloat16
    dma = lambda *dims: pltpu.SemaphoreType.DMA(dims)
    vmem = pl.BlockSpec(memory_space=pltpu.VMEM)
    hbm = pl.BlockSpec(memory_space=pltpu.HBM)
    wide = max(n_x - 1, 1)
    e_next, h_next, far, poles_next = pl.pallas_call(
        functools.partial(kernel, n_gx, n_gy, n_gz, cap, rows),
        out_shape=(
            jax.ShapeDtypeStruct(e_field.shape, f32),
            jax.ShapeDtypeStruct(h_field.shape, f32),
            jax.ShapeDtypeStruct((2 * mine, dirs), f32),
            jax.ShapeDtypeStruct(poles.shape, f32),
        ),
        in_specs=[hbm] * 12,
        out_specs=(vmem, vmem, vmem, vmem),
        scratch_shapes=[
            pltpu.SMEM(pole_decay.shape, f32),
            pltpu.SMEM(pole_gain.shape, f32),
            pltpu.VMEM(e_field.shape, f32),
            pltpu.VMEM(h_field.shape, f32),
            pltpu.VMEM(permittivity.shape, f32),
            pltpu.VMEM(wall_mask.shape, jnp.int32),
            pltpu.VMEM((1, count), jnp.int32),
            pltpu.VMEM((1, count), jnp.int32),
            pltpu.VMEM(hist.shape, bf16),
            pltpu.VMEM(table.shape[1:], f32),
            pltpu.VMEM(poles.shape, f32),
            pltpu.VMEM(steering.shape, bf16),
            pltpu.VMEM((2, span_x, span_z), f32),
            pltpu.VMEM((8, flat), f32),
            pltpu.VMEM((2, span_y, span_z), f32),
            pltpu.VMEM((2, span_x, span_z), f32),
            pltpu.VMEM((8, flat), f32),
            pltpu.VMEM((2, span_x, span_z), f32),
            pltpu.VMEM((8, flat), f32),
            pltpu.VMEM((2, span_y, span_z), f32),
            pltpu.VMEM((2, span_x, span_z), f32),
            pltpu.VMEM((8, flat), f32),
            pltpu.VMEM((n_gx, rows, 4 * steps), bf16),
            pltpu.VMEM((n_gx * n_gz, rows, 4 * steps), bf16),
            pltpu.VMEM((chunks, 8, 128), f32),
            pltpu.VMEM((half, 8, 128), f32),
            pltpu.VMEM((wide, piece, 8, 128), f32),
            pltpu.VMEM((n_gy - 1, own, 8, 128), f32),
            pltpu.VMEM((chunks, 8, 128), f32),
            dma(12), dma(6), dma(6), dma(n_gx * n_gz), dma(n_gx * n_gz),
            dma(n_x), dma(n_x), dma(wide, n_gy), dma(wide, n_gy), dma(n_gy - 1), dma(n_gy - 1),
            dma(n_gy - 1), dma(n_gy - 1), dma(wide, n_gy), dma(wide, n_gy), dma(n_x, n_gy), dma(n_x, n_gy),
        ],
        compiler_params=pltpu.CompilerParams(
            collective_id=0, has_side_effects=True, vmem_limit_bytes=32 * 1024 * 1024
        ),
    )(
        *(
            pltpu.with_memory_space_constraint(operand, pltpu.HBM)
            for operand in (
                pole_decay, pole_gain, e_field, h_field, permittivity, wall_mask, face_cells.reshape(1, count),
                owners.reshape(1, count), hist, jnp.asarray(table), poles, steering,
            )
        )
    )
    results = (e_next, h_next, poles_next, far)
    e_next, h_next, poles_next, far = pl.pallas_call(
        hand_out,
        out_shape=tuple(jax.ShapeDtypeStruct(result.shape, f32) for result in results),
        in_specs=[pl.BlockSpec(memory_space=pl.ANY)] * 4,
        out_specs=(hbm,) * 4,
        scratch_shapes=[dma(4)],
    )(*results)
    return (e_next, h_next, poles_next, far.reshape(2, mine, dirs))


def solution(mesh):
    return jax.shard_map(
        per_device,
        mesh=mesh,
        in_specs=(
            P(None, "gx", "gy", "gz"),
            P(None, "gx", "gy", "gz"),
            P("gx", "gy", "gz"),
            P("gx", "gy", "gz"),
            P(None, None, "gx", "gy", "gz"),
            P(),
            P(),
            P(("gx", "gy", "gz")),
            P(("gx", "gy", "gz"), None),
            P(None, None, ("gx", "gy", "gz")),
            P(None, ("gx", "gy"), "gz"),
        ),
        out_specs=(
            P(None, "gx", "gy", "gz"),
            P(None, "gx", "gy", "gz"),
            P(None, None, "gx", "gy", "gz"),
            P(None, ("gx", "gy"), "gz"),
        ),
        check_vma=False,
    )
```

```python
import functools
import math

import jax
import jax.numpy as jnp
import numpy as np
from jax import lax
from jax.experimental import pallas as pl
from jax.experimental.pallas import tpu as pltpu
from jax.sharding import PartitionSpec as P

FREQS = 256
MESH = pl.DeviceIdType.MESH


def spectral_rows(count, freqs, steps):
    times = np.arange(steps, dtype=np.float64)
    levels = np.arange(count, dtype=np.float64) + 0.5
    phase = math.pi / (2.0 * freqs) * levels[:, None] * times[None, :]
    scale = 1.0 / math.sqrt(steps)
    return np.stack([np.cos(phase) * scale, -np.sin(phase) * scale]).astype(np.float32)


def kernel(
    n_gx, n_gy, n_gz, cap, rows,
    decay_hbm, gain_hbm, e_hbm, h_hbm, perm_hbm, mask_hbm, cells_hbm, owners_hbm, hist_hbm,
    table_hbm, poles_hbm, steer_hbm,
    e_out, h_out, far_out, poles_out,
    decay, gain, e_ref, h_ref, perm_ref, mask_ref, cells_ref, own_ref, hist_ref, table_ref,
    poles, steer, edge_j, edge_k, got_i, got_j, got_k,
    low_j, low_k, from_i, from_j, from_k, compact, tile, part, got_1, got_2, got_3, full, new_out, new_in, new_row, got_row,
    local_sem, halo_send, halo_recv, tile_send, tile_recv,
    core_send, core_recv, mid_send, mid_recv, end_send, end_recv,
    new_send, new_recv, row_send, row_recv, back_z_send, back_z_recv, back_x_send, back_x_recv, back_c_send, back_c_recv,
):
    gx, gy, gz = lax.axis_index("gx"), lax.axis_index("gy"), lax.axis_index("gz")
    n_x = n_gx // 2
    core, mid = lax.rem(gx, 2), gx // 2
    span_x, span_y, span_z = e_ref.shape[1:]
    count, past = hist_ref.shape[1:]
    steps = past + 1
    chunks = part.shape[0]
    half = chunks // 2
    piece = half // n_x
    own = piece // n_gy
    t_blocks = steps // 8
    width = piece // t_blocks * 128
    early = own % t_blocks == 0 and rows == cap

    block = gx * n_gy + gy
    loads = [
        pltpu.make_async_copy(source, target, local_sem.at[index])
        for index, (source, target) in enumerate((
            (e_hbm, e_ref), (h_hbm, h_ref), (owners_hbm, own_ref), (hist_hbm, hist_ref),
            (cells_hbm, cells_ref), (steer_hbm, steer), (poles_hbm, poles), (perm_hbm, perm_ref),
            (mask_hbm, mask_ref), (decay_hbm, decay), (gain_hbm, gain),
            (table_hbm.at[block], table_ref),
        ))
    ]
    for load in loads:
        load.start()

    barrier = pltpu.get_barrier_semaphore()
    partners = 0
    for da in range(n_gx):
        for dz in range(n_gz):
            if da or dz:
                peer = (lax.rem(gx + da, n_gx), gy, lax.rem(gz + dz, n_gz))
                pl.semaphore_signal(barrier, inc=1, device_id=peer, device_id_type=MESH)
                partners += 1
    for da in range(n_gx if early else 1):
        for dw in range(1, n_gy):
            peer = (lax.rem(gx + da, n_gx), lax.rem(gy + dw, n_gy), gz)
            pl.semaphore_signal(barrier, inc=1, device_id=peer, device_id_type=MESH)
            partners += 1

    def remote(src, dst, send, recv, peer):
        return pltpu.make_async_remote_copy(
            src_ref=src, dst_ref=dst, send_sem=send, recv_sem=recv,
            device_id=peer, device_id_type=MESH,
        )

    flat = (span_x * span_y, span_z)
    cells = (span_x, span_y, span_z)

    def column(field, lane):
        return jnp.transpose(field.reshape(flat))[lane : lane + 1]

    def spread(row):
        return jnp.transpose(jnp.broadcast_to(row, (span_z, flat[0]))).reshape(cells)

    up_i = remote(e_ref.at[pl.ds(1, 2), 0], got_i, halo_send.at[0], halo_recv.at[0], (gx - 1, gy, gz))
    up_j = remote(edge_j, got_j, halo_send.at[1], halo_recv.at[1], (gx, gy - 1, gz))
    up_k = remote(edge_k, got_k, halo_send.at[2], halo_recv.at[2], (gx, gy, gz - 1))
    down_i = remote(
        h_out.at[pl.ds(1, 2), span_x - 1], from_i, halo_send.at[3], halo_recv.at[3], (gx + 1, gy, gz)
    )
    down_j = remote(low_j, from_j, halo_send.at[4], halo_recv.at[4], (gx, gy + 1, gz))
    down_k = remote(low_k, from_k, halo_send.at[5], halo_recv.at[5], (gx, gy, gz + 1))

    loads[0].wait()
    edge_k[0:1] = column(e_ref[0], 0)
    edge_k[1:2] = column(e_ref[1], 0)
    edge_k[2:8] = jnp.zeros((6, flat[0]), jnp.float32)
    edge_j[0] = e_ref[0, :, 0, :]
    edge_j[1] = e_ref[2, :, 0, :]

    for load in loads[1:5]:
        load.wait()
    sample = lax.broadcasted_iota(jnp.int32, (count, count), 0)
    other_sample = lax.broadcasted_iota(jnp.int32, (count, count), 1)

    def upright(row):
        kept = jnp.where(sample == other_sample, row.astype(jnp.float32), 0.0)
        return jnp.sum(kept, axis=1, keepdims=True).astype(jnp.int32)

    own_row = own_ref[...]
    same = jnp.where((upright(own_row) == own_row) & (sample < other_sample), 1.0, 0.0)
    rank = jnp.sum(same, axis=0, keepdims=True).astype(jnp.int32)
    slot = own_row * rows + rank
    place = (
        lax.broadcasted_iota(jnp.int32, (n_gx * rows, count), 0) == slot
    ).astype(jnp.float32).astype(jnp.bfloat16)

    lane = lax.broadcasted_iota(jnp.int32, (count, 4 * steps), 1)
    samples = jnp.zeros((count, 4 * steps), jnp.float32)
    step_in = lax.broadcasted_iota(jnp.int32, (past, 4 * steps), 0)
    step_out = lax.broadcasted_iota(jnp.int32, (past, 4 * steps), 1)
    for comp in range(4):
        spot = (step_out == step_in + comp * steps).astype(jnp.float32).astype(jnp.bfloat16)
        samples += jnp.dot(hist_ref[comp], spot, preferred_element_type=jnp.float32)
    me = gz * n_gx + gx

    def send(values, source, target, send_sem, recv_sem):
        packed = jnp.dot(
            place, values.astype(jnp.bfloat16), preferred_element_type=jnp.float32
        ).astype(jnp.bfloat16)
        source[...] = packed.reshape(source.shape)
        copies = []
        for da in range(n_gx):
            for dz in range(n_gz):
                to_x, to_z = lax.rem(gx + da, n_gx), lax.rem(gz + dz, n_gz)
                if da or dz:
                    index = da * n_gz + dz
                    copy = remote(
                        source.at[to_x], target.at[me], send_sem.at[index], recv_sem.at[index],
                        (to_x, gy, to_z),
                    )
                    copy.start()
                    copies.append(copy)
        target[me] = source[gx]
        return copies

    def send_tiles():
        return send(samples, compact, tile, tile_send, tile_recv)

    pl.semaphore_wait(barrier, partners)

    @pl.when(gz > 0)
    def _():
        up_k.start()

    @pl.when(gx > 0)
    def _():
        up_i.start()

    @pl.when(gy > 0)
    def _():
        up_j.start()

    if early:
        tile_copies = send_tiles()

    @pl.when(gx == n_gx - 1)
    def _():
        got_i[...] = jnp.zeros(got_i.shape, jnp.float32)

    @pl.when(gy == n_gy - 1)
    def _():
        got_j[...] = jnp.zeros(got_j.shape, jnp.float32)

    @pl.when(gz == n_gz - 1)
    def _():
        got_k[...] = jnp.zeros(got_k.shape, jnp.float32)

    @pl.when(gx == 0)
    def _():
        from_i[...] = jnp.zeros(from_i.shape, jnp.float32)

    @pl.when(gy == 0)
    def _():
        from_j[...] = jnp.zeros(from_j.shape, jnp.float32)

    @pl.when(gz == 0)
    def _():
        from_k[...] = jnp.zeros(from_k.shape, jnp.float32)

    at_j = lax.broadcasted_iota(jnp.int32, cells, 1)
    at_k = lax.broadcasted_iota(jnp.int32, cells, 2)

    def next_j(field, halo):
        return jnp.where(at_j == span_y - 1, halo[:, None, :], pltpu.roll(field, span_y - 1, 1))

    def next_k(field, halo):
        return jnp.where(at_k == span_z - 1, spread(halo), pltpu.roll(field, span_z - 1, 2))

    def prev_j(field, halo):
        return jnp.where(at_j == 0, halo[:, None, :], pltpu.roll(field, 1, 1))

    def prev_k(field, halo):
        return jnp.where(at_k == 0, spread(halo), pltpu.roll(field, 1, 2))

    @pl.when(gx < n_gx - 1)
    def _():
        up_i.wait_recv()

    @pl.when(gy < n_gy - 1)
    def _():
        up_j.wait_recv()

    @pl.when(gz < n_gz - 1)
    def _():
        up_k.wait_recv()

    ex, ey, ez = e_ref[0], e_ref[1], e_ref[2]
    ey_i = jnp.concatenate([ey[1:], got_i[0][None]], axis=0)
    ez_i = jnp.concatenate([ez[1:], got_i[1][None]], axis=0)
    mag_x = h_ref[0] - 0.5 * (next_j(ez, got_j[1]) - ez - (next_k(ey, got_k[1:2]) - ey))
    h_out[0] = mag_x
    mag_y = h_ref[1] - 0.5 * (next_k(ex, got_k[0:1]) - ex - (ez_i - ez))
    h_out[1] = mag_y
    mag_z = h_ref[2] - 0.5 * (ey_i - ey - (next_j(ex, got_j[0]) - ex))
    h_out[2] = mag_z

    @pl.when(gx < n_gx - 1)
    def _():
        down_i.start()

    @pl.when(gz < n_gz - 1)
    def _():
        low_k[0:1] = column(h_out[0], span_z - 1)
        low_k[1:2] = column(h_out[1], span_z - 1)
        low_k[2:8] = jnp.zeros((6, flat[0]), jnp.float32)
        down_k.start()

    @pl.when(gy < n_gy - 1)
    def _():
        low_j[0] = h_out[0, :, span_y - 1, :]
        low_j[1] = h_out[2, :, span_y - 1, :]
        down_j.start()

    order_x = list(range(1, n_x)) + [0]
    order_z = list(range(1, n_gy)) + [0]
    sends = []

    def begin(copy):
        copy.start()
        sends.append(copy)
        return copy

    other = (mid * 2 + 1 - core, gy, gz)
    second = {}

    def first_half(copies):
        loads[5].wait()
        loads[11].wait()
        for copy in copies:
            copy.wait_recv()

        sources = n_gx * n_gz
        slots = tile[...].reshape(sources * rows, 4 * steps)
        if rows != cap:
            place_row = lax.broadcasted_iota(jnp.int32, (sources * cap, sources * rows), 0)
            place_col = lax.broadcasted_iota(jnp.int32, (sources * cap, sources * rows), 1)
            keep = (place_col == place_row // cap * rows + lax.rem(place_row, cap)).astype(jnp.float32)
            slots = jnp.dot(
                keep.astype(jnp.bfloat16), slots, preferred_element_type=jnp.float32
            ).astype(jnp.bfloat16)
        turned = jnp.transpose(slots.astype(jnp.float32)).astype(jnp.bfloat16)
        currents = jnp.concatenate(
            [turned[comp * steps : (comp + 1) * steps] for comp in range(4)], axis=1
        )
        depth = 4 * slots.shape[0]

        def fill(start):
            offset = pl.multiple_of(start // t_blocks * 128, 128)
            weights = steer[:, :, pl.ds(offset, width)].reshape(depth, width)
            out = jnp.dot(currents, weights, preferred_element_type=jnp.float32)
            for block in range(width // 128):
                part[pl.ds(start + block * t_blocks, t_blocks)] = out[
                    :, block * 128 : (block + 1) * 128
                ].reshape(t_blocks, 8, 128)

        first = {}
        for dq in order_x:
            to = lax.rem(mid + dq, n_x)
            start = (1 - core) * half + to * piece
            fill(start)
            first[dq] = begin(
                remote(
                    part.at[pl.ds(start, piece)], got_1.at[pl.ds(to * piece, piece)],
                    core_send.at[dq], core_recv.at[dq], other,
                )
            )
        for dq in order_x:
            fill(core * half + lax.rem(mid + dq, n_x) * piece)
        for dq in order_x:
            to = lax.rem(mid + dq, n_x)
            start = core * half + to * piece
            first[dq].wait_recv()
            part[pl.ds(start, piece)] += got_1[pl.ds(to * piece, piece)]
            if dq:
                for dw in order_z:
                    at = lax.rem(gy + dw, n_gy) * own
                    second[dq, dw] = begin(
                        remote(
                            part.at[pl.ds(start + at, own)], got_2.at[dq - 1, pl.ds(at, own)],
                            mid_send.at[dq - 1, dw], mid_recv.at[dq - 1, dw], (to * 2 + core, gy, gz),
                        )
                    )

    if early:
        first_half(tile_copies)

    for load in loads[6:11]:
        load.wait()

    @pl.when(gx > 0)
    def _():
        down_i.wait_recv()

    @pl.when(gy > 0)
    def _():
        down_j.wait_recv()

    @pl.when(gz > 0)
    def _():
        down_k.wait_recv()

    mag_x, mag_y, mag_z = h_out[0], h_out[1], h_out[2]
    mag_y_i = jnp.concatenate([from_i[0][None], mag_y[:-1]], axis=0)
    mag_z_i = jnp.concatenate([from_i[1][None], mag_z[:-1]], axis=0)
    drives = (
        mag_z - prev_j(mag_z, from_j[1]) - (mag_y - prev_k(mag_y, from_k[1:2])),
        mag_x - prev_k(mag_x, from_k[0:1]) - (mag_z - mag_z_i),
        mag_y - mag_y_i - (mag_x - prev_j(mag_x, from_j[0])),
    )
    wall = mask_ref[...] == 1
    half_eps = 0.5 / perm_ref[...]
    for comp in range(3):
        drive = drives[comp]
        total = None
        for pole in range(poles.shape[0]):
            state = decay[pole] * poles[pole, comp] + gain[pole] * drive
            poles_out[pole, comp] = state
            total = state if total is None else total + state
        e_out[comp] = jnp.where(wall, total, e_ref[comp] + half_eps * drive)

    cell = upright(cells_ref[...])
    row_hot = (
        lax.broadcasted_iota(jnp.int32, (count, flat[0]), 1) == cell // span_z
    ).astype(jnp.float32).astype(jnp.bfloat16)
    lane_hot = lax.broadcasted_iota(jnp.int32, (count, span_z), 1) == lax.rem(cell, span_z)
    fresh_lane = lax.broadcasted_iota(jnp.int32, (count, 128), 1)
    fresh_all = jnp.zeros((count, 128), jnp.float32)
    for comp, field in enumerate((e_out[0], e_out[1], h_out[0], h_out[1])):
        found = jnp.dot(
            row_hot, field.reshape(flat).astype(jnp.bfloat16), preferred_element_type=jnp.float32
        )
        fresh = jnp.sum(jnp.where(lane_hot, found, 0.0), axis=1, keepdims=True)
        if early:
            fresh_all = jnp.where(fresh_lane == comp, fresh, fresh_all)
        else:
            samples = jnp.where(lane == comp * steps + steps - 1, fresh, samples)
    if early:
        new_copies = send(fresh_all, new_out, new_in, new_send, new_recv)
    else:
        tile_copies = send_tiles()
        first_half(tile_copies)
    base = core * half + mid * piece
    third = {}
    for dw in order_z:
        to = lax.rem(gy + dw, n_gy)
        at = to * own
        for dq in range(1, n_x):
            second[dq, dw].wait_recv()
            part[pl.ds(base + at, own)] += got_2[dq - 1, pl.ds(at, own)]
        if dw:
            third[dw] = begin(
                remote(
                    part.at[pl.ds(base + at, own)], got_3.at[dw - 1],
                    end_send.at[dw - 1], end_recv.at[dw - 1], (gx, to, gz),
                )
            )
    mine = base + gy * own
    rows_out = {}
    if early:
        for copy in new_copies:
            copy.wait_recv()
        turned = jnp.transpose(new_in[...].reshape(n_gx * n_gz * rows, 128).astype(jnp.float32))
        line = jnp.concatenate([turned[comp : comp + 1] for comp in range(4)], axis=1)
        line = jnp.broadcast_to(line, (16, line.shape[1])).astype(jnp.bfloat16)
        for start in range(0, new_row.shape[0], 4):
            weights = steer[:, :, start * 128 : (start + 4) * 128].reshape(line.shape[1], 512)
            out = jnp.dot(line, weights, preferred_element_type=jnp.float32)
            for index in range(4):
                new_row[start + index] = out[0:1, index * 128 : (index + 1) * 128]
        count_d = own // t_blocks
        for da in range(n_gx):
            for dw in range(n_gy):
                if da or dw:
                    to_x, to_y = lax.rem(gx + da, n_gx), lax.rem(gy + dw, n_gy)
                    begin_d = (
                        lax.rem(to_x, 2) * half + to_x // 2 * piece + to_y * own
                    ) // t_blocks
                    index = da * n_gy + dw
                    rows_out[index] = begin(
                        remote(
                            new_row.at[pl.ds(begin_d, count_d)], got_row.at[index],
                            row_send.at[index], row_recv.at[index], (to_x, to_y, gz),
                        )
                    )
    total = part[pl.ds(mine, own)]
    for dw in range(1, n_gy):
        third[dw].wait_recv()
        total = total + got_3[dw - 1]
    full[pl.ds(mine, own)] = total
    if early:
        added = new_row[pl.ds(mine // t_blocks, count_d)]
        for index in rows_out:
            rows_out[index].wait_recv()
            added = added + got_row[index]
        for index in range(count_d):
            full[mine + (index + 1) * t_blocks - 1, 7:8, :] += added[index]

    def transform(start, many):
        for index in range(many // t_blocks):
            at = start // t_blocks + index
            values = full[pl.ds(at * t_blocks, t_blocks)].reshape(steps, 128)
            if not isinstance(at, int):
                at = pl.multiple_of(at * 128, 128)
            else:
                at = at * 128
            far_out[:, pl.ds(at, 128)] = jnp.dot(
                table_ref[...], values, precision=lax.Precision.HIGHEST,
                preferred_element_type=jnp.float32,
            )

    def arrived(start):
        if early:
            transform(start, own)

    last = {}

    def to_core(start, dq, dw):
        block = full.at[pl.ds(start, own)]
        last[dq, dw] = begin(
            remote(block, block, back_c_send.at[dq, dw], back_c_recv.at[dq, dw], other)
        )

    wide = {}

    def to_mid(start, dw):
        block = full.at[pl.ds(start, own)]
        for dq in range(1, n_x):
            wide[dq, dw] = begin(
                remote(
                    block, block, back_x_send.at[dq - 1, dw], back_x_recv.at[dq - 1, dw],
                    (lax.rem(mid + dq, n_x) * 2 + core, gy, gz),
                )
            )

    long = {}
    for dw in range(1, n_gy):
        block = full.at[pl.ds(mine, own)]
        long[dw] = begin(
            remote(
                block, block, back_z_send.at[dw - 1], back_z_recv.at[dw - 1],
                (gx, lax.rem(gy + dw, n_gy), gz),
            )
        )
    to_mid(mine, 0)
    to_core(mine, 0, 0)
    arrived(mine)
    for dw in range(1, n_gy):
        long[dw].wait_recv()
        start = base + lax.rem(gy + n_gy - dw, n_gy) * own
        to_mid(start, dw)
        to_core(start, 0, dw)
        arrived(start)
    for dw in range(n_gy):
        for dq in range(1, n_x):
            wide[dq, dw].wait_recv()
            start = (
                core * half
                + lax.rem(mid + n_x - dq, n_x) * piece
                + lax.rem(gy + n_gy - dw, n_gy) * own
            )
            to_core(start, dq, dw)
            arrived(start)
    for dw in range(n_gy):
        for dq in range(n_x):
            last[dq, dw].wait_recv()
            arrived(
                (1 - core) * half
                + lax.rem(mid + n_x - dq, n_x) * piece
                + lax.rem(gy + n_gy - dw, n_gy) * own
            )
    if not early:
        transform(0, chunks)

    for copy in sends + tile_copies + (new_copies if early else []):
        copy.wait_send()

    @pl.when(gx > 0)
    def _():
        up_i.wait_send()

    @pl.when(gy > 0)
    def _():
        up_j.wait_send()

    @pl.when(gz > 0)
    def _():
        up_k.wait_send()

    @pl.when(gx < n_gx - 1)
    def _():
        down_i.wait_send()

    @pl.when(gy < n_gy - 1)
    def _():
        down_j.wait_send()

    @pl.when(gz < n_gz - 1)
    def _():
        down_k.wait_send()


def hand_out(*refs):
    copies = [
        pltpu.make_async_copy(refs[index], refs[4 + index], refs[8].at[index]) for index in range(4)
    ]
    for copy in copies:
        copy.start()
    for copy in copies:
        copy.wait()


def per_device(
    e_field, h_field, permittivity, wall_mask, poles, pole_decay, pole_gain,
    face_cells, owners, history, steering,
):
    n_gx, n_gy, n_gz = (lax.axis_size(axis) for axis in ("gx", "gy", "gz"))
    n_x = n_gx // 2
    count = face_cells.shape[0]
    steps = history.shape[0] + 1
    cap = steering.shape[1] // (n_gx * n_gz)
    rows = -(-cap // 16) * 16
    dirs = steering.shape[2]
    blocks = n_gx * n_gy
    mine = FREQS // blocks
    _, span_x, span_y, span_z = e_field.shape
    flat = span_x * span_y

    table = spectral_rows(FREQS, FREQS, steps)
    table = table.reshape(2, blocks, mine, steps).transpose(1, 0, 2, 3).reshape(blocks, 2 * mine, steps)
    hist = jnp.transpose(history, (1, 2, 0))

    chunks = steps // 8 * (dirs // 128)
    half = chunks // 2
    piece = half // n_x
    own = piece // n_gy
    f32, bf16 = jnp.float32, jnp.bfloat16
    dma = lambda *dims: pltpu.SemaphoreType.DMA(dims)
    vmem = pl.BlockSpec(memory_space=pltpu.VMEM)
    hbm = pl.BlockSpec(memory_space=pltpu.HBM)
    wide = max(n_x - 1, 1)
    e_next, h_next, far, poles_next = pl.pallas_call(
        functools.partial(kernel, n_gx, n_gy, n_gz, cap, rows),
        out_shape=(
            jax.ShapeDtypeStruct(e_field.shape, f32),
            jax.ShapeDtypeStruct(h_field.shape, f32),
            jax.ShapeDtypeStruct((2 * mine, dirs), f32),
            jax.ShapeDtypeStruct(poles.shape, f32),
        ),
        in_specs=[hbm] * 12,
        out_specs=(vmem, vmem, vmem, vmem),
        scratch_shapes=[
            pltpu.SMEM(pole_decay.shape, f32),
            pltpu.SMEM(pole_gain.shape, f32),
            pltpu.VMEM(e_field.shape, f32),
            pltpu.VMEM(h_field.shape, f32),
            pltpu.VMEM(permittivity.shape, f32),
            pltpu.VMEM(wall_mask.shape, jnp.int32),
            pltpu.VMEM((1, count), jnp.int32),
            pltpu.VMEM((1, count), jnp.int32),
            pltpu.VMEM(hist.shape, bf16),
            pltpu.VMEM(table.shape[1:], f32),
            pltpu.VMEM(poles.shape, f32),
            pltpu.VMEM(steering.shape, bf16),
            pltpu.VMEM((2, span_x, span_z), f32),
            pltpu.VMEM((8, flat), f32),
            pltpu.VMEM((2, span_y, span_z), f32),
            pltpu.VMEM((2, span_x, span_z), f32),
            pltpu.VMEM((8, flat), f32),
            pltpu.VMEM((2, span_x, span_z), f32),
            pltpu.VMEM((8, flat), f32),
            pltpu.VMEM((2, span_y, span_z), f32),
            pltpu.VMEM((2, span_x, span_z), f32),
            pltpu.VMEM((8, flat), f32),
            pltpu.VMEM((n_gx, rows, 4 * steps), bf16),
            pltpu.VMEM((n_gx * n_gz, rows, 4 * steps), bf16),
            pltpu.VMEM((chunks, 8, 128), f32),
            pltpu.VMEM((half, 8, 128), f32),
            pltpu.VMEM((wide, piece, 8, 128), f32),
            pltpu.VMEM((n_gy - 1, own, 8, 128), f32),
            pltpu.VMEM((chunks, 8, 128), f32),
            pltpu.VMEM((n_gx, rows, 128), bf16),
            pltpu.VMEM((n_gx * n_gz, rows, 128), bf16),
            pltpu.VMEM((dirs // 128, 1, 128), f32),
            pltpu.VMEM((n_gx * n_gy, max(own // (steps // 8), 1), 1, 128), f32),
            dma(12), dma(6), dma(6), dma(n_gx * n_gz), dma(n_gx * n_gz),
            dma(n_x), dma(n_x), dma(wide, n_gy), dma(wide, n_gy), dma(n_gy - 1), dma(n_gy - 1),
            dma(n_gx * n_gz), dma(n_gx * n_gz), dma(n_gx * n_gy), dma(n_gx * n_gy),
            dma(n_gy - 1), dma(n_gy - 1), dma(wide, n_gy), dma(wide, n_gy), dma(n_x, n_gy), dma(n_x, n_gy),
        ],
        compiler_params=pltpu.CompilerParams(
            collective_id=0, has_side_effects=True, vmem_limit_bytes=32 * 1024 * 1024
        ),
    )(
        *(
            pltpu.with_memory_space_constraint(operand, pltpu.HBM)
            for operand in (
                pole_decay, pole_gain, e_field, h_field, permittivity, wall_mask, face_cells.reshape(1, count),
                owners.reshape(1, count), hist, jnp.asarray(table), poles, steering,
            )
        )
    )
    results = (e_next, h_next, poles_next, far)
    e_next, h_next, poles_next, far = pl.pallas_call(
        hand_out,
        out_shape=tuple(jax.ShapeDtypeStruct(result.shape, f32) for result in results),
        in_specs=[vmem] * 4,
        out_specs=(hbm,) * 4,
        scratch_shapes=[dma(4)],
    )(*results)
    return (e_next, h_next, poles_next, far.reshape(2, mine, dirs))


def solution(mesh):
    return jax.shard_map(
        per_device,
        mesh=mesh,
        in_specs=(
            P(None, "gx", "gy", "gz"),
            P(None, "gx", "gy", "gz"),
            P("gx", "gy", "gz"),
            P("gx", "gy", "gz"),
            P(None, None, "gx", "gy", "gz"),
            P(),
            P(),
            P(("gx", "gy", "gz")),
            P(("gx", "gy", "gz"), None),
            P(None, None, ("gx", "gy", "gz")),
            P(None, ("gx", "gy"), "gz"),
        ),
        out_specs=(
            P(None, "gx", "gy", "gz"),
            P(None, "gx", "gy", "gz"),
            P(None, None, "gx", "gy", "gz"),
            P(None, ("gx", "gy"), "gz"),
        ),
        check_vma=False,
    )
```

```python
import functools
import math

import jax
import jax.numpy as jnp
import numpy as np
from jax import lax
from jax.experimental import pallas as pl
from jax.experimental.pallas import tpu as pltpu
from jax.sharding import PartitionSpec as P

FREQS = 256
MESH = pl.DeviceIdType.MESH


def spectral_rows(count, freqs, steps):
    times = np.arange(steps, dtype=np.float64)
    levels = np.arange(count, dtype=np.float64) + 0.5
    phase = math.pi / (2.0 * freqs) * levels[:, None] * times[None, :]
    scale = 1.0 / math.sqrt(steps)
    return np.stack([np.cos(phase) * scale, -np.sin(phase) * scale]).astype(np.float32)


def kernel(
    n_gx, n_gy, n_gz, cap, rows,
    decay_hbm, gain_hbm, e_hbm, h_hbm, perm_hbm, mask_hbm, cells_hbm, owners_hbm, hist_hbm,
    table_hbm, last_hbm, poles_hbm, steer_hbm,
    e_out, h_out, far_out, poles_out,
    decay, gain, e_ref, h_ref, perm_ref, mask_ref, cells_ref, own_ref, hist_ref, table_ref, last_ref,
    poles, steer, edge_j, edge_k, got_i, got_j, got_k,
    low_j, low_k, from_i, from_j, from_k, compact, tile, part, got_1, got_2, got_3, full, new_out, new_in, new_row, got_row, row_all,
    local_sem, halo_send, halo_recv, tile_send, tile_recv,
    core_send, core_recv, mid_send, mid_recv, end_send, end_recv,
    new_send, new_recv, row_send, row_recv, all_send, all_recv, back_z_send, back_z_recv, back_x_send, back_x_recv, back_c_send, back_c_recv,
):
    gx, gy, gz = lax.axis_index("gx"), lax.axis_index("gy"), lax.axis_index("gz")
    n_x = n_gx // 2
    core, mid = lax.rem(gx, 2), gx // 2
    span_x, span_y, span_z = e_ref.shape[1:]
    count, past = hist_ref.shape[1:]
    steps = past + 1
    chunks = part.shape[0]
    half = chunks // 2
    piece = half // n_x
    own = piece // n_gy
    t_blocks = steps // 8
    width = piece // t_blocks * 128
    early = own % t_blocks == 0 and rows == cap

    barrier = pltpu.get_barrier_semaphore()
    partners = 0
    for da in range(n_gx):
        for dz in range(n_gz):
            if da or dz:
                peer = (lax.rem(gx + da, n_gx), gy, lax.rem(gz + dz, n_gz))
                pl.semaphore_signal(barrier, inc=1, device_id=peer, device_id_type=MESH)
                partners += 1
    for da in range(n_gx if early else 1):
        for dw in range(1, n_gy):
            peer = (lax.rem(gx + da, n_gx), lax.rem(gy + dw, n_gy), gz)
            pl.semaphore_signal(barrier, inc=1, device_id=peer, device_id_type=MESH)
            partners += 1

    block = gx * n_gy + gy
    loads = [
        pltpu.make_async_copy(source, target, local_sem.at[index])
        for index, (source, target) in enumerate((
            (e_hbm, e_ref), (h_hbm, h_ref), (owners_hbm, own_ref), (hist_hbm, hist_ref),
            (cells_hbm, cells_ref), (steer_hbm, steer), (poles_hbm, poles), (perm_hbm, perm_ref),
            (mask_hbm, mask_ref), (decay_hbm, decay), (gain_hbm, gain),
            (table_hbm.at[block], table_ref), (last_hbm.at[block], last_ref),
        ))
    ]
    for load in loads:
        load.start()

    def remote(src, dst, send, recv, peer):
        return pltpu.make_async_remote_copy(
            src_ref=src, dst_ref=dst, send_sem=send, recv_sem=recv,
            device_id=peer, device_id_type=MESH,
        )

    flat = (span_x * span_y, span_z)
    cells = (span_x, span_y, span_z)

    def column(field, lane):
        return jnp.transpose(field.reshape(flat))[lane : lane + 1]

    def spread(row):
        return jnp.transpose(jnp.broadcast_to(row, (span_z, flat[0]))).reshape(cells)

    up_i = remote(e_ref.at[pl.ds(1, 2), 0], got_i, halo_send.at[0], halo_recv.at[0], (gx - 1, gy, gz))
    up_j = remote(edge_j, got_j, halo_send.at[1], halo_recv.at[1], (gx, gy - 1, gz))
    up_k = remote(edge_k, got_k, halo_send.at[2], halo_recv.at[2], (gx, gy, gz - 1))
    down_i = remote(
        h_out.at[pl.ds(1, 2), span_x - 1], from_i, halo_send.at[3], halo_recv.at[3], (gx + 1, gy, gz)
    )
    down_j = remote(low_j, from_j, halo_send.at[4], halo_recv.at[4], (gx, gy + 1, gz))
    down_k = remote(low_k, from_k, halo_send.at[5], halo_recv.at[5], (gx, gy, gz + 1))

    loads[0].wait()
    edge_k[0:1] = column(e_ref[0], 0)
    edge_k[1:2] = column(e_ref[1], 0)
    edge_k[2:8] = jnp.zeros((6, flat[0]), jnp.float32)
    edge_j[0] = e_ref[0, :, 0, :]
    edge_j[1] = e_ref[2, :, 0, :]

    for load in loads[1:5]:
        load.wait()
    sample = lax.broadcasted_iota(jnp.int32, (count, count), 0)
    other_sample = lax.broadcasted_iota(jnp.int32, (count, count), 1)

    def upright(row):
        kept = jnp.where(sample == other_sample, row.astype(jnp.float32), 0.0)
        return jnp.sum(kept, axis=1, keepdims=True).astype(jnp.int32)

    own_row = own_ref[...]
    same = jnp.where((upright(own_row) == own_row) & (sample < other_sample), 1.0, 0.0)
    rank = jnp.sum(same, axis=0, keepdims=True).astype(jnp.int32)
    slot = own_row * rows + rank
    place = (
        lax.broadcasted_iota(jnp.int32, (n_gx * rows, count), 0) == slot
    ).astype(jnp.float32).astype(jnp.bfloat16)

    lane = lax.broadcasted_iota(jnp.int32, (count, 4 * steps), 1)
    samples = jnp.zeros((count, 4 * steps), jnp.float32)
    step_in = lax.broadcasted_iota(jnp.int32, (past, 4 * steps), 0)
    step_out = lax.broadcasted_iota(jnp.int32, (past, 4 * steps), 1)
    for comp in range(4):
        spot = (step_out == step_in + comp * steps).astype(jnp.float32).astype(jnp.bfloat16)
        samples += jnp.dot(hist_ref[comp], spot, preferred_element_type=jnp.float32)
    me = gz * n_gx + gx

    def send(values, source, target, send_sem, recv_sem):
        packed = jnp.dot(
            place, values.astype(jnp.bfloat16), preferred_element_type=jnp.float32
        ).astype(jnp.bfloat16)
        source[...] = packed.reshape(source.shape)
        copies = []
        for da in range(n_gx):
            for dz in range(n_gz):
                to_x, to_z = lax.rem(gx + da, n_gx), lax.rem(gz + dz, n_gz)
                if da or dz:
                    index = da * n_gz + dz
                    copy = remote(
                        source.at[to_x], target.at[me], send_sem.at[index], recv_sem.at[index],
                        (to_x, gy, to_z),
                    )
                    copy.start()
                    copies.append(copy)
        target[me] = source[gx]
        return copies

    def send_tiles():
        return send(samples, compact, tile, tile_send, tile_recv)

    pl.semaphore_wait(barrier, partners)

    @pl.when(gz > 0)
    def _():
        up_k.start()

    @pl.when(gx > 0)
    def _():
        up_i.start()

    @pl.when(gy > 0)
    def _():
        up_j.start()

    if early:
        tile_copies = send_tiles()

    @pl.when(gx == n_gx - 1)
    def _():
        got_i[...] = jnp.zeros(got_i.shape, jnp.float32)

    @pl.when(gy == n_gy - 1)
    def _():
        got_j[...] = jnp.zeros(got_j.shape, jnp.float32)

    @pl.when(gz == n_gz - 1)
    def _():
        got_k[...] = jnp.zeros(got_k.shape, jnp.float32)

    @pl.when(gx == 0)
    def _():
        from_i[...] = jnp.zeros(from_i.shape, jnp.float32)

    @pl.when(gy == 0)
    def _():
        from_j[...] = jnp.zeros(from_j.shape, jnp.float32)

    @pl.when(gz == 0)
    def _():
        from_k[...] = jnp.zeros(from_k.shape, jnp.float32)

    at_j = lax.broadcasted_iota(jnp.int32, cells, 1)
    at_k = lax.broadcasted_iota(jnp.int32, cells, 2)

    def next_j(field, halo):
        return jnp.where(at_j == span_y - 1, halo[:, None, :], pltpu.roll(field, span_y - 1, 1))

    def next_k(field, halo):
        return jnp.where(at_k == span_z - 1, spread(halo), pltpu.roll(field, span_z - 1, 2))

    def prev_j(field, halo):
        return jnp.where(at_j == 0, halo[:, None, :], pltpu.roll(field, 1, 1))

    def prev_k(field, halo):
        return jnp.where(at_k == 0, spread(halo), pltpu.roll(field, 1, 2))

    @pl.when(gx < n_gx - 1)
    def _():
        up_i.wait_recv()

    @pl.when(gy < n_gy - 1)
    def _():
        up_j.wait_recv()

    @pl.when(gz < n_gz - 1)
    def _():
        up_k.wait_recv()

    ex, ey, ez = e_ref[0], e_ref[1], e_ref[2]
    ey_i = jnp.concatenate([ey[1:], got_i[0][None]], axis=0)
    ez_i = jnp.concatenate([ez[1:], got_i[1][None]], axis=0)
    mag_x = h_ref[0] - 0.5 * (next_j(ez, got_j[1]) - ez - (next_k(ey, got_k[1:2]) - ey))
    h_out[0] = mag_x
    mag_y = h_ref[1] - 0.5 * (next_k(ex, got_k[0:1]) - ex - (ez_i - ez))
    h_out[1] = mag_y
    mag_z = h_ref[2] - 0.5 * (ey_i - ey - (next_j(ex, got_j[0]) - ex))
    h_out[2] = mag_z

    @pl.when(gx < n_gx - 1)
    def _():
        down_i.start()

    @pl.when(gz < n_gz - 1)
    def _():
        low_k[0:1] = column(h_out[0], span_z - 1)
        low_k[1:2] = column(h_out[1], span_z - 1)
        low_k[2:8] = jnp.zeros((6, flat[0]), jnp.float32)
        down_k.start()

    @pl.when(gy < n_gy - 1)
    def _():
        low_j[0] = h_out[0, :, span_y - 1, :]
        low_j[1] = h_out[2, :, span_y - 1, :]
        down_j.start()

    order_x = list(range(1, n_x)) + [0]
    order_z = list(range(1, n_gy)) + [0]
    sends = []

    def begin(copy):
        copy.start()
        sends.append(copy)
        return copy

    other = (mid * 2 + 1 - core, gy, gz)
    second = {}

    def first_half(copies):
        loads[5].wait()
        loads[11].wait()
        loads[12].wait()
        for copy in copies:
            copy.wait_recv()

        sources = n_gx * n_gz
        slots = tile[...].reshape(sources * rows, 4 * steps)
        if rows != cap:
            place_row = lax.broadcasted_iota(jnp.int32, (sources * cap, sources * rows), 0)
            place_col = lax.broadcasted_iota(jnp.int32, (sources * cap, sources * rows), 1)
            keep = (place_col == place_row // cap * rows + lax.rem(place_row, cap)).astype(jnp.float32)
            slots = jnp.dot(
                keep.astype(jnp.bfloat16), slots, preferred_element_type=jnp.float32
            ).astype(jnp.bfloat16)
        turned = jnp.transpose(slots.astype(jnp.float32)).astype(jnp.bfloat16)
        currents = jnp.concatenate(
            [turned[comp * steps : (comp + 1) * steps] for comp in range(4)], axis=1
        )
        depth = 4 * slots.shape[0]

        def fill(start):
            offset = pl.multiple_of(start // t_blocks * 128, 128)
            weights = steer[:, :, pl.ds(offset, width)].reshape(depth, width)
            out = jnp.dot(currents, weights, preferred_element_type=jnp.float32)
            for block in range(width // 128):
                part[pl.ds(start + block * t_blocks, t_blocks)] = out[
                    :, block * 128 : (block + 1) * 128
                ].reshape(t_blocks, 8, 128)

        first = {}
        for dq in order_x:
            to = lax.rem(mid + dq, n_x)
            start = (1 - core) * half + to * piece
            fill(start)
            first[dq] = begin(
                remote(
                    part.at[pl.ds(start, piece)], got_1.at[pl.ds(to * piece, piece)],
                    core_send.at[dq], core_recv.at[dq], other,
                )
            )
        for dq in order_x:
            fill(core * half + lax.rem(mid + dq, n_x) * piece)
        for dq in order_x:
            to = lax.rem(mid + dq, n_x)
            start = core * half + to * piece
            first[dq].wait_recv()
            part[pl.ds(start, piece)] += got_1[pl.ds(to * piece, piece)]
            if dq:
                for dw in order_z:
                    at = lax.rem(gy + dw, n_gy) * own
                    second[dq, dw] = begin(
                        remote(
                            part.at[pl.ds(start + at, own)], got_2.at[dq - 1, pl.ds(at, own)],
                            mid_send.at[dq - 1, dw], mid_recv.at[dq - 1, dw], (to * 2 + core, gy, gz),
                        )
                    )

    if early:
        first_half(tile_copies)

    for load in loads[6:11]:
        load.wait()

    @pl.when(gx > 0)
    def _():
        down_i.wait_recv()

    @pl.when(gy > 0)
    def _():
        down_j.wait_recv()

    @pl.when(gz > 0)
    def _():
        down_k.wait_recv()

    mag_x, mag_y, mag_z = h_out[0], h_out[1], h_out[2]
    mag_y_i = jnp.concatenate([from_i[0][None], mag_y[:-1]], axis=0)
    mag_z_i = jnp.concatenate([from_i[1][None], mag_z[:-1]], axis=0)
    drives = (
        mag_z - prev_j(mag_z, from_j[1]) - (mag_y - prev_k(mag_y, from_k[1:2])),
        mag_x - prev_k(mag_x, from_k[0:1]) - (mag_z - mag_z_i),
        mag_y - mag_y_i - (mag_x - prev_j(mag_x, from_j[0])),
    )
    wall = mask_ref[...] == 1
    half_eps = 0.5 / perm_ref[...]
    for comp in range(3):
        drive = drives[comp]
        total = None
        for pole in range(poles.shape[0]):
            state = decay[pole] * poles[pole, comp] + gain[pole] * drive
            poles_out[pole, comp] = state
            total = state if total is None else total + state
        e_out[comp] = jnp.where(wall, total, e_ref[comp] + half_eps * drive)

    cell = upright(cells_ref[...])
    row_hot = (
        lax.broadcasted_iota(jnp.int32, (count, flat[0]), 1) == cell // span_z
    ).astype(jnp.float32).astype(jnp.bfloat16)
    lane_hot = lax.broadcasted_iota(jnp.int32, (count, span_z), 1) == lax.rem(cell, span_z)
    fresh_lane = lax.broadcasted_iota(jnp.int32, (count, 128), 1)
    fresh_all = jnp.zeros((count, 128), jnp.float32)
    for comp, field in enumerate((e_out[0], e_out[1], h_out[0], h_out[1])):
        found = jnp.dot(
            row_hot, field.reshape(flat).astype(jnp.bfloat16), preferred_element_type=jnp.float32
        )
        fresh = jnp.sum(jnp.where(lane_hot, found, 0.0), axis=1, keepdims=True)
        if early:
            fresh_all = jnp.where(fresh_lane == comp, fresh, fresh_all)
        else:
            samples = jnp.where(lane == comp * steps + steps - 1, fresh, samples)
    if early:
        new_copies = send(fresh_all, new_out, new_in, new_send, new_recv)
    else:
        tile_copies = send_tiles()
        first_half(tile_copies)
    base = core * half + mid * piece
    third = {}
    for dw in order_z:
        to = lax.rem(gy + dw, n_gy)
        at = to * own
        for dq in range(1, n_x):
            second[dq, dw].wait_recv()
            part[pl.ds(base + at, own)] += got_2[dq - 1, pl.ds(at, own)]
        if dw:
            third[dw] = begin(
                remote(
                    part.at[pl.ds(base + at, own)], got_3.at[dw - 1],
                    end_send.at[dw - 1], end_recv.at[dw - 1], (gx, to, gz),
                )
            )
    mine = base + gy * own
    rows_out = {}
    if early:
        for copy in new_copies:
            copy.wait_recv()
        turned = jnp.transpose(new_in[...].reshape(n_gx * n_gz * rows, 128).astype(jnp.float32))
        line = jnp.concatenate([turned[comp : comp + 1] for comp in range(4)], axis=1)
        line = jnp.broadcast_to(line, (16, line.shape[1])).astype(jnp.bfloat16)
        for start in range(0, new_row.shape[0], 4):
            weights = steer[:, :, start * 128 : (start + 4) * 128].reshape(line.shape[1], 512)
            out = jnp.dot(line, weights, preferred_element_type=jnp.float32)
            for index in range(4):
                new_row[start + index] = out[0:1, index * 128 : (index + 1) * 128]
        count_d = own // t_blocks
        for da in range(n_gx):
            for dw in range(n_gy):
                if da or dw:
                    to_x, to_y = lax.rem(gx + da, n_gx), lax.rem(gy + dw, n_gy)
                    begin_d = (
                        lax.rem(to_x, 2) * half + to_x // 2 * piece + to_y * own
                    ) // t_blocks
                    index = da * n_gy + dw
                    rows_out[index] = begin(
                        remote(
                            new_row.at[pl.ds(begin_d, count_d)], got_row.at[index],
                            row_send.at[index], row_recv.at[index], (to_x, to_y, gz),
                        )
                    )
    total = part[pl.ds(mine, own)]
    for dw in range(1, n_gy):
        third[dw].wait_recv()
        total = total + got_3[dw - 1]
    full[pl.ds(mine, own)] = total
    def transform(start, many):
        for index in range(many // t_blocks):
            at = start // t_blocks + index
            values = full[pl.ds(at * t_blocks, t_blocks)].reshape(steps, 128)
            if not isinstance(at, int):
                at = pl.multiple_of(at * 128, 128)
            else:
                at = at * 128
            high = values.astype(jnp.bfloat16)
            low = (values - high.astype(jnp.float32)).astype(jnp.bfloat16)
            far_out[:, pl.ds(at, 128)] = jnp.dot(
                table_ref[...], jnp.concatenate([high, low, high], axis=0),
                preferred_element_type=jnp.float32,
            )

    def arrived(start):
        if early:
            transform(start, own)

    last = {}

    def to_core(start, dq, dw):
        block = full.at[pl.ds(start, own)]
        last[dq, dw] = begin(
            remote(block, block, back_c_send.at[dq, dw], back_c_recv.at[dq, dw], other)
        )

    wide = {}

    def to_mid(start, dw):
        block = full.at[pl.ds(start, own)]
        for dq in range(1, n_x):
            wide[dq, dw] = begin(
                remote(
                    block, block, back_x_send.at[dq - 1, dw], back_x_recv.at[dq - 1, dw],
                    (lax.rem(mid + dq, n_x) * 2 + core, gy, gz),
                )
            )

    long = {}
    for dw in range(1, n_gy):
        block = full.at[pl.ds(mine, own)]
        long[dw] = begin(
            remote(
                block, block, back_z_send.at[dw - 1], back_z_recv.at[dw - 1],
                (gx, lax.rem(gy + dw, n_gy), gz),
            )
        )
    to_mid(mine, 0)
    to_core(mine, 0, 0)
    arrived(mine)
    rows_back = []
    if early:
        mine_d = mine // t_blocks
        added = new_row[pl.ds(mine_d, count_d)]
        for index in rows_out:
            rows_out[index].wait_recv()
            added = added + got_row[index]
        row_all[pl.ds(mine_d, count_d)] = added
        for da in range(n_gx):
            for dw in range(n_gy):
                if da or dw:
                    index = da * n_gy + dw
                    block = row_all.at[pl.ds(mine_d, count_d)]
                    rows_back.append(
                        begin(
                            remote(
                                block, block, all_send.at[index], all_recv.at[index],
                                (lax.rem(gx + da, n_gx), lax.rem(gy + dw, n_gy), gz),
                            )
                        )
                    )
    for dw in range(1, n_gy):
        long[dw].wait_recv()
        start = base + lax.rem(gy + n_gy - dw, n_gy) * own
        to_mid(start, dw)
        to_core(start, 0, dw)
        arrived(start)
    for dw in range(n_gy):
        for dq in range(1, n_x):
            wide[dq, dw].wait_recv()
            start = (
                core * half
                + lax.rem(mid + n_x - dq, n_x) * piece
                + lax.rem(gy + n_gy - dw, n_gy) * own
            )
            to_core(start, dq, dw)
            arrived(start)
    for dw in range(n_gy):
        for dq in range(n_x):
            last[dq, dw].wait_recv()
            arrived(
                (1 - core) * half
                + lax.rem(mid + n_x - dq, n_x) * piece
                + lax.rem(gy + n_gy - dw, n_gy) * own
            )
    if early:
        for copy in rows_back:
            copy.wait_recv()
        last_step = last_ref[...]
        for index in range(chunks // t_blocks):
            far_out[:, index * 128 : (index + 1) * 128] += last_step * row_all[index]
    else:
        transform(0, chunks)

    for copy in sends + tile_copies + (new_copies if early else []):
        copy.wait_send()

    @pl.when(gx > 0)
    def _():
        up_i.wait_send()

    @pl.when(gy > 0)
    def _():
        up_j.wait_send()

    @pl.when(gz > 0)
    def _():
        up_k.wait_send()

    @pl.when(gx < n_gx - 1)
    def _():
        down_i.wait_send()

    @pl.when(gy < n_gy - 1)
    def _():
        down_j.wait_send()

    @pl.when(gz < n_gz - 1)
    def _():
        down_k.wait_send()


def hand_out(*refs):
    copies = [
        pltpu.make_async_copy(refs[index], refs[4 + index], refs[8].at[index]) for index in range(4)
    ]
    for copy in copies:
        copy.start()
    for copy in copies:
        copy.wait()


def per_device(
    e_field, h_field, permittivity, wall_mask, poles, pole_decay, pole_gain,
    face_cells, owners, history, steering,
):
    n_gx, n_gy, n_gz = (lax.axis_size(axis) for axis in ("gx", "gy", "gz"))
    n_x = n_gx // 2
    count = face_cells.shape[0]
    steps = history.shape[0] + 1
    cap = steering.shape[1] // (n_gx * n_gz)
    rows = -(-cap // 16) * 16
    dirs = steering.shape[2]
    blocks = n_gx * n_gy
    mine = FREQS // blocks
    _, span_x, span_y, span_z = e_field.shape
    flat = span_x * span_y

    table = spectral_rows(FREQS, FREQS, steps)
    table = table.reshape(2, blocks, mine, steps).transpose(1, 0, 2, 3).reshape(blocks, 2 * mine, steps)
    high = table.astype(jnp.bfloat16)
    low = (table - high.astype(np.float32)).astype(jnp.bfloat16)
    split = np.concatenate([high, high, low], axis=2)
    last = np.broadcast_to(table[:, :, -1:], table.shape[:2] + (128,)).copy()
    hist = jnp.transpose(history, (1, 2, 0))

    chunks = steps // 8 * (dirs // 128)
    half = chunks // 2
    piece = half // n_x
    own = piece // n_gy
    f32, bf16 = jnp.float32, jnp.bfloat16
    dma = lambda *dims: pltpu.SemaphoreType.DMA(dims)
    vmem = pl.BlockSpec(memory_space=pltpu.VMEM)
    hbm = pl.BlockSpec(memory_space=pltpu.HBM)
    wide = max(n_x - 1, 1)
    e_next, h_next, far, poles_next = pl.pallas_call(
        functools.partial(kernel, n_gx, n_gy, n_gz, cap, rows),
        out_shape=(
            jax.ShapeDtypeStruct(e_field.shape, f32),
            jax.ShapeDtypeStruct(h_field.shape, f32),
            jax.ShapeDtypeStruct((2 * mine, dirs), f32),
            jax.ShapeDtypeStruct(poles.shape, f32),
        ),
        in_specs=[hbm] * 13,
        out_specs=(vmem, vmem, vmem, vmem),
        scratch_shapes=[
            pltpu.SMEM(pole_decay.shape, f32),
            pltpu.SMEM(pole_gain.shape, f32),
            pltpu.VMEM(e_field.shape, f32),
            pltpu.VMEM(h_field.shape, f32),
            pltpu.VMEM(permittivity.shape, f32),
            pltpu.VMEM(wall_mask.shape, jnp.int32),
            pltpu.VMEM((1, count), jnp.int32),
            pltpu.VMEM((1, count), jnp.int32),
            pltpu.VMEM(hist.shape, bf16),
            pltpu.VMEM(split.shape[1:], bf16),
            pltpu.VMEM(last.shape[1:], f32),
            pltpu.VMEM(poles.shape, f32),
            pltpu.VMEM(steering.shape, bf16),
            pltpu.VMEM((2, span_x, span_z), f32),
            pltpu.VMEM((8, flat), f32),
            pltpu.VMEM((2, span_y, span_z), f32),
            pltpu.VMEM((2, span_x, span_z), f32),
            pltpu.VMEM((8, flat), f32),
            pltpu.VMEM((2, span_x, span_z), f32),
            pltpu.VMEM((8, flat), f32),
            pltpu.VMEM((2, span_y, span_z), f32),
            pltpu.VMEM((2, span_x, span_z), f32),
            pltpu.VMEM((8, flat), f32),
            pltpu.VMEM((n_gx, rows, 4 * steps), bf16),
            pltpu.VMEM((n_gx * n_gz, rows, 4 * steps), bf16),
            pltpu.VMEM((chunks, 8, 128), f32),
            pltpu.VMEM((half, 8, 128), f32),
            pltpu.VMEM((wide, piece, 8, 128), f32),
            pltpu.VMEM((n_gy - 1, own, 8, 128), f32),
            pltpu.VMEM((chunks, 8, 128), f32),
            pltpu.VMEM((n_gx, rows, 128), bf16),
            pltpu.VMEM((n_gx * n_gz, rows, 128), bf16),
            pltpu.VMEM((dirs // 128, 1, 128), f32),
            pltpu.VMEM((n_gx * n_gy, max(own // (steps // 8), 1), 1, 128), f32),
            pltpu.VMEM((dirs // 128, 1, 128), f32),
            dma(13), dma(6), dma(6), dma(n_gx * n_gz), dma(n_gx * n_gz),
            dma(n_x), dma(n_x), dma(wide, n_gy), dma(wide, n_gy), dma(n_gy - 1), dma(n_gy - 1),
            dma(n_gx * n_gz), dma(n_gx * n_gz), dma(n_gx * n_gy), dma(n_gx * n_gy),
            dma(n_gx * n_gy), dma(n_gx * n_gy), dma(n_gy - 1), dma(n_gy - 1), dma(wide, n_gy), dma(wide, n_gy), dma(n_x, n_gy), dma(n_x, n_gy),
        ],
        compiler_params=pltpu.CompilerParams(
            collective_id=0, has_side_effects=True, vmem_limit_bytes=32 * 1024 * 1024
        ),
    )(
        *(
            pltpu.with_memory_space_constraint(operand, pltpu.HBM)
            for operand in (
                pole_decay, pole_gain, e_field, h_field, permittivity, wall_mask, face_cells.reshape(1, count),
                owners.reshape(1, count), hist, jnp.asarray(split), jnp.asarray(last), poles, steering,
            )
        )
    )
    results = (e_next, h_next, poles_next, far)
    e_next, h_next, poles_next, far = pl.pallas_call(
        hand_out,
        out_shape=tuple(jax.ShapeDtypeStruct(result.shape, f32) for result in results),
        in_specs=[vmem] * 4,
        out_specs=(hbm,) * 4,
        scratch_shapes=[dma(4)],
        compiler_params=pltpu.CompilerParams(vmem_limit_bytes=8 * 1024 * 1024),
    )(*results)
    return (e_next, h_next, poles_next, far.reshape(2, mine, dirs))


def solution(mesh):
    return jax.shard_map(
        per_device,
        mesh=mesh,
        in_specs=(
            P(None, "gx", "gy", "gz"),
            P(None, "gx", "gy", "gz"),
            P("gx", "gy", "gz"),
            P("gx", "gy", "gz"),
            P(None, None, "gx", "gy", "gz"),
            P(),
            P(),
            P(("gx", "gy", "gz")),
            P(("gx", "gy", "gz"), None),
            P(None, None, ("gx", "gy", "gz")),
            P(None, ("gx", "gy"), "gz"),
        ),
        out_specs=(
            P(None, "gx", "gy", "gz"),
            P(None, "gx", "gy", "gz"),
            P(None, None, "gx", "gy", "gz"),
            P(None, ("gx", "gy"), "gz"),
        ),
        check_vma=False,
    )
```

```python
import functools
import math

import jax
import jax.numpy as jnp
import numpy as np
from jax import lax
from jax.experimental import pallas as pl
from jax.experimental.pallas import tpu as pltpu
from jax.sharding import PartitionSpec as P

FREQS = 256
MESH = pl.DeviceIdType.MESH


def spectral_rows(count, freqs, steps):
    times = np.arange(steps, dtype=np.float64)
    levels = np.arange(count, dtype=np.float64) + 0.5
    phase = math.pi / (2.0 * freqs) * levels[:, None] * times[None, :]
    scale = 1.0 / math.sqrt(steps)
    return np.stack([np.cos(phase) * scale, -np.sin(phase) * scale]).astype(np.float32)


def kernel(
    n_gx, n_gy, n_gz, cap, rows,
    decay_hbm, gain_hbm, e_hbm, h_hbm, perm_hbm, mask_hbm, cells_hbm, owners_hbm, hist_hbm,
    table_hbm, last_hbm, poles_hbm, steer_hbm,
    e_out, h_out, far_out, poles_out,
    decay, gain, e_ref, h_ref, perm_ref, mask_ref, cells_ref, own_ref, hist_ref, table_ref, last_ref,
    poles, steer, edge_j, edge_k, got_i, got_j, got_k,
    low_j, low_k, from_i, from_j, from_k, compact, tile, part, got_1, got_2, got_3, full, new_out, new_in, new_row, got_row, row_all,
    local_sem, halo_send, halo_recv, tile_send, tile_recv,
    core_send, core_recv, mid_send, mid_recv, end_send, end_recv,
    new_send, new_recv, row_send, row_recv, all_send, all_recv, back_z_send, back_z_recv, back_x_send, back_x_recv, back_c_send, back_c_recv,
):
    gx, gy, gz = lax.axis_index("gx"), lax.axis_index("gy"), lax.axis_index("gz")
    n_x = n_gx // 2
    core, mid = lax.rem(gx, 2), gx // 2
    span_x, span_y, span_z = e_ref.shape[1:]
    count, past = hist_ref.shape[1:]
    steps = past + 1
    chunks = part.shape[0]
    half = chunks // 2
    piece = half // n_x
    own = piece // n_gy
    t_blocks = steps // 8
    width = piece // t_blocks * 128
    early = own % t_blocks == 0 and rows == cap

    barrier = pltpu.get_barrier_semaphore()
    partners = 0
    for da in range(n_gx):
        for dz in range(n_gz):
            if da or dz:
                peer = (lax.rem(gx + da, n_gx), gy, lax.rem(gz + dz, n_gz))
                pl.semaphore_signal(barrier, inc=1, device_id=peer, device_id_type=MESH)
                partners += 1
    for da in range(n_gx if early else 1):
        for dw in range(1, n_gy):
            peer = (lax.rem(gx + da, n_gx), lax.rem(gy + dw, n_gy), gz)
            pl.semaphore_signal(barrier, inc=1, device_id=peer, device_id_type=MESH)
            partners += 1

    block = gx * n_gy + gy
    loads = [
        pltpu.make_async_copy(source, target, local_sem.at[index])
        for index, (source, target) in enumerate((
            (owners_hbm, own_ref), (hist_hbm, hist_ref), (e_hbm, e_ref), (h_hbm, h_ref),
            (cells_hbm, cells_ref), (steer_hbm, steer), (poles_hbm, poles), (perm_hbm, perm_ref),
            (mask_hbm, mask_ref), (decay_hbm, decay), (gain_hbm, gain),
            (table_hbm.at[block], table_ref), (last_hbm.at[block], last_ref),
        ))
    ]
    for load in loads:
        load.start()

    def remote(src, dst, send, recv, peer):
        return pltpu.make_async_remote_copy(
            src_ref=src, dst_ref=dst, send_sem=send, recv_sem=recv,
            device_id=peer, device_id_type=MESH,
        )

    flat = (span_x * span_y, span_z)
    cells = (span_x, span_y, span_z)

    def column(field, lane):
        return jnp.transpose(field.reshape(flat))[lane : lane + 1]

    def spread(row):
        return jnp.transpose(jnp.broadcast_to(row, (span_z, flat[0]))).reshape(cells)

    up_i = remote(e_ref.at[pl.ds(1, 2), 0], got_i, halo_send.at[0], halo_recv.at[0], (gx - 1, gy, gz))
    up_j = remote(edge_j, got_j, halo_send.at[1], halo_recv.at[1], (gx, gy - 1, gz))
    up_k = remote(edge_k, got_k, halo_send.at[2], halo_recv.at[2], (gx, gy, gz - 1))
    down_i = remote(
        h_out.at[pl.ds(1, 2), span_x - 1], from_i, halo_send.at[3], halo_recv.at[3], (gx + 1, gy, gz)
    )
    down_j = remote(low_j, from_j, halo_send.at[4], halo_recv.at[4], (gx, gy + 1, gz))
    down_k = remote(low_k, from_k, halo_send.at[5], halo_recv.at[5], (gx, gy, gz + 1))

    for load in loads[:2]:
        load.wait()
    sample = lax.broadcasted_iota(jnp.int32, (count, count), 0)
    other_sample = lax.broadcasted_iota(jnp.int32, (count, count), 1)

    def upright(row):
        kept = jnp.where(sample == other_sample, row.astype(jnp.float32), 0.0)
        return jnp.sum(kept, axis=1, keepdims=True).astype(jnp.int32)

    own_row = own_ref[...]
    same = jnp.where((upright(own_row) == own_row) & (sample < other_sample), 1.0, 0.0)
    rank = jnp.sum(same, axis=0, keepdims=True).astype(jnp.int32)
    slot = own_row * rows + rank
    place = (
        lax.broadcasted_iota(jnp.int32, (n_gx * rows, count), 0) == slot
    ).astype(jnp.float32).astype(jnp.bfloat16)

    lane = lax.broadcasted_iota(jnp.int32, (count, 4 * steps), 1)
    samples = jnp.zeros((count, 4 * steps), jnp.float32)
    step_in = lax.broadcasted_iota(jnp.int32, (past, 4 * steps), 0)
    step_out = lax.broadcasted_iota(jnp.int32, (past, 4 * steps), 1)
    for comp in range(4):
        spot = (step_out == step_in + comp * steps).astype(jnp.float32).astype(jnp.bfloat16)
        samples += jnp.dot(hist_ref[comp], spot, preferred_element_type=jnp.float32)
    me = gz * n_gx + gx

    def pack(values, source):
        packed = jnp.dot(
            place, values.astype(jnp.bfloat16), preferred_element_type=jnp.float32
        ).astype(jnp.bfloat16)
        source[...] = packed.reshape(source.shape)

    def send(values, source, target, send_sem, recv_sem):
        pack(values, source)
        return launch(source, target, send_sem, recv_sem)

    def launch(source, target, send_sem, recv_sem):
        copies = []
        for da in range(n_gx):
            for dz in range(n_gz):
                to_x, to_z = lax.rem(gx + da, n_gx), lax.rem(gz + dz, n_gz)
                if da or dz:
                    index = da * n_gz + dz
                    copy = remote(
                        source.at[to_x], target.at[me], send_sem.at[index], recv_sem.at[index],
                        (to_x, gy, to_z),
                    )
                    copy.start()
                    copies.append(copy)
        target[me] = source[gx]
        return copies

    def send_tiles():
        return send(samples, compact, tile, tile_send, tile_recv)

    if early:
        pack(samples, compact)
    loads[2].wait()
    edge_k[0:1] = column(e_ref[0], 0)
    edge_k[1:2] = column(e_ref[1], 0)
    edge_k[2:8] = jnp.zeros((6, flat[0]), jnp.float32)
    edge_j[0] = e_ref[0, :, 0, :]
    edge_j[1] = e_ref[2, :, 0, :]

    pl.semaphore_wait(barrier, partners)
    if early:
        tile_copies = launch(compact, tile, tile_send, tile_recv)

    @pl.when(gz > 0)
    def _():
        up_k.start()

    @pl.when(gx > 0)
    def _():
        up_i.start()

    @pl.when(gy > 0)
    def _():
        up_j.start()

    for load in loads[3:5]:
        load.wait()

    @pl.when(gx == n_gx - 1)
    def _():
        got_i[...] = jnp.zeros(got_i.shape, jnp.float32)

    @pl.when(gy == n_gy - 1)
    def _():
        got_j[...] = jnp.zeros(got_j.shape, jnp.float32)

    @pl.when(gz == n_gz - 1)
    def _():
        got_k[...] = jnp.zeros(got_k.shape, jnp.float32)

    @pl.when(gx == 0)
    def _():
        from_i[...] = jnp.zeros(from_i.shape, jnp.float32)

    @pl.when(gy == 0)
    def _():
        from_j[...] = jnp.zeros(from_j.shape, jnp.float32)

    @pl.when(gz == 0)
    def _():
        from_k[...] = jnp.zeros(from_k.shape, jnp.float32)

    at_j = lax.broadcasted_iota(jnp.int32, cells, 1)
    at_k = lax.broadcasted_iota(jnp.int32, cells, 2)

    def next_j(field, halo):
        return jnp.where(at_j == span_y - 1, halo[:, None, :], pltpu.roll(field, span_y - 1, 1))

    def next_k(field, halo):
        return jnp.where(at_k == span_z - 1, spread(halo), pltpu.roll(field, span_z - 1, 2))

    def prev_j(field, halo):
        return jnp.where(at_j == 0, halo[:, None, :], pltpu.roll(field, 1, 1))

    def prev_k(field, halo):
        return jnp.where(at_k == 0, spread(halo), pltpu.roll(field, 1, 2))

    @pl.when(gx < n_gx - 1)
    def _():
        up_i.wait_recv()

    @pl.when(gy < n_gy - 1)
    def _():
        up_j.wait_recv()

    @pl.when(gz < n_gz - 1)
    def _():
        up_k.wait_recv()

    ex, ey, ez = e_ref[0], e_ref[1], e_ref[2]
    ey_i = jnp.concatenate([ey[1:], got_i[0][None]], axis=0)
    ez_i = jnp.concatenate([ez[1:], got_i[1][None]], axis=0)
    mag_x = h_ref[0] - 0.5 * (next_j(ez, got_j[1]) - ez - (next_k(ey, got_k[1:2]) - ey))
    h_out[0] = mag_x
    mag_y = h_ref[1] - 0.5 * (next_k(ex, got_k[0:1]) - ex - (ez_i - ez))
    h_out[1] = mag_y
    mag_z = h_ref[2] - 0.5 * (ey_i - ey - (next_j(ex, got_j[0]) - ex))
    h_out[2] = mag_z

    @pl.when(gx < n_gx - 1)
    def _():
        down_i.start()

    @pl.when(gz < n_gz - 1)
    def _():
        low_k[0:1] = column(h_out[0], span_z - 1)
        low_k[1:2] = column(h_out[1], span_z - 1)
        low_k[2:8] = jnp.zeros((6, flat[0]), jnp.float32)
        down_k.start()

    @pl.when(gy < n_gy - 1)
    def _():
        low_j[0] = h_out[0, :, span_y - 1, :]
        low_j[1] = h_out[2, :, span_y - 1, :]
        down_j.start()

    order_x = list(range(1, n_x)) + [0]
    order_z = list(range(1, n_gy)) + [0]
    sends = []

    def begin(copy):
        copy.start()
        sends.append(copy)
        return copy

    other = (mid * 2 + 1 - core, gy, gz)
    first, second = {}, {}

    def first_half(copies):
        loads[5].wait()
        loads[11].wait()
        loads[12].wait()
        for copy in copies:
            copy.wait_recv()

        sources = n_gx * n_gz
        slots = tile[...].reshape(sources * rows, 4 * steps)
        if rows != cap:
            place_row = lax.broadcasted_iota(jnp.int32, (sources * cap, sources * rows), 0)
            place_col = lax.broadcasted_iota(jnp.int32, (sources * cap, sources * rows), 1)
            keep = (place_col == place_row // cap * rows + lax.rem(place_row, cap)).astype(jnp.float32)
            slots = jnp.dot(
                keep.astype(jnp.bfloat16), slots, preferred_element_type=jnp.float32
            ).astype(jnp.bfloat16)
        turned = jnp.transpose(slots.astype(jnp.float32)).astype(jnp.bfloat16)
        currents = jnp.concatenate(
            [turned[comp * steps : (comp + 1) * steps] for comp in range(4)], axis=1
        )
        depth = 4 * slots.shape[0]

        def fill(start):
            offset = pl.multiple_of(start // t_blocks * 128, 128)
            weights = steer[:, :, pl.ds(offset, width)].reshape(depth, width)
            out = jnp.dot(currents, weights, preferred_element_type=jnp.float32)
            for block in range(width // 128):
                part[pl.ds(start + block * t_blocks, t_blocks)] = out[
                    :, block * 128 : (block + 1) * 128
                ].reshape(t_blocks, 8, 128)

        for dq in order_x:
            to = lax.rem(mid + dq, n_x)
            start = (1 - core) * half + to * piece
            fill(start)
            first[dq] = begin(
                remote(
                    part.at[pl.ds(start, piece)], got_1.at[pl.ds(to * piece, piece)],
                    core_send.at[dq], core_recv.at[dq], other,
                )
            )
        for dq in order_x:
            fill(core * half + lax.rem(mid + dq, n_x) * piece)
    def pass_on():
        for dq in order_x:
            to = lax.rem(mid + dq, n_x)
            start = core * half + to * piece
            first[dq].wait_recv()
            part[pl.ds(start, piece)] += got_1[pl.ds(to * piece, piece)]
            if dq:
                for dw in order_z:
                    at = lax.rem(gy + dw, n_gy) * own
                    second[dq, dw] = begin(
                        remote(
                            part.at[pl.ds(start + at, own)], got_2.at[dq - 1, pl.ds(at, own)],
                            mid_send.at[dq - 1, dw], mid_recv.at[dq - 1, dw], (to * 2 + core, gy, gz),
                        )
                    )

    if early:
        first_half(tile_copies)

    for load in loads[6:11]:
        load.wait()

    @pl.when(gx > 0)
    def _():
        down_i.wait_recv()

    @pl.when(gy > 0)
    def _():
        down_j.wait_recv()

    @pl.when(gz > 0)
    def _():
        down_k.wait_recv()

    mag_x, mag_y, mag_z = h_out[0], h_out[1], h_out[2]
    mag_y_i = jnp.concatenate([from_i[0][None], mag_y[:-1]], axis=0)
    mag_z_i = jnp.concatenate([from_i[1][None], mag_z[:-1]], axis=0)
    drives = (
        mag_z - prev_j(mag_z, from_j[1]) - (mag_y - prev_k(mag_y, from_k[1:2])),
        mag_x - prev_k(mag_x, from_k[0:1]) - (mag_z - mag_z_i),
        mag_y - mag_y_i - (mag_x - prev_j(mag_x, from_j[0])),
    )
    wall = mask_ref[...] == 1
    half_eps = 0.5 / perm_ref[...]
    for comp in range(3):
        drive = drives[comp]
        total = None
        for pole in range(poles.shape[0]):
            state = decay[pole] * poles[pole, comp] + gain[pole] * drive
            poles_out[pole, comp] = state
            total = state if total is None else total + state
        e_out[comp] = jnp.where(wall, total, e_ref[comp] + half_eps * drive)

    cell = upright(cells_ref[...])
    row_hot = (
        lax.broadcasted_iota(jnp.int32, (count, flat[0]), 1) == cell // span_z
    ).astype(jnp.float32).astype(jnp.bfloat16)
    lane_hot = lax.broadcasted_iota(jnp.int32, (count, span_z), 1) == lax.rem(cell, span_z)
    fresh_lane = lax.broadcasted_iota(jnp.int32, (count, 128), 1)
    fresh_all = jnp.zeros((count, 128), jnp.float32)
    for comp, field in enumerate((e_out[0], e_out[1], h_out[0], h_out[1])):
        found = jnp.dot(
            row_hot, field.reshape(flat).astype(jnp.bfloat16), preferred_element_type=jnp.float32
        )
        fresh = jnp.sum(jnp.where(lane_hot, found, 0.0), axis=1, keepdims=True)
        if early:
            fresh_all = jnp.where(fresh_lane == comp, fresh, fresh_all)
        else:
            samples = jnp.where(lane == comp * steps + steps - 1, fresh, samples)
    if early:
        new_copies = send(fresh_all, new_out, new_in, new_send, new_recv)
    else:
        tile_copies = send_tiles()
        first_half(tile_copies)
    pass_on()

    rows_out = {}
    if early:
        for copy in new_copies:
            copy.wait_recv()
        turned = jnp.transpose(new_in[...].reshape(n_gx * n_gz * rows, 128).astype(jnp.float32))
        line = jnp.concatenate([turned[comp : comp + 1] for comp in range(4)], axis=1)
        line = jnp.broadcast_to(line, (16, line.shape[1])).astype(jnp.bfloat16)
        for start in range(0, new_row.shape[0], 4):
            weights = steer[:, :, start * 128 : (start + 4) * 128].reshape(line.shape[1], 512)
            out = jnp.dot(line, weights, preferred_element_type=jnp.float32)
            for index in range(4):
                new_row[start + index] = out[0:1, index * 128 : (index + 1) * 128]
        count_d = own // t_blocks
        for da in range(n_gx):
            for dw in range(n_gy):
                if da or dw:
                    to_x, to_y = lax.rem(gx + da, n_gx), lax.rem(gy + dw, n_gy)
                    begin_d = (
                        lax.rem(to_x, 2) * half + to_x // 2 * piece + to_y * own
                    ) // t_blocks
                    index = da * n_gy + dw
                    rows_out[index] = begin(
                        remote(
                            new_row.at[pl.ds(begin_d, count_d)], got_row.at[index],
                            row_send.at[index], row_recv.at[index], (to_x, to_y, gz),
                        )
                    )
    base = core * half + mid * piece
    third = {}
    for dw in order_z:
        to = lax.rem(gy + dw, n_gy)
        at = to * own
        for dq in range(1, n_x):
            second[dq, dw].wait_recv()
            part[pl.ds(base + at, own)] += got_2[dq - 1, pl.ds(at, own)]
        if dw:
            third[dw] = begin(
                remote(
                    part.at[pl.ds(base + at, own)], got_3.at[dw - 1],
                    end_send.at[dw - 1], end_recv.at[dw - 1], (gx, to, gz),
                )
            )
    mine = base + gy * own
    total = part[pl.ds(mine, own)]
    for dw in range(1, n_gy):
        third[dw].wait_recv()
        total = total + got_3[dw - 1]
    full[pl.ds(mine, own)] = total
    def transform(start, many):
        for index in range(many // t_blocks):
            at = start // t_blocks + index
            values = full[pl.ds(at * t_blocks, t_blocks)].reshape(steps, 128)
            if not isinstance(at, int):
                at = pl.multiple_of(at * 128, 128)
            else:
                at = at * 128
            high = values.astype(jnp.bfloat16)
            low = (values - high.astype(jnp.float32)).astype(jnp.bfloat16)
            far_out[:, pl.ds(at, 128)] = jnp.dot(
                table_ref[...], jnp.concatenate([high, low, high], axis=0),
                preferred_element_type=jnp.float32,
            )

    def arrived(start):
        if early:
            transform(start, own)

    last = {}

    def to_core(start, dq, dw):
        block = full.at[pl.ds(start, own)]
        last[dq, dw] = begin(
            remote(block, block, back_c_send.at[dq, dw], back_c_recv.at[dq, dw], other)
        )

    wide = {}

    def to_mid(start, dw):
        block = full.at[pl.ds(start, own)]
        for dq in range(1, n_x):
            wide[dq, dw] = begin(
                remote(
                    block, block, back_x_send.at[dq - 1, dw], back_x_recv.at[dq - 1, dw],
                    (lax.rem(mid + dq, n_x) * 2 + core, gy, gz),
                )
            )

    long = {}
    for dw in range(1, n_gy):
        block = full.at[pl.ds(mine, own)]
        long[dw] = begin(
            remote(
                block, block, back_z_send.at[dw - 1], back_z_recv.at[dw - 1],
                (gx, lax.rem(gy + dw, n_gy), gz),
            )
        )
    to_mid(mine, 0)
    to_core(mine, 0, 0)
    arrived(mine)
    rows_back = []
    if early:
        mine_d = mine // t_blocks
        added = new_row[pl.ds(mine_d, count_d)]
        for index in rows_out:
            rows_out[index].wait_recv()
            added = added + got_row[index]
        row_all[pl.ds(mine_d, count_d)] = added
        for da in range(n_gx):
            for dw in range(n_gy):
                if da or dw:
                    index = da * n_gy + dw
                    block = row_all.at[pl.ds(mine_d, count_d)]
                    rows_back.append(
                        begin(
                            remote(
                                block, block, all_send.at[index], all_recv.at[index],
                                (lax.rem(gx + da, n_gx), lax.rem(gy + dw, n_gy), gz),
                            )
                        )
                    )
    for dw in range(1, n_gy):
        long[dw].wait_recv()
        start = base + lax.rem(gy + n_gy - dw, n_gy) * own
        to_mid(start, dw)
        to_core(start, 0, dw)
        arrived(start)
    for dw in range(n_gy):
        for dq in range(1, n_x):
            wide[dq, dw].wait_recv()
            start = (
                core * half
                + lax.rem(mid + n_x - dq, n_x) * piece
                + lax.rem(gy + n_gy - dw, n_gy) * own
            )
            to_core(start, dq, dw)
            arrived(start)
    for dw in range(n_gy):
        for dq in range(n_x):
            last[dq, dw].wait_recv()
            arrived(
                (1 - core) * half
                + lax.rem(mid + n_x - dq, n_x) * piece
                + lax.rem(gy + n_gy - dw, n_gy) * own
            )
    if early:
        for copy in rows_back:
            copy.wait_recv()
        last_step = last_ref[...]
        for index in range(chunks // t_blocks):
            far_out[:, index * 128 : (index + 1) * 128] += last_step * row_all[index]
    else:
        transform(0, chunks)

    for copy in sends + tile_copies + (new_copies if early else []):
        copy.wait_send()

    @pl.when(gx > 0)
    def _():
        up_i.wait_send()

    @pl.when(gy > 0)
    def _():
        up_j.wait_send()

    @pl.when(gz > 0)
    def _():
        up_k.wait_send()

    @pl.when(gx < n_gx - 1)
    def _():
        down_i.wait_send()

    @pl.when(gy < n_gy - 1)
    def _():
        down_j.wait_send()

    @pl.when(gz < n_gz - 1)
    def _():
        down_k.wait_send()


def hand_out(*refs):
    sources, targets, sems = refs[:4], refs[4:8], refs[8]
    pairs = [(sources[index], targets[index]) for index in (0, 1, 3)]
    for pole in range(sources[2].shape[0]):
        pairs.append((sources[2].at[pole], targets[2].at[pole]))
    copies = [
        pltpu.make_async_copy(source, target, sems.at[index])
        for index, (source, target) in enumerate(pairs)
    ]
    for copy in copies:
        copy.start()
    for copy in copies:
        copy.wait()


def per_device(
    e_field, h_field, permittivity, wall_mask, poles, pole_decay, pole_gain,
    face_cells, owners, history, steering,
):
    n_gx, n_gy, n_gz = (lax.axis_size(axis) for axis in ("gx", "gy", "gz"))
    n_x = n_gx // 2
    count = face_cells.shape[0]
    steps = history.shape[0] + 1
    cap = steering.shape[1] // (n_gx * n_gz)
    rows = -(-cap // 16) * 16
    dirs = steering.shape[2]
    blocks = n_gx * n_gy
    mine = FREQS // blocks
    _, span_x, span_y, span_z = e_field.shape
    flat = span_x * span_y

    table = spectral_rows(FREQS, FREQS, steps)
    table = table.reshape(2, blocks, mine, steps).transpose(1, 0, 2, 3).reshape(blocks, 2 * mine, steps)
    high = table.astype(jnp.bfloat16)
    low = (table - high.astype(np.float32)).astype(jnp.bfloat16)
    split = np.concatenate([high, high, low], axis=2)
    last = np.broadcast_to(table[:, :, -1:], table.shape[:2] + (128,)).copy()
    hist = jnp.transpose(history, (1, 2, 0))

    chunks = steps // 8 * (dirs // 128)
    half = chunks // 2
    piece = half // n_x
    own = piece // n_gy
    f32, bf16 = jnp.float32, jnp.bfloat16
    dma = lambda *dims: pltpu.SemaphoreType.DMA(dims)
    vmem = pl.BlockSpec(memory_space=pltpu.VMEM)
    hbm = pl.BlockSpec(memory_space=pltpu.HBM)
    wide = max(n_x - 1, 1)
    e_next, h_next, far, poles_next = pl.pallas_call(
        functools.partial(kernel, n_gx, n_gy, n_gz, cap, rows),
        out_shape=(
            jax.ShapeDtypeStruct(e_field.shape, f32),
            jax.ShapeDtypeStruct(h_field.shape, f32),
            jax.ShapeDtypeStruct((2 * mine, dirs), f32),
            jax.ShapeDtypeStruct(poles.shape, f32),
        ),
        in_specs=[hbm] * 13,
        out_specs=(vmem, vmem, vmem, vmem),
        scratch_shapes=[
            pltpu.SMEM(pole_decay.shape, f32),
            pltpu.SMEM(pole_gain.shape, f32),
            pltpu.VMEM(e_field.shape, f32),
            pltpu.VMEM(h_field.shape, f32),
            pltpu.VMEM(permittivity.shape, f32),
            pltpu.VMEM(wall_mask.shape, jnp.int32),
            pltpu.VMEM((1, count), jnp.int32),
            pltpu.VMEM((1, count), jnp.int32),
            pltpu.VMEM(hist.shape, bf16),
            pltpu.VMEM(split.shape[1:], bf16),
            pltpu.VMEM(last.shape[1:], f32),
            pltpu.VMEM(poles.shape, f32),
            pltpu.VMEM(steering.shape, bf16),
            pltpu.VMEM((2, span_x, span_z), f32),
            pltpu.VMEM((8, flat), f32),
            pltpu.VMEM((2, span_y, span_z), f32),
            pltpu.VMEM((2, span_x, span_z), f32),
            pltpu.VMEM((8, flat), f32),
            pltpu.VMEM((2, span_x, span_z), f32),
            pltpu.VMEM((8, flat), f32),
            pltpu.VMEM((2, span_y, span_z), f32),
            pltpu.VMEM((2, span_x, span_z), f32),
            pltpu.VMEM((8, flat), f32),
            pltpu.VMEM((n_gx, rows, 4 * steps), bf16),
            pltpu.VMEM((n_gx * n_gz, rows, 4 * steps), bf16),
            pltpu.VMEM((chunks, 8, 128), f32),
            pltpu.VMEM((half, 8, 128), f32),
            pltpu.VMEM((wide, piece, 8, 128), f32),
            pltpu.VMEM((n_gy - 1, own, 8, 128), f32),
            pltpu.VMEM((chunks, 8, 128), f32),
            pltpu.VMEM((n_gx, rows, 128), bf16),
            pltpu.VMEM((n_gx * n_gz, rows, 128), bf16),
            pltpu.VMEM((dirs // 128, 1, 128), f32),
            pltpu.VMEM((n_gx * n_gy, max(own // (steps // 8), 1), 1, 128), f32),
            pltpu.VMEM((dirs // 128, 1, 128), f32),
            dma(13), dma(6), dma(6), dma(n_gx * n_gz), dma(n_gx * n_gz),
            dma(n_x), dma(n_x), dma(wide, n_gy), dma(wide, n_gy), dma(n_gy - 1), dma(n_gy - 1),
            dma(n_gx * n_gz), dma(n_gx * n_gz), dma(n_gx * n_gy), dma(n_gx * n_gy),
            dma(n_gx * n_gy), dma(n_gx * n_gy), dma(n_gy - 1), dma(n_gy - 1), dma(wide, n_gy), dma(wide, n_gy), dma(n_x, n_gy), dma(n_x, n_gy),
        ],
        compiler_params=pltpu.CompilerParams(
            collective_id=0, has_side_effects=True, vmem_limit_bytes=32 * 1024 * 1024
        ),
    )(
        *(
            pltpu.with_memory_space_constraint(operand, pltpu.HBM)
            for operand in (
                pole_decay, pole_gain, e_field, h_field, permittivity, wall_mask, face_cells.reshape(1, count),
                owners.reshape(1, count), hist, jnp.asarray(split), jnp.asarray(last), poles, steering,
            )
        )
    )
    results = (e_next, h_next, poles_next, far)
    e_next, h_next, poles_next, far = pl.pallas_call(
        hand_out,
        out_shape=tuple(jax.ShapeDtypeStruct(result.shape, f32) for result in results),
        in_specs=[vmem] * 4,
        out_specs=(hbm,) * 4,
        scratch_shapes=[dma(3 + poles.shape[0])],
        compiler_params=pltpu.CompilerParams(vmem_limit_bytes=8 * 1024 * 1024),
    )(*results)
    return (e_next, h_next, poles_next, far.reshape(2, mine, dirs))


def solution(mesh):
    return jax.shard_map(
        per_device,
        mesh=mesh,
        in_specs=(
            P(None, "gx", "gy", "gz"),
            P(None, "gx", "gy", "gz"),
            P("gx", "gy", "gz"),
            P("gx", "gy", "gz"),
            P(None, None, "gx", "gy", "gz"),
            P(),
            P(),
            P(("gx", "gy", "gz")),
            P(("gx", "gy", "gz"), None),
            P(None, None, ("gx", "gy", "gz")),
            P(None, ("gx", "gy"), "gz"),
        ),
        out_specs=(
            P(None, "gx", "gy", "gz"),
            P(None, "gx", "gy", "gz"),
            P(None, None, "gx", "gy", "gz"),
            P(None, ("gx", "gy"), "gz"),
        ),
        check_vma=False,
    )
```

```python
import functools
import math

import jax
import jax.numpy as jnp
import numpy as np
from jax import lax
from jax.experimental import pallas as pl
from jax.experimental.pallas import tpu as pltpu
from jax.sharding import PartitionSpec as P

FREQS = 256
MESH = pl.DeviceIdType.MESH


def spectral_rows(count, freqs, steps):
    times = np.arange(steps, dtype=np.float64)
    levels = np.arange(count, dtype=np.float64) + 0.5
    phase = math.pi / (2.0 * freqs) * levels[:, None] * times[None, :]
    scale = 1.0 / math.sqrt(steps)
    return np.stack([np.cos(phase) * scale, -np.sin(phase) * scale]).astype(np.float32)


def kernel(
    n_gx, n_gy, n_gz, cap, rows,
    decay_hbm, gain_hbm, e_hbm, h_hbm, perm_hbm, mask_hbm, cells_hbm, owners_hbm, hist_hbm,
    table_hbm, last_hbm, poles_hbm, steer_hbm,
    e_out, h_out, far_out, poles_out,
    decay, gain, e_ref, h_ref, perm_ref, mask_ref, cells_ref, own_ref, hist_ref, table_ref, last_ref,
    poles, steer, edge_j, edge_k, got_i, got_j, got_k,
    low_j, low_k, from_i, from_j, from_k, compact, tile, part, got_1, got_2, got_3, full, new_out, new_in, new_row, got_row, row_all,
    local_sem, halo_send, halo_recv, tile_send, tile_recv,
    core_send, core_recv, mid_send, mid_recv, end_send, end_recv,
    new_send, new_recv, row_send, row_recv, all_send, all_recv, back_z_send, back_z_recv, back_x_send, back_x_recv, back_c_send, back_c_recv,
):
    gx, gy, gz = lax.axis_index("gx"), lax.axis_index("gy"), lax.axis_index("gz")
    n_x = n_gx // 2
    core, mid = lax.rem(gx, 2), gx // 2
    span_x, span_y, span_z = e_ref.shape[1:]
    count, past = hist_ref.shape[1:]
    steps = past + 1
    chunks = part.shape[0]
    half = chunks // 2
    piece = half // n_x
    own = piece // n_gy
    t_blocks = steps // 8
    width = piece // t_blocks * 128
    early = own % t_blocks == 0 and rows == cap

    barrier = pltpu.get_barrier_semaphore()
    partners = 0
    for da in range(n_gx):
        for dz in range(n_gz):
            if da or dz:
                peer = (lax.rem(gx + da, n_gx), gy, lax.rem(gz + dz, n_gz))
                pl.semaphore_signal(barrier, inc=1, device_id=peer, device_id_type=MESH)
                partners += 1
    for da in range(n_gx if early else 1):
        for dw in range(1, n_gy):
            peer = (lax.rem(gx + da, n_gx), lax.rem(gy + dw, n_gy), gz)
            pl.semaphore_signal(barrier, inc=1, device_id=peer, device_id_type=MESH)
            partners += 1

    block = gx * n_gy + gy
    loads = [
        pltpu.make_async_copy(source, target, local_sem.at[index])
        for index, (source, target) in enumerate((
            (owners_hbm, own_ref), (hist_hbm, hist_ref), (e_hbm, e_ref), (h_hbm, h_ref),
            (cells_hbm, cells_ref), (steer_hbm, steer), (poles_hbm, poles), (perm_hbm, perm_ref),
            (mask_hbm, mask_ref), (decay_hbm, decay), (gain_hbm, gain),
            (table_hbm.at[block], table_ref), (last_hbm.at[block], last_ref),
        ))
    ]
    for load in loads:
        load.start()

    def remote(src, dst, send, recv, peer):
        return pltpu.make_async_remote_copy(
            src_ref=src, dst_ref=dst, send_sem=send, recv_sem=recv,
            device_id=peer, device_id_type=MESH,
        )

    flat = (span_x * span_y, span_z)
    cells = (span_x, span_y, span_z)

    def column(field, lane):
        return jnp.transpose(field.reshape(flat))[lane : lane + 1]

    def spread(row):
        return jnp.transpose(jnp.broadcast_to(row, (span_z, flat[0]))).reshape(cells)

    up_i = remote(e_ref.at[pl.ds(1, 2), 0], got_i, halo_send.at[0], halo_recv.at[0], (gx - 1, gy, gz))
    up_j = remote(edge_j, got_j, halo_send.at[1], halo_recv.at[1], (gx, gy - 1, gz))
    up_k = remote(edge_k, got_k, halo_send.at[2], halo_recv.at[2], (gx, gy, gz - 1))
    down_i = remote(
        h_out.at[pl.ds(1, 2), span_x - 1], from_i, halo_send.at[3], halo_recv.at[3], (gx + 1, gy, gz)
    )
    down_j = remote(low_j, from_j, halo_send.at[4], halo_recv.at[4], (gx, gy + 1, gz))
    down_k = remote(low_k, from_k, halo_send.at[5], halo_recv.at[5], (gx, gy, gz + 1))

    for load in loads[:2]:
        load.wait()
    sample = lax.broadcasted_iota(jnp.int32, (count, count), 0)
    other_sample = lax.broadcasted_iota(jnp.int32, (count, count), 1)

    def upright(row):
        kept = jnp.where(sample == other_sample, row.astype(jnp.float32), 0.0)
        return jnp.sum(kept, axis=1, keepdims=True).astype(jnp.int32)

    own_row = own_ref[...]
    same = jnp.where((upright(own_row) == own_row) & (sample < other_sample), 1.0, 0.0)
    rank = jnp.sum(same, axis=0, keepdims=True).astype(jnp.int32)
    slot = own_row * rows + rank
    place = (
        lax.broadcasted_iota(jnp.int32, (n_gx * rows, count), 0) == slot
    ).astype(jnp.float32).astype(jnp.bfloat16)

    lane = lax.broadcasted_iota(jnp.int32, (count, 4 * steps), 1)
    samples = jnp.zeros((count, 4 * steps), jnp.float32)
    step_in = lax.broadcasted_iota(jnp.int32, (past, 4 * steps), 0)
    step_out = lax.broadcasted_iota(jnp.int32, (past, 4 * steps), 1)
    for comp in range(4):
        spot = (step_out == step_in + comp * steps).astype(jnp.float32).astype(jnp.bfloat16)
        samples += jnp.dot(hist_ref[comp], spot, preferred_element_type=jnp.float32)
    me = gz * n_gx + gx

    def pack(values, source):
        packed = jnp.dot(
            place, values.astype(jnp.bfloat16), preferred_element_type=jnp.float32
        ).astype(jnp.bfloat16)
        source[...] = packed.reshape(source.shape)

    def send(values, source, target, send_sem, recv_sem):
        pack(values, source)
        return launch(source, target, send_sem, recv_sem)

    def launch(source, target, send_sem, recv_sem):
        copies = []
        for da in range(n_gx):
            for dz in range(n_gz):
                to_x, to_z = lax.rem(gx + da, n_gx), lax.rem(gz + dz, n_gz)
                if da or dz:
                    index = da * n_gz + dz
                    copy = remote(
                        source.at[to_x], target.at[me], send_sem.at[index], recv_sem.at[index],
                        (to_x, gy, to_z),
                    )
                    copy.start()
                    copies.append(copy)
        target[me] = source[gx]
        return copies

    def send_tiles():
        return send(samples, compact, tile, tile_send, tile_recv)

    if early:
        pack(samples, compact)
    loads[2].wait()
    edge_k[0:1] = column(e_ref[0], 0)
    edge_k[1:2] = column(e_ref[1], 0)
    edge_k[2:8] = jnp.zeros((6, flat[0]), jnp.float32)
    edge_j[0] = e_ref[0, :, 0, :]
    edge_j[1] = e_ref[2, :, 0, :]

    pl.semaphore_wait(barrier, partners)
    if early:
        tile_copies = launch(compact, tile, tile_send, tile_recv)

    @pl.when(gz > 0)
    def _():
        up_k.start()

    @pl.when(gx > 0)
    def _():
        up_i.start()

    @pl.when(gy > 0)
    def _():
        up_j.start()

    for load in loads[3:5]:
        load.wait()

    @pl.when(gx == n_gx - 1)
    def _():
        got_i[...] = jnp.zeros(got_i.shape, jnp.float32)

    @pl.when(gy == n_gy - 1)
    def _():
        got_j[...] = jnp.zeros(got_j.shape, jnp.float32)

    @pl.when(gz == n_gz - 1)
    def _():
        got_k[...] = jnp.zeros(got_k.shape, jnp.float32)

    @pl.when(gx == 0)
    def _():
        from_i[...] = jnp.zeros(from_i.shape, jnp.float32)

    @pl.when(gy == 0)
    def _():
        from_j[...] = jnp.zeros(from_j.shape, jnp.float32)

    @pl.when(gz == 0)
    def _():
        from_k[...] = jnp.zeros(from_k.shape, jnp.float32)

    at_j = lax.broadcasted_iota(jnp.int32, cells, 1)
    at_k = lax.broadcasted_iota(jnp.int32, cells, 2)

    def next_j(field, halo):
        return jnp.where(at_j == span_y - 1, halo[:, None, :], pltpu.roll(field, span_y - 1, 1))

    def next_k(field, halo):
        return jnp.where(at_k == span_z - 1, spread(halo), pltpu.roll(field, span_z - 1, 2))

    def prev_j(field, halo):
        return jnp.where(at_j == 0, halo[:, None, :], pltpu.roll(field, 1, 1))

    def prev_k(field, halo):
        return jnp.where(at_k == 0, spread(halo), pltpu.roll(field, 1, 2))

    order_x = list(range(1, n_x)) + [0]
    order_z = list(range(1, n_gy)) + [0]
    sends = []

    def begin(copy):
        copy.start()
        sends.append(copy)
        return copy

    other = (mid * 2 + 1 - core, gy, gz)
    first, second = {}, {}

    def first_half(copies):
        loads[5].wait()
        loads[11].wait()
        loads[12].wait()
        for copy in copies:
            copy.wait_recv()

        sources = n_gx * n_gz
        slots = tile[...].reshape(sources * rows, 4 * steps)
        if rows != cap:
            place_row = lax.broadcasted_iota(jnp.int32, (sources * cap, sources * rows), 0)
            place_col = lax.broadcasted_iota(jnp.int32, (sources * cap, sources * rows), 1)
            keep = (place_col == place_row // cap * rows + lax.rem(place_row, cap)).astype(jnp.float32)
            slots = jnp.dot(
                keep.astype(jnp.bfloat16), slots, preferred_element_type=jnp.float32
            ).astype(jnp.bfloat16)
        turned = jnp.transpose(slots.astype(jnp.float32)).astype(jnp.bfloat16)
        currents = jnp.concatenate(
            [turned[comp * steps : (comp + 1) * steps] for comp in range(4)], axis=1
        )
        depth = 4 * slots.shape[0]

        def fill(start):
            offset = pl.multiple_of(start // t_blocks * 128, 128)
            weights = steer[:, :, pl.ds(offset, width)].reshape(depth, width)
            out = jnp.dot(currents, weights, preferred_element_type=jnp.float32)
            for block in range(width // 128):
                part[pl.ds(start + block * t_blocks, t_blocks)] = out[
                    :, block * 128 : (block + 1) * 128
                ].reshape(t_blocks, 8, 128)

        for dq in order_x:
            to = lax.rem(mid + dq, n_x)
            start = (1 - core) * half + to * piece
            fill(start)
            first[dq] = begin(
                remote(
                    part.at[pl.ds(start, piece)], got_1.at[pl.ds(to * piece, piece)],
                    core_send.at[dq], core_recv.at[dq], other,
                )
            )
        for dq in order_x:
            fill(core * half + lax.rem(mid + dq, n_x) * piece)
    def pass_on():
        for dq in order_x:
            to = lax.rem(mid + dq, n_x)
            start = core * half + to * piece
            first[dq].wait_recv()
            part[pl.ds(start, piece)] += got_1[pl.ds(to * piece, piece)]
            if dq:
                for dw in order_z:
                    at = lax.rem(gy + dw, n_gy) * own
                    second[dq, dw] = begin(
                        remote(
                            part.at[pl.ds(start + at, own)], got_2.at[dq - 1, pl.ds(at, own)],
                            mid_send.at[dq - 1, dw], mid_recv.at[dq - 1, dw], (to * 2 + core, gy, gz),
                        )
                    )

    if early:
        first_half(tile_copies)

    @pl.when(gx < n_gx - 1)
    def _():
        up_i.wait_recv()

    @pl.when(gy < n_gy - 1)
    def _():
        up_j.wait_recv()

    @pl.when(gz < n_gz - 1)
    def _():
        up_k.wait_recv()

    ex, ey, ez = e_ref[0], e_ref[1], e_ref[2]
    ey_i = jnp.concatenate([ey[1:], got_i[0][None]], axis=0)
    ez_i = jnp.concatenate([ez[1:], got_i[1][None]], axis=0)
    mag_x = h_ref[0] - 0.5 * (next_j(ez, got_j[1]) - ez - (next_k(ey, got_k[1:2]) - ey))
    h_out[0] = mag_x
    mag_y = h_ref[1] - 0.5 * (next_k(ex, got_k[0:1]) - ex - (ez_i - ez))
    h_out[1] = mag_y
    mag_z = h_ref[2] - 0.5 * (ey_i - ey - (next_j(ex, got_j[0]) - ex))
    h_out[2] = mag_z

    @pl.when(gx < n_gx - 1)
    def _():
        down_i.start()

    @pl.when(gz < n_gz - 1)
    def _():
        low_k[0:1] = column(h_out[0], span_z - 1)
        low_k[1:2] = column(h_out[1], span_z - 1)
        low_k[2:8] = jnp.zeros((6, flat[0]), jnp.float32)
        down_k.start()

    @pl.when(gy < n_gy - 1)
    def _():
        low_j[0] = h_out[0, :, span_y - 1, :]
        low_j[1] = h_out[2, :, span_y - 1, :]
        down_j.start()

    if early:
        pass_on()

    for load in loads[6:11]:
        load.wait()

    @pl.when(gx > 0)
    def _():
        down_i.wait_recv()

    @pl.when(gy > 0)
    def _():
        down_j.wait_recv()

    @pl.when(gz > 0)
    def _():
        down_k.wait_recv()

    mag_x, mag_y, mag_z = h_out[0], h_out[1], h_out[2]
    mag_y_i = jnp.concatenate([from_i[0][None], mag_y[:-1]], axis=0)
    mag_z_i = jnp.concatenate([from_i[1][None], mag_z[:-1]], axis=0)
    drives = (
        mag_z - prev_j(mag_z, from_j[1]) - (mag_y - prev_k(mag_y, from_k[1:2])),
        mag_x - prev_k(mag_x, from_k[0:1]) - (mag_z - mag_z_i),
        mag_y - mag_y_i - (mag_x - prev_j(mag_x, from_j[0])),
    )
    wall = mask_ref[...] == 1
    half_eps = 0.5 / perm_ref[...]

    def advance(comp):
        drive = drives[comp]
        total = None
        for pole in range(poles.shape[0]):
            state = decay[pole] * poles[pole, comp] + gain[pole] * drive
            poles_out[pole, comp] = state
            total = state if total is None else total + state
        e_out[comp] = jnp.where(wall, total, e_ref[comp] + half_eps * drive)

    advance(0)
    advance(1)


    cell = upright(cells_ref[...])
    row_hot = (
        lax.broadcasted_iota(jnp.int32, (count, flat[0]), 1) == cell // span_z
    ).astype(jnp.float32).astype(jnp.bfloat16)
    lane_hot = lax.broadcasted_iota(jnp.int32, (count, span_z), 1) == lax.rem(cell, span_z)
    fresh_lane = lax.broadcasted_iota(jnp.int32, (count, 128), 1)
    fresh_all = jnp.zeros((count, 128), jnp.float32)
    for comp, field in enumerate((e_out[0], e_out[1], h_out[0], h_out[1])):
        found = jnp.dot(
            row_hot, field.reshape(flat).astype(jnp.bfloat16), preferred_element_type=jnp.float32
        )
        fresh = jnp.sum(jnp.where(lane_hot, found, 0.0), axis=1, keepdims=True)
        if early:
            fresh_all = jnp.where(fresh_lane == comp, fresh, fresh_all)
        else:
            samples = jnp.where(lane == comp * steps + steps - 1, fresh, samples)
    if early:
        new_copies = send(fresh_all, new_out, new_in, new_send, new_recv)
    else:
        tile_copies = send_tiles()
        first_half(tile_copies)
        pass_on()

    base = core * half + mid * piece
    third = {}
    for dw in order_z:
        to = lax.rem(gy + dw, n_gy)
        at = to * own
        for dq in range(1, n_x):
            second[dq, dw].wait_recv()
            part[pl.ds(base + at, own)] += got_2[dq - 1, pl.ds(at, own)]
        if dw:
            third[dw] = begin(
                remote(
                    part.at[pl.ds(base + at, own)], got_3.at[dw - 1],
                    end_send.at[dw - 1], end_recv.at[dw - 1], (gx, to, gz),
                )
            )
    mine = base + gy * own
    rows_out = {}
    if early:
        for copy in new_copies:
            copy.wait_recv()
        turned = jnp.transpose(new_in[...].reshape(n_gx * n_gz * rows, 128).astype(jnp.float32))
        line = jnp.concatenate([turned[comp : comp + 1] for comp in range(4)], axis=1)
        line = jnp.broadcast_to(line, (16, line.shape[1])).astype(jnp.bfloat16)
        for start in range(0, new_row.shape[0], 4):
            weights = steer[:, :, start * 128 : (start + 4) * 128].reshape(line.shape[1], 512)
            out = jnp.dot(line, weights, preferred_element_type=jnp.float32)
            for index in range(4):
                new_row[start + index] = out[0:1, index * 128 : (index + 1) * 128]
        count_d = own // t_blocks
        for da in range(n_gx):
            for dw in range(n_gy):
                if da or dw:
                    to_x, to_y = lax.rem(gx + da, n_gx), lax.rem(gy + dw, n_gy)
                    begin_d = (
                        lax.rem(to_x, 2) * half + to_x // 2 * piece + to_y * own
                    ) // t_blocks
                    index = da * n_gy + dw
                    rows_out[index] = begin(
                        remote(
                            new_row.at[pl.ds(begin_d, count_d)], got_row.at[index],
                            row_send.at[index], row_recv.at[index], (to_x, to_y, gz),
                        )
                    )
    total = part[pl.ds(mine, own)]
    for dw in range(1, n_gy):
        third[dw].wait_recv()
        total = total + got_3[dw - 1]
    full[pl.ds(mine, own)] = total
    def transform(start, many):
        for index in range(many // t_blocks):
            at = start // t_blocks + index
            values = full[pl.ds(at * t_blocks, t_blocks)].reshape(steps, 128)
            if not isinstance(at, int):
                at = pl.multiple_of(at * 128, 128)
            else:
                at = at * 128
            high = values.astype(jnp.bfloat16)
            low = (values - high.astype(jnp.float32)).astype(jnp.bfloat16)
            far_out[:, pl.ds(at, 128)] = jnp.dot(
                table_ref[...], jnp.concatenate([high, low, high], axis=0),
                preferred_element_type=jnp.float32,
            )

    def arrived(start):
        if early:
            transform(start, own)

    last = {}

    def to_core(start, dq, dw):
        block = full.at[pl.ds(start, own)]
        last[dq, dw] = begin(
            remote(block, block, back_c_send.at[dq, dw], back_c_recv.at[dq, dw], other)
        )

    wide = {}

    def to_mid(start, dw):
        block = full.at[pl.ds(start, own)]
        for dq in range(1, n_x):
            wide[dq, dw] = begin(
                remote(
                    block, block, back_x_send.at[dq - 1, dw], back_x_recv.at[dq - 1, dw],
                    (lax.rem(mid + dq, n_x) * 2 + core, gy, gz),
                )
            )

    long = {}
    for dw in range(1, n_gy):
        block = full.at[pl.ds(mine, own)]
        long[dw] = begin(
            remote(
                block, block, back_z_send.at[dw - 1], back_z_recv.at[dw - 1],
                (gx, lax.rem(gy + dw, n_gy), gz),
            )
        )
    to_mid(mine, 0)
    to_core(mine, 0, 0)
    arrived(mine)
    advance(2)
    rows_back = []
    if early:
        mine_d = mine // t_blocks
        added = new_row[pl.ds(mine_d, count_d)]
        for index in rows_out:
            rows_out[index].wait_recv()
            added = added + got_row[index]
        row_all[pl.ds(mine_d, count_d)] = added
        for da in range(n_gx):
            for dw in range(n_gy):
                if da or dw:
                    index = da * n_gy + dw
                    block = row_all.at[pl.ds(mine_d, count_d)]
                    rows_back.append(
                        begin(
                            remote(
                                block, block, all_send.at[index], all_recv.at[index],
                                (lax.rem(gx + da, n_gx), lax.rem(gy + dw, n_gy), gz),
                            )
                        )
                    )
    for dw in range(1, n_gy):
        long[dw].wait_recv()
        start = base + lax.rem(gy + n_gy - dw, n_gy) * own
        to_mid(start, dw)
        to_core(start, 0, dw)
        arrived(start)
    for dw in range(n_gy):
        for dq in range(1, n_x):
            wide[dq, dw].wait_recv()
            start = (
                core * half
                + lax.rem(mid + n_x - dq, n_x) * piece
                + lax.rem(gy + n_gy - dw, n_gy) * own
            )
            to_core(start, dq, dw)
            arrived(start)
    for dw in range(n_gy):
        for dq in range(n_x):
            last[dq, dw].wait_recv()
            arrived(
                (1 - core) * half
                + lax.rem(mid + n_x - dq, n_x) * piece
                + lax.rem(gy + n_gy - dw, n_gy) * own
            )
    if early:
        for copy in rows_back:
            copy.wait_recv()
        last_step = last_ref[...]
        for index in range(chunks // t_blocks):
            far_out[:, index * 128 : (index + 1) * 128] += last_step * row_all[index]
    else:
        transform(0, chunks)

    for copy in sends + tile_copies + (new_copies if early else []):
        copy.wait_send()

    @pl.when(gx > 0)
    def _():
        up_i.wait_send()

    @pl.when(gy > 0)
    def _():
        up_j.wait_send()

    @pl.when(gz > 0)
    def _():
        up_k.wait_send()

    @pl.when(gx < n_gx - 1)
    def _():
        down_i.wait_send()

    @pl.when(gy < n_gy - 1)
    def _():
        down_j.wait_send()

    @pl.when(gz < n_gz - 1)
    def _():
        down_k.wait_send()


def hand_out(*refs):
    sources, targets, sems = refs[:4], refs[4:8], refs[8]
    pairs = zip(sources, targets)
    copies = [
        pltpu.make_async_copy(source, target, sems.at[index])
        for index, (source, target) in enumerate(pairs)
    ]
    for copy in copies:
        copy.start()
    for copy in copies:
        copy.wait()


def per_device(
    e_field, h_field, permittivity, wall_mask, poles, pole_decay, pole_gain,
    face_cells, owners, history, steering,
):
    n_gx, n_gy, n_gz = (lax.axis_size(axis) for axis in ("gx", "gy", "gz"))
    n_x = n_gx // 2
    count = face_cells.shape[0]
    steps = history.shape[0] + 1
    cap = steering.shape[1] // (n_gx * n_gz)
    rows = -(-cap // 16) * 16
    dirs = steering.shape[2]
    blocks = n_gx * n_gy
    mine = FREQS // blocks
    _, span_x, span_y, span_z = e_field.shape
    flat = span_x * span_y

    table = spectral_rows(FREQS, FREQS, steps)
    table = table.reshape(2, blocks, mine, steps).transpose(1, 0, 2, 3).reshape(blocks, 2 * mine, steps)
    high = table.astype(jnp.bfloat16)
    low = (table - high.astype(np.float32)).astype(jnp.bfloat16)
    split = np.concatenate([high, high, low], axis=2)
    last = np.broadcast_to(table[:, :, -1:], table.shape[:2] + (128,)).copy()
    hist = jnp.transpose(history, (1, 2, 0))

    chunks = steps // 8 * (dirs // 128)
    half = chunks // 2
    piece = half // n_x
    own = piece // n_gy
    f32, bf16 = jnp.float32, jnp.bfloat16
    dma = lambda *dims: pltpu.SemaphoreType.DMA(dims)
    vmem = pl.BlockSpec(memory_space=pltpu.VMEM)
    hbm = pl.BlockSpec(memory_space=pltpu.HBM)
    wide = max(n_x - 1, 1)
    e_next, h_next, far, poles_next = pl.pallas_call(
        functools.partial(kernel, n_gx, n_gy, n_gz, cap, rows),
        out_shape=(
            jax.ShapeDtypeStruct(e_field.shape, f32),
            jax.ShapeDtypeStruct(h_field.shape, f32),
            jax.ShapeDtypeStruct((2 * mine, dirs), f32),
            jax.ShapeDtypeStruct(poles.shape, f32),
        ),
        in_specs=[hbm] * 13,
        out_specs=(vmem, vmem, vmem, vmem),
        scratch_shapes=[
            pltpu.SMEM(pole_decay.shape, f32),
            pltpu.SMEM(pole_gain.shape, f32),
            pltpu.VMEM(e_field.shape, f32),
            pltpu.VMEM(h_field.shape, f32),
            pltpu.VMEM(permittivity.shape, f32),
            pltpu.VMEM(wall_mask.shape, jnp.int32),
            pltpu.VMEM((1, count), jnp.int32),
            pltpu.VMEM((1, count), jnp.int32),
            pltpu.VMEM(hist.shape, bf16),
            pltpu.VMEM(split.shape[1:], bf16),
            pltpu.VMEM(last.shape[1:], f32),
            pltpu.VMEM(poles.shape, f32),
            pltpu.VMEM(steering.shape, bf16),
            pltpu.VMEM((2, span_x, span_z), f32),
            pltpu.VMEM((8, flat), f32),
            pltpu.VMEM((2, span_y, span_z), f32),
            pltpu.VMEM((2, span_x, span_z), f32),
            pltpu.VMEM((8, flat), f32),
            pltpu.VMEM((2, span_x, span_z), f32),
            pltpu.VMEM((8, flat), f32),
            pltpu.VMEM((2, span_y, span_z), f32),
            pltpu.VMEM((2, span_x, span_z), f32),
            pltpu.VMEM((8, flat), f32),
            pltpu.VMEM((n_gx, rows, 4 * steps), bf16),
            pltpu.VMEM((n_gx * n_gz, rows, 4 * steps), bf16),
            pltpu.VMEM((chunks, 8, 128), f32),
            pltpu.VMEM((half, 8, 128), f32),
            pltpu.VMEM((wide, piece, 8, 128), f32),
            pltpu.VMEM((n_gy - 1, own, 8, 128), f32),
            pltpu.VMEM((chunks, 8, 128), f32),
            pltpu.VMEM((n_gx, rows, 128), bf16),
            pltpu.VMEM((n_gx * n_gz, rows, 128), bf16),
            pltpu.VMEM((dirs // 128, 1, 128), f32),
            pltpu.VMEM((n_gx * n_gy, max(own // (steps // 8), 1), 1, 128), f32),
            pltpu.VMEM((dirs // 128, 1, 128), f32),
            dma(13), dma(6), dma(6), dma(n_gx * n_gz), dma(n_gx * n_gz),
            dma(n_x), dma(n_x), dma(wide, n_gy), dma(wide, n_gy), dma(n_gy - 1), dma(n_gy - 1),
            dma(n_gx * n_gz), dma(n_gx * n_gz), dma(n_gx * n_gy), dma(n_gx * n_gy),
            dma(n_gx * n_gy), dma(n_gx * n_gy), dma(n_gy - 1), dma(n_gy - 1), dma(wide, n_gy), dma(wide, n_gy), dma(n_x, n_gy), dma(n_x, n_gy),
        ],
        compiler_params=pltpu.CompilerParams(
            collective_id=0, has_side_effects=True, vmem_limit_bytes=32 * 1024 * 1024
        ),
    )(
        *(
            pltpu.with_memory_space_constraint(operand, pltpu.HBM)
            for operand in (
                pole_decay, pole_gain, e_field, h_field, permittivity, wall_mask, face_cells.reshape(1, count),
                owners.reshape(1, count), hist, jnp.asarray(split), jnp.asarray(last), poles, steering,
            )
        )
    )
    results = (e_next, h_next, poles_next, far)
    e_next, h_next, poles_next, far = pl.pallas_call(
        hand_out,
        out_shape=tuple(jax.ShapeDtypeStruct(result.shape, f32) for result in results),
        in_specs=[vmem] * 4,
        out_specs=(hbm,) * 4,
        scratch_shapes=[dma(4)],
        compiler_params=pltpu.CompilerParams(vmem_limit_bytes=8 * 1024 * 1024),
    )(*results)
    return (e_next, h_next, poles_next, far.reshape(2, mine, dirs))


def solution(mesh):
    return jax.shard_map(
        per_device,
        mesh=mesh,
        in_specs=(
            P(None, "gx", "gy", "gz"),
            P(None, "gx", "gy", "gz"),
            P("gx", "gy", "gz"),
            P("gx", "gy", "gz"),
            P(None, None, "gx", "gy", "gz"),
            P(),
            P(),
            P(("gx", "gy", "gz")),
            P(("gx", "gy", "gz"), None),
            P(None, None, ("gx", "gy", "gz")),
            P(None, ("gx", "gy"), "gz"),
        ),
        out_specs=(
            P(None, "gx", "gy", "gz"),
            P(None, "gx", "gy", "gz"),
            P(None, None, "gx", "gy", "gz"),
            P(None, ("gx", "gy"), "gz"),
        ),
        check_vma=False,
    )
```

```python
import functools
import math

import jax
import jax.numpy as jnp
import numpy as np
from jax import lax
from jax.experimental import pallas as pl
from jax.experimental.pallas import tpu as pltpu
from jax.sharding import PartitionSpec as P

FREQS = 256
MESH = pl.DeviceIdType.MESH


def spectral_rows(count, freqs, steps):
    times = np.arange(steps, dtype=np.float64)
    levels = np.arange(count, dtype=np.float64) + 0.5
    phase = math.pi / (2.0 * freqs) * levels[:, None] * times[None, :]
    scale = 1.0 / math.sqrt(steps)
    return np.stack([np.cos(phase) * scale, -np.sin(phase) * scale]).astype(np.float32)


def kernel(
    n_gx, n_gy, n_gz, cap, rows,
    decay_hbm, gain_hbm, e_hbm, h_hbm, perm_hbm, mask_hbm, cells_hbm, owners_hbm, hist_hbm,
    table_hbm, last_hbm, poles_hbm, steer_hbm,
    e_out, h_out, far_out, poles_out,
    decay, gain, e_ref, h_ref, perm_ref, mask_ref, cells_ref, own_ref, hist_ref, table_ref, last_ref,
    poles, steer, edge_j, edge_k, got_i, got_j, got_k,
    low_j, low_k, from_i, from_j, from_k, compact, tile, part, got_1, got_2, got_3, full, new_out, new_in, new_row, got_row, row_all,
    local_sem, halo_send, halo_recv, tile_send, tile_recv,
    core_send, core_recv, mid_send, mid_recv, end_send, end_recv,
    new_send, new_recv, row_send, row_recv, all_send, all_recv, back_z_send, back_z_recv, back_x_send, back_x_recv, back_c_send, back_c_recv,
):
    gx, gy, gz = lax.axis_index("gx"), lax.axis_index("gy"), lax.axis_index("gz")
    n_x = n_gx // 2
    core, mid = lax.rem(gx, 2), gx // 2
    span_x, span_y, span_z = e_ref.shape[1:]
    count, past = hist_ref.shape[1:]
    steps = past + 1
    chunks = part.shape[0]
    half = chunks // 2
    piece = half // n_x
    own = piece // n_gy
    t_blocks = steps // 8
    width = piece // t_blocks * 128
    early = own % t_blocks == 0 and rows == cap

    barrier = pltpu.get_barrier_semaphore()
    partners = 0
    for da in range(n_gx):
        for dz in range(n_gz):
            if da or dz:
                peer = (lax.rem(gx + da, n_gx), gy, lax.rem(gz + dz, n_gz))
                pl.semaphore_signal(barrier, inc=1, device_id=peer, device_id_type=MESH)
                partners += 1
    for da in range(n_gx if early else 1):
        for dw in range(1, n_gy):
            peer = (lax.rem(gx + da, n_gx), lax.rem(gy + dw, n_gy), gz)
            pl.semaphore_signal(barrier, inc=1, device_id=peer, device_id_type=MESH)
            partners += 1

    block = gx * n_gy + gy
    loads = [
        pltpu.make_async_copy(source, target, local_sem.at[index])
        for index, (source, target) in enumerate((
            (owners_hbm, own_ref), (hist_hbm, hist_ref), (e_hbm, e_ref), (h_hbm, h_ref),
            (cells_hbm, cells_ref), (steer_hbm, steer), (poles_hbm, poles), (perm_hbm, perm_ref),
            (mask_hbm, mask_ref), (decay_hbm, decay), (gain_hbm, gain),
            (table_hbm.at[block], table_ref), (last_hbm.at[block], last_ref),
        ))
    ]
    for load in loads:
        load.start()

    def remote(src, dst, send, recv, peer):
        return pltpu.make_async_remote_copy(
            src_ref=src, dst_ref=dst, send_sem=send, recv_sem=recv,
            device_id=peer, device_id_type=MESH,
        )

    flat = (span_x * span_y, span_z)
    cells = (span_x, span_y, span_z)

    def column(field, lane):
        return jnp.transpose(field.reshape(flat))[lane : lane + 1]

    def spread(row):
        return jnp.transpose(jnp.broadcast_to(row, (span_z, flat[0]))).reshape(cells)

    up_i = remote(e_ref.at[pl.ds(1, 2), 0], got_i, halo_send.at[0], halo_recv.at[0], (gx - 1, gy, gz))
    up_j = remote(edge_j, got_j, halo_send.at[1], halo_recv.at[1], (gx, gy - 1, gz))
    up_k = remote(edge_k, got_k, halo_send.at[2], halo_recv.at[2], (gx, gy, gz - 1))
    down_i = remote(
        h_out.at[pl.ds(1, 2), span_x - 1], from_i, halo_send.at[3], halo_recv.at[3], (gx + 1, gy, gz)
    )
    down_j = remote(low_j, from_j, halo_send.at[4], halo_recv.at[4], (gx, gy + 1, gz))
    down_k = remote(low_k, from_k, halo_send.at[5], halo_recv.at[5], (gx, gy, gz + 1))

    for load in loads[:2]:
        load.wait()
    sample = lax.broadcasted_iota(jnp.int32, (count, count), 0)
    other_sample = lax.broadcasted_iota(jnp.int32, (count, count), 1)

    def upright(row):
        kept = jnp.where(sample == other_sample, row.astype(jnp.float32), 0.0)
        return jnp.sum(kept, axis=1, keepdims=True).astype(jnp.int32)

    own_row = own_ref[...]
    same = jnp.where((upright(own_row) == own_row) & (sample < other_sample), 1.0, 0.0)
    rank = jnp.sum(same, axis=0, keepdims=True).astype(jnp.int32)
    slot = own_row * rows + rank
    place = (
        lax.broadcasted_iota(jnp.int32, (n_gx * rows, count), 0) == slot
    ).astype(jnp.float32).astype(jnp.bfloat16)

    lane = lax.broadcasted_iota(jnp.int32, (count, 4 * steps), 1)
    samples = jnp.zeros((count, 4 * steps), jnp.float32)
    step_in = lax.broadcasted_iota(jnp.int32, (past, 4 * steps), 0)
    step_out = lax.broadcasted_iota(jnp.int32, (past, 4 * steps), 1)
    for comp in range(4):
        spot = (step_out == step_in + comp * steps).astype(jnp.float32).astype(jnp.bfloat16)
        samples += jnp.dot(hist_ref[comp], spot, preferred_element_type=jnp.float32)
    me = gz * n_gx + gx

    def pack(values, source):
        packed = jnp.dot(
            place, values.astype(jnp.bfloat16), preferred_element_type=jnp.float32
        ).astype(jnp.bfloat16)
        source[...] = packed.reshape(source.shape)

    def send(values, source, target, send_sem, recv_sem):
        pack(values, source)
        return launch(source, target, send_sem, recv_sem)

    def launch(source, target, send_sem, recv_sem):
        copies = []
        for da in range(n_gx):
            for dz in range(n_gz):
                to_x, to_z = lax.rem(gx + da, n_gx), lax.rem(gz + dz, n_gz)
                if da or dz:
                    index = da * n_gz + dz
                    copy = remote(
                        source.at[to_x], target.at[me], send_sem.at[index], recv_sem.at[index],
                        (to_x, gy, to_z),
                    )
                    copy.start()
                    copies.append(copy)
        target[me] = source[gx]
        return copies

    def send_tiles():
        return send(samples, compact, tile, tile_send, tile_recv)

    if early:
        pack(samples, compact)
    loads[2].wait()
    edge_k[0:1] = column(e_ref[0], 0)
    edge_k[1:2] = column(e_ref[1], 0)
    edge_k[2:8] = jnp.zeros((6, flat[0]), jnp.float32)
    edge_j[0] = e_ref[0, :, 0, :]
    edge_j[1] = e_ref[2, :, 0, :]

    pl.semaphore_wait(barrier, partners)
    if early:
        tile_copies = launch(compact, tile, tile_send, tile_recv)

    @pl.when(gz > 0)
    def _():
        up_k.start()

    @pl.when(gx > 0)
    def _():
        up_i.start()

    @pl.when(gy > 0)
    def _():
        up_j.start()

    for load in loads[3:5]:
        load.wait()

    @pl.when(gx == n_gx - 1)
    def _():
        got_i[...] = jnp.zeros(got_i.shape, jnp.float32)

    @pl.when(gy == n_gy - 1)
    def _():
        got_j[...] = jnp.zeros(got_j.shape, jnp.float32)

    @pl.when(gz == n_gz - 1)
    def _():
        got_k[...] = jnp.zeros(got_k.shape, jnp.float32)

    @pl.when(gx == 0)
    def _():
        from_i[...] = jnp.zeros(from_i.shape, jnp.float32)

    @pl.when(gy == 0)
    def _():
        from_j[...] = jnp.zeros(from_j.shape, jnp.float32)

    @pl.when(gz == 0)
    def _():
        from_k[...] = jnp.zeros(from_k.shape, jnp.float32)

    at_j = lax.broadcasted_iota(jnp.int32, cells, 1)
    at_k = lax.broadcasted_iota(jnp.int32, cells, 2)

    def next_j(field, halo):
        return jnp.where(at_j == span_y - 1, halo[:, None, :], pltpu.roll(field, span_y - 1, 1))

    def next_k(field, halo):
        return jnp.where(at_k == span_z - 1, spread(halo), pltpu.roll(field, span_z - 1, 2))

    def prev_j(field, halo):
        return jnp.where(at_j == 0, halo[:, None, :], pltpu.roll(field, 1, 1))

    def prev_k(field, halo):
        return jnp.where(at_k == 0, spread(halo), pltpu.roll(field, 1, 2))

    order_x = list(range(1, n_x)) + [0]
    order_z = list(range(1, n_gy)) + [0]
    sends = []

    def begin(copy):
        copy.start()
        sends.append(copy)
        return copy

    other = (mid * 2 + 1 - core, gy, gz)
    first, second = {}, {}

    def first_half(copies):
        loads[5].wait()
        loads[11].wait()
        loads[12].wait()
        for copy in copies:
            copy.wait_recv()

        sources = n_gx * n_gz
        slots = tile[...].reshape(sources * rows, 4 * steps)
        if rows != cap:
            place_row = lax.broadcasted_iota(jnp.int32, (sources * cap, sources * rows), 0)
            place_col = lax.broadcasted_iota(jnp.int32, (sources * cap, sources * rows), 1)
            keep = (place_col == place_row // cap * rows + lax.rem(place_row, cap)).astype(jnp.float32)
            slots = jnp.dot(
                keep.astype(jnp.bfloat16), slots, preferred_element_type=jnp.float32
            ).astype(jnp.bfloat16)
        turned = jnp.transpose(slots.astype(jnp.float32)).astype(jnp.bfloat16)
        currents = jnp.concatenate(
            [turned[comp * steps : (comp + 1) * steps] for comp in range(4)], axis=1
        )
        depth = 4 * slots.shape[0]

        def fill(start):
            offset = pl.multiple_of(start // t_blocks * 128, 128)
            weights = steer[:, :, pl.ds(offset, width)].reshape(depth, width)
            out = jnp.dot(currents, weights, preferred_element_type=jnp.float32)
            for block in range(width // 128):
                part[pl.ds(start + block * t_blocks, t_blocks)] = out[
                    :, block * 128 : (block + 1) * 128
                ].reshape(t_blocks, 8, 128)

        for dq in order_x:
            to = lax.rem(mid + dq, n_x)
            start = (1 - core) * half + to * piece
            fill(start)
            first[dq] = begin(
                remote(
                    part.at[pl.ds(start, piece)], got_1.at[pl.ds(to * piece, piece)],
                    core_send.at[dq], core_recv.at[dq], other,
                )
            )
        for dq in order_x:
            fill(core * half + lax.rem(mid + dq, n_x) * piece)
    def pass_on():
        for dq in order_x:
            to = lax.rem(mid + dq, n_x)
            start = core * half + to * piece
            first[dq].wait_recv()
            part[pl.ds(start, piece)] += got_1[pl.ds(to * piece, piece)]
            if dq:
                for dw in order_z:
                    at = lax.rem(gy + dw, n_gy) * own
                    second[dq, dw] = begin(
                        remote(
                            part.at[pl.ds(start + at, own)], got_2.at[dq - 1, pl.ds(at, own)],
                            mid_send.at[dq - 1, dw], mid_recv.at[dq - 1, dw], (to * 2 + core, gy, gz),
                        )
                    )

    if early:
        first_half(tile_copies)

    @pl.when(gx < n_gx - 1)
    def _():
        up_i.wait_recv()

    @pl.when(gy < n_gy - 1)
    def _():
        up_j.wait_recv()

    @pl.when(gz < n_gz - 1)
    def _():
        up_k.wait_recv()

    ex, ey, ez = e_ref[0], e_ref[1], e_ref[2]
    ey_i = jnp.concatenate([ey[1:], got_i[0][None]], axis=0)
    ez_i = jnp.concatenate([ez[1:], got_i[1][None]], axis=0)
    mag_x = h_ref[0] - 0.5 * (next_j(ez, got_j[1]) - ez - (next_k(ey, got_k[1:2]) - ey))
    h_out[0] = mag_x
    mag_y = h_ref[1] - 0.5 * (next_k(ex, got_k[0:1]) - ex - (ez_i - ez))
    h_out[1] = mag_y
    mag_z = h_ref[2] - 0.5 * (ey_i - ey - (next_j(ex, got_j[0]) - ex))
    h_out[2] = mag_z

    @pl.when(gx < n_gx - 1)
    def _():
        down_i.start()

    @pl.when(gz < n_gz - 1)
    def _():
        low_k[0:1] = column(h_out[0], span_z - 1)
        low_k[1:2] = column(h_out[1], span_z - 1)
        low_k[2:8] = jnp.zeros((6, flat[0]), jnp.float32)
        down_k.start()

    @pl.when(gy < n_gy - 1)
    def _():
        low_j[0] = h_out[0, :, span_y - 1, :]
        low_j[1] = h_out[2, :, span_y - 1, :]
        down_j.start()

    if early:
        pass_on()

    for load in loads[6:11]:
        load.wait()

    @pl.when(gx > 0)
    def _():
        down_i.wait_recv()

    @pl.when(gy > 0)
    def _():
        down_j.wait_recv()

    @pl.when(gz > 0)
    def _():
        down_k.wait_recv()

    mag_x, mag_y, mag_z = h_out[0], h_out[1], h_out[2]
    mag_y_i = jnp.concatenate([from_i[0][None], mag_y[:-1]], axis=0)
    mag_z_i = jnp.concatenate([from_i[1][None], mag_z[:-1]], axis=0)
    drives = (
        mag_z - prev_j(mag_z, from_j[1]) - (mag_y - prev_k(mag_y, from_k[1:2])),
        mag_x - prev_k(mag_x, from_k[0:1]) - (mag_z - mag_z_i),
        mag_y - mag_y_i - (mag_x - prev_j(mag_x, from_j[0])),
    )
    wall = mask_ref[...] == 1
    half_eps = 0.5 / perm_ref[...]

    def advance(comp):
        drive = drives[comp]
        total = None
        for pole in range(poles.shape[0]):
            state = decay[pole] * poles[pole, comp] + gain[pole] * drive
            poles_out[pole, comp] = state
            total = state if total is None else total + state
        e_out[comp] = jnp.where(wall, total, e_ref[comp] + half_eps * drive)

    advance(0)
    advance(1)


    cell = upright(cells_ref[...])
    row_hot = (
        lax.broadcasted_iota(jnp.int32, (count, flat[0]), 1) == cell // span_z
    ).astype(jnp.float32).astype(jnp.bfloat16)
    lane_hot = lax.broadcasted_iota(jnp.int32, (count, span_z), 1) == lax.rem(cell, span_z)
    fresh_lane = lax.broadcasted_iota(jnp.int32, (count, 128), 1)
    fresh_all = jnp.zeros((count, 128), jnp.float32)
    for comp, field in enumerate((e_out[0], e_out[1], h_out[0], h_out[1])):
        found = jnp.dot(
            row_hot, field.reshape(flat).astype(jnp.bfloat16), preferred_element_type=jnp.float32
        )
        fresh = jnp.sum(jnp.where(lane_hot, found, 0.0), axis=1, keepdims=True)
        if early:
            fresh_all = jnp.where(fresh_lane == comp, fresh, fresh_all)
        else:
            samples = jnp.where(lane == comp * steps + steps - 1, fresh, samples)
    if early:
        new_copies = send(fresh_all, new_out, new_in, new_send, new_recv)
    else:
        tile_copies = send_tiles()
        first_half(tile_copies)
        pass_on()

    base = core * half + mid * piece
    third = {}
    for dw in order_z:
        to = lax.rem(gy + dw, n_gy)
        at = to * own
        for dq in range(1, n_x):
            second[dq, dw].wait_recv()
            part[pl.ds(base + at, own)] += got_2[dq - 1, pl.ds(at, own)]
        if dw:
            third[dw] = begin(
                remote(
                    part.at[pl.ds(base + at, own)], got_3.at[dw - 1],
                    end_send.at[dw - 1], end_recv.at[dw - 1], (gx, to, gz),
                )
            )
    mine = base + gy * own
    total = part[pl.ds(mine, own)]
    for dw in range(1, n_gy):
        third[dw].wait_recv()
        total = total + got_3[dw - 1]
    full[pl.ds(mine, own)] = total
    def transform(start, many):
        for index in range(many // t_blocks):
            at = start // t_blocks + index
            values = full[pl.ds(at * t_blocks, t_blocks)].reshape(steps, 128)
            if not isinstance(at, int):
                at = pl.multiple_of(at * 128, 128)
            else:
                at = at * 128
            high = values.astype(jnp.bfloat16)
            low = (values - high.astype(jnp.float32)).astype(jnp.bfloat16)
            far_out[:, pl.ds(at, 128)] = jnp.dot(
                table_ref[...], jnp.concatenate([high, low, high], axis=0),
                preferred_element_type=jnp.float32,
            )

    def arrived(start):
        if early:
            transform(start, own)

    last = {}

    def to_core(start, dq, dw):
        block = full.at[pl.ds(start, own)]
        last[dq, dw] = begin(
            remote(block, block, back_c_send.at[dq, dw], back_c_recv.at[dq, dw], other)
        )

    wide = {}

    def to_mid(start, dw):
        block = full.at[pl.ds(start, own)]
        for dq in range(1, n_x):
            wide[dq, dw] = begin(
                remote(
                    block, block, back_x_send.at[dq - 1, dw], back_x_recv.at[dq - 1, dw],
                    (lax.rem(mid + dq, n_x) * 2 + core, gy, gz),
                )
            )

    long = {}
    for dw in range(1, n_gy):
        block = full.at[pl.ds(mine, own)]
        long[dw] = begin(
            remote(
                block, block, back_z_send.at[dw - 1], back_z_recv.at[dw - 1],
                (gx, lax.rem(gy + dw, n_gy), gz),
            )
        )
    to_mid(mine, 0)
    to_core(mine, 0, 0)
    arrived(mine)
    rows_out = {}
    if early:
        for copy in new_copies:
            copy.wait_recv()
        turned = jnp.transpose(new_in[...].reshape(n_gx * n_gz * rows, 128).astype(jnp.float32))
        line = jnp.concatenate([turned[comp : comp + 1] for comp in range(4)], axis=1)
        line = jnp.broadcast_to(line, (16, line.shape[1])).astype(jnp.bfloat16)
        for start in range(0, new_row.shape[0], 4):
            weights = steer[:, :, start * 128 : (start + 4) * 128].reshape(line.shape[1], 512)
            out = jnp.dot(line, weights, preferred_element_type=jnp.float32)
            for index in range(4):
                new_row[start + index] = out[0:1, index * 128 : (index + 1) * 128]
        count_d = own // t_blocks
        for da in range(n_gx):
            for dw in range(n_gy):
                if da or dw:
                    to_x, to_y = lax.rem(gx + da, n_gx), lax.rem(gy + dw, n_gy)
                    begin_d = (
                        lax.rem(to_x, 2) * half + to_x // 2 * piece + to_y * own
                    ) // t_blocks
                    index = da * n_gy + dw
                    rows_out[index] = begin(
                        remote(
                            new_row.at[pl.ds(begin_d, count_d)], got_row.at[index],
                            row_send.at[index], row_recv.at[index], (to_x, to_y, gz),
                        )
                    )
    for dw in range(1, n_gy):
        long[dw].wait_recv()
        start = base + lax.rem(gy + n_gy - dw, n_gy) * own
        to_mid(start, dw)
        to_core(start, 0, dw)
        arrived(start)
    advance(2)
    rows_back = []
    if early:
        mine_d = mine // t_blocks
        added = new_row[pl.ds(mine_d, count_d)]
        for index in rows_out:
            rows_out[index].wait_recv()
            added = added + got_row[index]
        row_all[pl.ds(mine_d, count_d)] = added
        for da in range(n_gx):
            for dw in range(n_gy):
                if da or dw:
                    index = da * n_gy + dw
                    block = row_all.at[pl.ds(mine_d, count_d)]
                    rows_back.append(
                        begin(
                            remote(
                                block, block, all_send.at[index], all_recv.at[index],
                                (lax.rem(gx + da, n_gx), lax.rem(gy + dw, n_gy), gz),
                            )
                        )
                    )
    for dw in range(n_gy):
        for dq in range(1, n_x):
            wide[dq, dw].wait_recv()
            start = (
                core * half
                + lax.rem(mid + n_x - dq, n_x) * piece
                + lax.rem(gy + n_gy - dw, n_gy) * own
            )
            to_core(start, dq, dw)
            arrived(start)
    for dw in range(n_gy):
        for dq in range(n_x):
            last[dq, dw].wait_recv()
            arrived(
                (1 - core) * half
                + lax.rem(mid + n_x - dq, n_x) * piece
                + lax.rem(gy + n_gy - dw, n_gy) * own
            )
    if early:
        for copy in rows_back:
            copy.wait_recv()
        last_step = last_ref[...]
        for index in range(chunks // t_blocks):
            far_out[:, index * 128 : (index + 1) * 128] += last_step * row_all[index]
    else:
        transform(0, chunks)

    for copy in sends + tile_copies + (new_copies if early else []):
        copy.wait_send()

    @pl.when(gx > 0)
    def _():
        up_i.wait_send()

    @pl.when(gy > 0)
    def _():
        up_j.wait_send()

    @pl.when(gz > 0)
    def _():
        up_k.wait_send()

    @pl.when(gx < n_gx - 1)
    def _():
        down_i.wait_send()

    @pl.when(gy < n_gy - 1)
    def _():
        down_j.wait_send()

    @pl.when(gz < n_gz - 1)
    def _():
        down_k.wait_send()


def hand_out(*refs):
    sources, targets, sems = refs[:4], refs[4:8], refs[8]
    pairs = zip(sources, targets)
    copies = [
        pltpu.make_async_copy(source, target, sems.at[index])
        for index, (source, target) in enumerate(pairs)
    ]
    for copy in copies:
        copy.start()
    for copy in copies:
        copy.wait()


def per_device(
    e_field, h_field, permittivity, wall_mask, poles, pole_decay, pole_gain,
    face_cells, owners, history, steering,
):
    n_gx, n_gy, n_gz = (lax.axis_size(axis) for axis in ("gx", "gy", "gz"))
    n_x = n_gx // 2
    count = face_cells.shape[0]
    steps = history.shape[0] + 1
    cap = steering.shape[1] // (n_gx * n_gz)
    rows = -(-cap // 16) * 16
    dirs = steering.shape[2]
    blocks = n_gx * n_gy
    mine = FREQS // blocks
    _, span_x, span_y, span_z = e_field.shape
    flat = span_x * span_y

    table = spectral_rows(FREQS, FREQS, steps)
    table = table.reshape(2, blocks, mine, steps).transpose(1, 0, 2, 3).reshape(blocks, 2 * mine, steps)
    high = table.astype(jnp.bfloat16)
    low = (table - high.astype(np.float32)).astype(jnp.bfloat16)
    split = np.concatenate([high, high, low], axis=2)
    last = np.broadcast_to(table[:, :, -1:], table.shape[:2] + (128,)).copy()
    hist = jnp.transpose(history, (1, 2, 0))

    chunks = steps // 8 * (dirs // 128)
    half = chunks // 2
    piece = half // n_x
    own = piece // n_gy
    f32, bf16 = jnp.float32, jnp.bfloat16
    dma = lambda *dims: pltpu.SemaphoreType.DMA(dims)
    vmem = pl.BlockSpec(memory_space=pltpu.VMEM)
    hbm = pl.BlockSpec(memory_space=pltpu.HBM)
    wide = max(n_x - 1, 1)
    e_next, h_next, far, poles_next = pl.pallas_call(
        functools.partial(kernel, n_gx, n_gy, n_gz, cap, rows),
        out_shape=(
            jax.ShapeDtypeStruct(e_field.shape, f32),
            jax.ShapeDtypeStruct(h_field.shape, f32),
            jax.ShapeDtypeStruct((2 * mine, dirs), f32),
            jax.ShapeDtypeStruct(poles.shape, f32),
        ),
        in_specs=[hbm] * 13,
        out_specs=(vmem, vmem, vmem, vmem),
        scratch_shapes=[
            pltpu.SMEM(pole_decay.shape, f32),
            pltpu.SMEM(pole_gain.shape, f32),
            pltpu.VMEM(e_field.shape, f32),
            pltpu.VMEM(h_field.shape, f32),
            pltpu.VMEM(permittivity.shape, f32),
            pltpu.VMEM(wall_mask.shape, jnp.int32),
            pltpu.VMEM((1, count), jnp.int32),
            pltpu.VMEM((1, count), jnp.int32),
            pltpu.VMEM(hist.shape, bf16),
            pltpu.VMEM(split.shape[1:], bf16),
            pltpu.VMEM(last.shape[1:], f32),
            pltpu.VMEM(poles.shape, f32),
            pltpu.VMEM(steering.shape, bf16),
            pltpu.VMEM((2, span_x, span_z), f32),
            pltpu.VMEM((8, flat), f32),
            pltpu.VMEM((2, span_y, span_z), f32),
            pltpu.VMEM((2, span_x, span_z), f32),
            pltpu.VMEM((8, flat), f32),
            pltpu.VMEM((2, span_x, span_z), f32),
            pltpu.VMEM((8, flat), f32),
            pltpu.VMEM((2, span_y, span_z), f32),
            pltpu.VMEM((2, span_x, span_z), f32),
            pltpu.VMEM((8, flat), f32),
            pltpu.VMEM((n_gx, rows, 4 * steps), bf16),
            pltpu.VMEM((n_gx * n_gz, rows, 4 * steps), bf16),
            pltpu.VMEM((chunks, 8, 128), f32),
            pltpu.VMEM((half, 8, 128), f32),
            pltpu.VMEM((wide, piece, 8, 128), f32),
            pltpu.VMEM((n_gy - 1, own, 8, 128), f32),
            pltpu.VMEM((chunks, 8, 128), f32),
            pltpu.VMEM((n_gx, rows, 128), bf16),
            pltpu.VMEM((n_gx * n_gz, rows, 128), bf16),
            pltpu.VMEM((dirs // 128, 1, 128), f32),
            pltpu.VMEM((n_gx * n_gy, max(own // (steps // 8), 1), 1, 128), f32),
            pltpu.VMEM((dirs // 128, 1, 128), f32),
            dma(13), dma(6), dma(6), dma(n_gx * n_gz), dma(n_gx * n_gz),
            dma(n_x), dma(n_x), dma(wide, n_gy), dma(wide, n_gy), dma(n_gy - 1), dma(n_gy - 1),
            dma(n_gx * n_gz), dma(n_gx * n_gz), dma(n_gx * n_gy), dma(n_gx * n_gy),
            dma(n_gx * n_gy), dma(n_gx * n_gy), dma(n_gy - 1), dma(n_gy - 1), dma(wide, n_gy), dma(wide, n_gy), dma(n_x, n_gy), dma(n_x, n_gy),
        ],
        compiler_params=pltpu.CompilerParams(
            collective_id=0, has_side_effects=True, vmem_limit_bytes=32 * 1024 * 1024
        ),
    )(
        *(
            pltpu.with_memory_space_constraint(operand, pltpu.HBM)
            for operand in (
                pole_decay, pole_gain, e_field, h_field, permittivity, wall_mask, face_cells.reshape(1, count),
                owners.reshape(1, count), hist, jnp.asarray(split), jnp.asarray(last), poles, steering,
            )
        )
    )
    results = (e_next, h_next, poles_next, far)
    e_next, h_next, poles_next, far = pl.pallas_call(
        hand_out,
        out_shape=tuple(jax.ShapeDtypeStruct(result.shape, f32) for result in results),
        in_specs=[vmem] * 4,
        out_specs=(hbm,) * 4,
        scratch_shapes=[dma(4)],
        compiler_params=pltpu.CompilerParams(vmem_limit_bytes=8 * 1024 * 1024),
    )(*results)
    return (e_next, h_next, poles_next, far.reshape(2, mine, dirs))


def solution(mesh):
    return jax.shard_map(
        per_device,
        mesh=mesh,
        in_specs=(
            P(None, "gx", "gy", "gz"),
            P(None, "gx", "gy", "gz"),
            P("gx", "gy", "gz"),
            P("gx", "gy", "gz"),
            P(None, None, "gx", "gy", "gz"),
            P(),
            P(),
            P(("gx", "gy", "gz")),
            P(("gx", "gy", "gz"), None),
            P(None, None, ("gx", "gy", "gz")),
            P(None, ("gx", "gy"), "gz"),
        ),
        out_specs=(
            P(None, "gx", "gy", "gz"),
            P(None, "gx", "gy", "gz"),
            P(None, None, "gx", "gy", "gz"),
            P(None, ("gx", "gy"), "gz"),
        ),
        check_vma=False,
    )
```
